32 devices in a mesh: section: 2 (over x), dp: 16 (over z, y, core).
Axes of the slice: x: 2, y: 2, z: 4, core: 2. Of those that a mesh axis runs over, the one named last changes fastest.
Arguments:
- tokens: bfloat16 [32, 128, 768], P('dp'), may hold values from -6 to 6
- cotangent: bfloat16 [32, 128, 768], P('dp'), may hold values from -6 to 6
- page_lengths: int32 [32], P('dp'), may hold values from 1 to 128, 3072 in all
- cut_order: int32 [32, 128], P('dp'), may hold values from 0 to 127, each once within a row
- cut_region: int32 [32, 128], P('dp'), may hold values from 0 to 15, never falling along the last dimension, each value on 1 to 12 neighbouring positions
- cell_column: int32 [32, 128], P('dp'), may hold values from 0 to 63
- cell_row: int32 [32, 128], P('dp'), may hold values from 0 to 63
- input_proj: bfloat16 [2, 768, 2304], P('section'), may hold values from -0.21875 to 0.21875
- output_proj: bfloat16 [2, 768, 768], P('section'), may hold values from -0.875 to 0.875
- up_proj: bfloat16 [2, 768, 3072], P('section'), may hold values from -0.21875 to 0.21875
- down_proj: bfloat16 [2, 3072, 768], P('section'), may hold values from -0.109375 to 0.109375
- up_bias: bfloat16 [2, 3072], P('section'), may hold values from -4 to 4
- bias_rows: bfloat16 [2, 7, 768], P('section'), may hold values from -4 to 4
- gain_rows: bfloat16 [2, 2, 768], P('section'), may hold values from 0.25 to 1.75
- conv_taps: bfloat16 [2, 7, 768], P('section'), may hold values from -4 to 4
- bias_table: bfloat16 [2, 1920], P('section'), may hold values from -6 to 6
Outputs:
- layer_outputs: bfloat16 [2, 32, 128, 768], P('section', 'dp')
- input_grads: float32 [2, 32, 128, 768], P('section', 'dp')
- input_proj_grad: float32 [2, 768, 2304], P('section', 'dp')
- output_proj_grad: float32 [2, 768, 768], P('section', 'dp')
- up_proj_grad: float32 [2, 768, 3072], P('section', 'dp')
- down_proj_grad: float32 [2, 3072, 768], P('section', 'dp')
- up_bias_grad: float32 [2, 3072], P('section', 'dp')
- bias_rows_grad: float32 [2, 7, 768], P('section', None, 'dp')
- gain_rows_grad: float32 [2, 2, 768], P('section', None, 'dp')
- conv_taps_grad: float32 [2, 7, 768], P('section', None, 'dp')
- bias_table_grad: float32 [2, 1920], P('section', 'dp')
The draws below stay inside these ranges and needn't reach their ends.
Inputs may be any that keep to these rules, and one draw needn't show every extreme that they name: `cut_order`: each row holds every slot 0 to 127 exactly once. `cut_region`: never falls along a row; a region spans at most 12 places. `page_lengths`: slots 0 to length - 1 of a page are live.
All inputs are finite; a program needn't handle non-finite values. No bound on the sum of `page_lengths` on one device may be relied on, other than what follows from the above.
Results may differ from the reference program's by a relative error of at most 0.025.
Values may be sent and summed in bfloat16 or wider, within the bound.
No kernel may reach another device: no remote copies, remote signals or barrier semaphores. Data moves between devices by JAX's collectives and lax.ppermute only.
A program may use at most 256 MiB of HBM per device.

```python
import math
import jax
import jax.numpy as jnp
import numpy as np
from jax import lax

D = 768
HEADS = 12
HEAD = 64
FF = 3072
B1D = 32
B2D = 64
TAPS = 7
REGION_MOST = 12
SLOT = 128
LAYERS = 2
PAGES = 32
BUCKETS = 160


def with_ends(values, own_key, low, high):
    extent = values.shape
    spot = [jax.random.randint(jax.random.fold_in(own_key, axis), (), 0, extent[axis]) for axis in range(len(extent))]
    values = values.at[tuple(spot)].set(low)
    longest = extent.index(max(extent))
    spot[longest] = (spot[longest] + 1) % extent[longest]
    return values.at[tuple(spot)].set(high)


def raised(entries, stream_key, source, target, blocks, factor):
    def block_of(axis_at):
        return (jnp.arange(entries.shape[axis_at]) // (entries.shape[axis_at] // blocks)).reshape((-1,) + (1,) * (entries.ndim - 1 - axis_at))

    one_side = jax.random.permutation(stream_key, blocks)[block_of(target)]
    other_side = (block_of(target) + blocks // 2) % blocks
    return jnp.where((block_of(source) == one_side) | (block_of(source) == other_side), factor * entries, entries)


def steps_of(own_key, extent, pieces, smallest, largest):
    gain, own = 1.0, jax.random.fold_in(own_key, 6)
    for axis_at, blocks in pieces:
        heights = jnp.exp(jax.random.uniform(jax.random.fold_in(own, axis_at), (blocks,), jnp.float32, smallest / len(pieces), largest / len(pieces)))
        gain = gain * jnp.repeat(heights, extent[axis_at] // blocks).reshape([-1 if axis == axis_at else 1 for axis in range(len(extent))])
    return gain


def split_up(number_of, total, reach, skew):
    weights = [(1 << 20) // math.isqrt(standing ** skew) + 1 for standing in range(2, number_of + 1)]
    surplus, counts = total - reach - (number_of - 1), [1] * (number_of - 1)
    while surplus > 0:
        free = [i for i in range(number_of - 1) if counts[i] < reach]
        pool, left = sum([weights[i] for i in free]), surplus
        for i in free:
            addition = min(reach - counts[i], max(1, left * weights[i] // pool), surplus)
            counts[i] = counts[i] + addition
            surplus = surplus - addition
    return np.array([reach] + counts)


def uneven_parts(key, amount, total, limit, slope):
    if amount == 2:
        one = jax.random.randint(key, (), max(1, total - limit), min(limit, total - 1) + 1)
        return jnp.stack([one, total - one])
    lengths = jnp.asarray(split_up(amount, total, limit, slope), jnp.int32)
    twos = (amount - 1) // 2
    source_of, sink = lengths[1:1 + 2 * twos:2], lengths[2:2 + 2 * twos:2]
    room = jnp.minimum(source_of - 1, limit - sink)
    moved = jax.random.randint(jax.random.fold_in(key, 1), (twos,), 0, 1 << 20) % (room + 1)
    lengths = lengths.at[1:1 + 2 * twos:2].set(source_of - moved).at[2:2 + 2 * twos:2].set(sink + moved)
    return lengths[jax.random.permutation(jax.random.fold_in(key, 2), amount)]


def noise(own_key, extent, deviation, limit, split=(), held_as=jnp.bfloat16):
    entries = jax.random.normal(own_key, extent, jnp.float32) * deviation
    if len(split) > 0:
        entries = steps_of(own_key, extent, split, -0.22, 0.18) * entries
    return jnp.clip(entries, min=-limit, max=limit).astype(held_as)


def bell_draw_with(key, shape, deviation, most, pieces, heavy, kind=jnp.bfloat16):
    entries = deviation * jax.random.normal(key, shape, jnp.float32)
    if pieces:
        entries = entries * steps_of(key, shape, pieces, -0.22, 0.18)
    return jnp.clip(raised(entries, jax.random.fold_in(key, 3), *heavy), -most, most).astype(kind)


def setup_inputs(seed: int = 0) -> dict:
    arg_keys = jax.random.split(jax.random.key(seed), 17)
    tokens = bell_draw_with(arg_keys[0], (PAGES, SLOT, D), 1.0, 6.0, ((0, 16),), (0, 2, 16, 2.0))
    cotangent = noise(arg_keys[1], (PAGES, SLOT, D), 1.0, 6.0, ((0, 16),))
    page_lengths = uneven_parts(arg_keys[2], PAGES, PAGES * SLOT * 3 // 4, SLOT, 1).astype(jnp.int32)
    cut_order = jax.vmap(lambda own: jax.random.permutation(own, SLOT))(jax.random.split(arg_keys[3], PAGES)).reshape((PAGES, SLOT)).astype(jnp.int32)
    cut_region = jax.vmap(lambda own: jnp.searchsorted(jnp.cumsum(uneven_parts(own, SLOT // 8, SLOT, REGION_MOST, 1)), jnp.arange(SLOT), side="right"))(jax.random.split(arg_keys[4], PAGES)).reshape((PAGES, SLOT)).astype(jnp.int32)
    cell_column = with_ends(jax.random.randint(arg_keys[5], (PAGES, SLOT), 0, B2D), jax.random.fold_in(arg_keys[5], 1), 0, B2D - 1).astype(jnp.int32)
    cell_row = with_ends(jax.random.randint(arg_keys[6], (PAGES, SLOT), 0, B2D), jax.random.fold_in(arg_keys[6], 1), 0, B2D - 1).astype(jnp.int32)
    input_proj = noise(arg_keys[7], (LAYERS, D, 3 * D), D ** -0.5, 0.21875, ((0, 2),))
    output_proj = noise(arg_keys[8], (LAYERS, D, D), (D // 16) ** -0.5, 0.875, ((0, 2),))
    up_proj = noise(arg_keys[9], (LAYERS, D, FF), D ** -0.5, 0.21875, ((0, 2),))
    down_proj = noise(arg_keys[10], (LAYERS, FF, D), FF ** -0.5, 0.109375, ((0, 2),))
    up_bias = noise(arg_keys[11], (LAYERS, FF), 0.3, 4.0, ((0, 2),))
    bias_rows = noise(arg_keys[12], (LAYERS, 7, D), 0.3, 4.0, ((0, 2),))
    gain_rows = jnp.clip(1.0 + 0.15 * jax.random.normal(arg_keys[13], (LAYERS, 2, D), jnp.float32), 0.25, 1.75).astype(jnp.bfloat16)
    conv_taps = noise(arg_keys[14], (LAYERS, TAPS, D), 0.25, 4.0, ((0, 2),))
    bias_table = noise(arg_keys[15], (LAYERS, BUCKETS * HEADS), 1.0, 6.0, ((0, 2),))
    return {"tokens": tokens, "cotangent": cotangent, "page_lengths": page_lengths, "cut_order": cut_order, "cut_region": cut_region, "cell_column": cell_column, "cell_row": cell_row, "input_proj": input_proj, "output_proj": output_proj, "up_proj": up_proj, "down_proj": down_proj, "up_bias": up_bias, "bias_rows": bias_rows, "gain_rows": gain_rows, "conv_taps": conv_taps, "bias_table": bias_table}


@jax.custom_vjp
def low(v):
    return lax.optimization_barrier(v.astype(jnp.bfloat16)).astype(jnp.float32)

@jax.custom_vjp
def low_back(v):
    return v

def low_keep(v):
    return (low(v), None)

def low_pass(kept, grad):
    return (grad,)

def back_keep(v):
    return (v, None)

def back_low(kept, grad):
    return (low(grad),)
low.defvjp(low_keep, low_pass)
low_back.defvjp(back_keep, back_low)
highest_precision = lax.Precision.HIGHEST
norm_epsilon = 1e-05
masked_score = -1000000000.0
tap_reach = 3

def low_both(value_in):
    return low_back(low(value_in))

def shifted(values_in, offset):
    length_all = values_in.shape[0]
    padding = [(tap_reach, tap_reach)] + [(0, 0)] * (values_in.ndim - 1)
    padded = jnp.pad(values_in, padding)
    return padded[tap_reach + offset:tap_reach + offset + length_all]

def page_geometry(cut_order, cut_region, cell_column, cell_row, page_length):
    tokens_here = cut_order.shape[0]
    places = jnp.arange(tokens_here, dtype=jnp.int32)
    ranking = jnp.zeros((tokens_here,), jnp.int32).at[cut_order].set(places)
    live_order = cut_order < page_length
    ones_int = jnp.ones((tokens_here,), jnp.int32)
    tap_masks = []
    for offset in range(-tap_reach, tap_reach + 1):
        joined = (shifted(ones_int, offset) > 0) & (shifted(cut_region, offset) == cut_region) & shifted(live_order, offset)
        tap_masks.append(joined.astype(jnp.float32))
    key_live = places < page_length
    return (cut_order, ranking, jnp.stack(tap_masks), key_live, cell_column, cell_row)

def conv_apply(hidden, taps, geometry):
    cut_order, ranking, tap_masks = (geometry[0], geometry[1], geometry[2])
    ordered = jnp.take(hidden, cut_order, axis=0)
    mixed_sum = jnp.zeros_like(ordered)
    for column in range(2 * tap_reach + 1):
        mixed_sum = mixed_sum + taps[column] * shifted(ordered, column - tap_reach) * tap_masks[column][:, None]
    return jnp.take(mixed_sum, ranking, axis=0)

def relative_bias(bias_table, geometry):
    ranking, cell_column, cell_row = (geometry[1], geometry[4], geometry[5])
    lookup = bias_table.reshape(B1D + 2 * B2D, HEADS)
    near_bucket = jnp.clip(ranking[None, :] - ranking[:, None] + B1D // 2, 0, B1D - 1)
    result = jnp.einsum('qkb,bh->hqk', jax.nn.one_hot(near_bucket, B1D, dtype=jnp.float32), lookup[:B1D], precision=highest_precision)
    for cell_pos, first_row in ((cell_column, B1D), (cell_row, B1D + B2D)):
        apart_bucket = jnp.clip(cell_pos[None, :] - cell_pos[:, None] + B2D // 2, 0, B2D - 1)
        result = result + jnp.einsum('qkb,bh->hqk', jax.nn.one_hot(apart_bucket, B2D, dtype=jnp.float32), lookup[first_row:first_row + B2D], precision=highest_precision)
    return result

def normalize(hidden):
    average = lax.optimization_barrier(jnp.mean(hidden, axis=-1, keepdims=True))
    centered = hidden - average
    spread = lax.optimization_barrier(jnp.mean(centered * centered, axis=-1, keepdims=True))
    return centered * lax.rsqrt(spread + norm_epsilon)

def layer(hidden, weights, geometry, with_conv):
    input_proj, output_proj, up_proj, down_proj, up_bias, bias_rows, gain_rows, conv_taps, bias_table = weights
    model_width = hidden.shape[1]
    key_live = geometry[3]
    if with_conv:
        mixed = hidden + conv_apply(hidden, conv_taps, geometry) + bias_rows[6]
    else:
        mixed = hidden
    projected = jnp.dot(low(mixed), input_proj, precision=highest_precision, preferred_element_type=jnp.float32)
    queries = low_both(projected[:, :model_width] + bias_rows[0]).reshape(-1, HEADS, HEAD)
    keys_all = low_both(projected[:, model_width:2 * model_width]).reshape(-1, HEADS, HEAD)
    values_all = low_both(projected[:, 2 * model_width:] + bias_rows[1]).reshape(-1, HEADS, HEAD)
    scores = jnp.einsum('qhd,khd->hqk', queries, keys_all, precision=highest_precision) * HEAD ** (-0.5) + relative_bias(bias_table, geometry)
    scores = low_back(scores)
    scores = jnp.where(key_live[None, None, :], scores, masked_score)
    probs = jax.nn.softmax(scores, axis=-1)
    attended = jnp.einsum('hqk,khd->qhd', low(probs), values_all, precision=highest_precision).reshape(-1, model_width)
    attended = low_both(attended)
    branch = low_back(jnp.dot(attended, output_proj, precision=highest_precision, preferred_element_type=jnp.float32) + bias_rows[2])
    first = normalize(mixed + branch) * gain_rows[0] + bias_rows[3]
    gate_in = low_back(jnp.dot(low(first), up_proj, precision=highest_precision, preferred_element_type=jnp.float32) + up_bias)
    activated = low(jax.nn.gelu(gate_in, approximate=False))
    second = low_back(jnp.dot(activated, down_proj, precision=highest_precision, preferred_element_type=jnp.float32) + bias_rows[4])
    return normalize(first + second) * gain_rows[1] + bias_rows[5]

def reference(tokens, cotangent, page_lengths, cut_order, cut_region, cell_column, cell_row, input_proj, output_proj, up_proj, down_proj, up_bias, bias_rows, gain_rows, conv_taps, bias_table):
    params = tuple((stacked.astype(jnp.float32) for stacked in (input_proj, output_proj, up_proj, down_proj, up_bias, bias_rows, gain_rows, conv_taps, bias_table)))
    tokens_float = tokens.astype(jnp.float32)
    page_count = tokens.shape[0]
    layer_count = input_proj.shape[0]
    zeros_in = jnp.zeros((page_count, layer_count) + tokens.shape[1:], jnp.float32)

    def forward(tokens_float, zeros_in, params):

        def one_page(carried):
            page_tokens, page_zeros, length_one, order_one, region_one, column_one, row_one = carried
            geometry = page_geometry(order_one, region_one, column_one, row_one, length_one)
            hidden = page_tokens + page_zeros[0]
            results = []
            sent = hidden
            for level in range(layer_count):
                weights = tuple((stacked[level] for stacked in params))
                if level > 0:
                    hidden = low_back(sent) + page_zeros[level]
                sent = low(layer(hidden, weights, geometry, level == 0))
                results.append(sent)
            return jnp.stack(results)
        return lax.map(jax.checkpoint(one_page), (tokens_float, zeros_in, page_lengths, cut_order, cut_region, cell_column, cell_row))
    outputs, pullback = jax.vjp(forward, tokens_float, zeros_in, params)
    cot_all = jnp.zeros(outputs.shape, jnp.float32).at[:, layer_count - 1].set(cotangent.astype(jnp.float32))
    grad_tokens, grad_zeros, grad_params = pullback(cot_all)
    layer_outputs = jnp.transpose(outputs, (1, 0, 2, 3)).astype(jnp.bfloat16)
    input_grads = jnp.transpose(grad_zeros, (1, 0, 2, 3))
    return (layer_outputs, input_grads, grad_params[0], grad_params[1], grad_params[2], grad_params[3], grad_params[4], grad_params[5], grad_params[6], grad_params[7], grad_params[8])
```

```python
import functools

import jax
import jax.numpy as jnp
from jax import lax
from jax.experimental import pallas as pl
from jax.experimental.pallas import tpu as pltpu
from jax.sharding import PartitionSpec as P

HEADS = 12
HEAD = 64
B1D = 32
B2D = 64
SLOT = 128
PAIRS = HEADS // 2
TAPS = 7
REACH = 3
EPSILON = 1e-05
MASKED = -1000000000.0
STRIP = 64

f32 = jnp.float32
bf16 = jnp.bfloat16
NN = ((1,), (0,))
NT = ((1,), (1,))
TN = ((0,), (0,))

IN_VMEM = pl.BlockSpec(memory_space=pltpu.VMEM)
IN_SMEM = pl.BlockSpec(memory_space=pltpu.SMEM)
IN_PLACE = pl.BlockSpec(memory_space=pl.ANY)


def dot(left, right, dims=NN, precision=None):
    return lax.dot_general(
        left, right, (dims, ((), ())), precision=precision, preferred_element_type=f32
    )


def iota(shape, axis):
    return lax.broadcasted_iota(jnp.int32, shape, axis)


def hot(mask):
    return mask.astype(f32).astype(bf16)


def identity():
    return hot(iota((SLOT, SLOT), 0) == iota((SLOT, SLOT), 1))


def rank_hot_of(order):
    return hot(order == iota((SLOT, SLOT), 0))


def page_hot(order, column, row):
    cells = iota((SLOT, SLOT), 0)
    wanted = jnp.where(cells < B2D, column, row + B2D)
    cell_hot = dot(identity(), hot(wanted == cells), NT).astype(bf16)
    return jnp.concatenate([rank_hot_of(order), cell_hot], axis=1)


def tap_columns(order, region, length):
    shape = (8, SLOT)
    order, region = jnp.broadcast_to(order, shape), jnp.broadcast_to(region, shape)
    live = (order < length).astype(jnp.int32)
    lane, tap = iota(shape, 1), iota(shape, 0)
    masks = jnp.zeros(shape, f32)
    for j in range(TAPS):
        offset = j - REACH
        shift = (-offset) % SLOT
        region_j = pltpu.roll(region, shift, 1) if shift else region
        live_j = pltpu.roll(live, shift, 1) if shift else live
        joined = (lane + offset >= 0) & (lane + offset < SLOT) & (region_j == region) & (live_j > 0)
        masks = jnp.where((tap == j) & joined, 1.0, masks)
    return dot(identity(), masks.astype(bf16), NT)


def shifted(rows, offset):
    shift = (-offset) % SLOT
    return pltpu.roll(rows, shift, 0) if shift else rows


def place_rows(rank_hot, rows, dims):
    high = rows.astype(bf16)
    low = (rows - high.astype(f32)).astype(bf16)
    return dot(rank_hot, high, dims) + dot(rank_hot, low, dims)


def bucket_places():
    shape = (B1D + 2 * B2D, 4 * SLOT)
    bucket, lane = iota(shape, 0), iota(shape, 1)
    near = jnp.clip(lane - (SLOT - 1) + B1D // 2, 0, B1D - 1)
    column = B1D + jnp.clip(lane - 2 * SLOT - (B2D - 1) + B2D // 2, 0, B2D - 1)
    row = B1D + B2D + jnp.clip(lane - 3 * SLOT - (B2D - 1) + B2D // 2, 0, B2D - 1)
    wanted = jnp.where(lane < 2 * SLOT, near, jnp.where(lane < 3 * SLOT, column, row))
    return bucket == wanted


def halves(pair):
    lane = iota((1, SLOT), 1)
    first = hot(lane < HEAD)
    second = hot(lane >= HEAD)
    return jnp.concatenate([pair * first, pair * second], axis=0)


def side_by_side(stacked):
    return jnp.concatenate([stacked[:SLOT], stacked[SLOT:]], axis=1)


def normed_of(value):
    average = jnp.mean(value, axis=-1, keepdims=True)
    centered = value - average
    spread = jnp.mean(centered * centered, axis=-1, keepdims=True)
    inverse = lax.rsqrt(spread + EPSILON)
    return centered * inverse, inverse


def norm_back(grad, normed, inverse):
    first_mean = jnp.mean(grad, axis=-1, keepdims=True)
    second_mean = jnp.mean(grad * normed, axis=-1, keepdims=True)
    return inverse * (grad - first_mean - normed * second_mean)


def copies_in(pairs, sems):
    copies = [pltpu.make_async_copy(a, b, sems.at[i]) for i, (a, b) in enumerate(pairs)]
    for copy in copies:
        copy.start()
    return copies


def bias_body(order_ref, column_ref, row_ref, table_ref, bias_ref):
    pages = order_ref.shape[0]
    hots = [
        page_hot(order_ref[p : p + 1, :], column_ref[p : p + 1, :], row_ref[p : p + 1, :])
        for p in range(pages)
    ]
    every = jnp.concatenate(hots, axis=0)
    reach = dot(table_ref[...], hot(bucket_places()), TN)
    lane = iota((B2D, SLOT), 1)
    for h in range(HEADS):
        row = reach[h : h + 1, :]
        near = jnp.broadcast_to(row[:, : 2 * SLOT], (SLOT, 2 * SLOT))
        near = pltpu.roll(near, SLOT + 1, 1, stride=1, stride_axis=0)[:, :SLOT]
        across = jnp.broadcast_to(row[:, 2 * SLOT : 3 * SLOT], (B2D, SLOT))
        across = pltpu.roll(across, B2D + 1, 1, stride=1, stride_axis=0)
        down = jnp.broadcast_to(row[:, 3 * SLOT :], (B2D, SLOT))
        down = pltpu.roll(down, 1, 1, stride=1, stride_axis=0)
        cells = jnp.concatenate(
            [jnp.where(lane < B2D, across, 0.0), jnp.where(lane >= B2D, down, 0.0)], axis=0
        )
        blank = jnp.zeros((SLOT, SLOT), bf16)
        grid = jnp.concatenate(
            [
                jnp.concatenate([near.astype(bf16), blank], axis=1),
                jnp.concatenate([blank, cells.astype(bf16)], axis=1),
            ],
            axis=0,
        )
        rows = dot(every, grid).astype(bf16)
        for p in range(pages):
            at = (p * HEADS + h) * SLOT
            bias_ref[at : at + SLOT, :] = dot(rows[p * SLOT : (p + 1) * SLOT], hots[p], NT)


def forward_body(weights, waits, lengths_ref, vectors, bias_ref, work, keep, done):
    input_ref, output_ref, up_ref, down_ref = weights
    rows_ref, gains_ref, up_bias_ref = vectors
    mixed_ref, packed_ref, attended_ref, sum_ref, first_ref, low_ref, act_ref, result_ref = work
    rows, gains = rows_ref[...].astype(f32), gains_ref[...].astype(f32)
    tokens, width = mixed_ref.shape
    hidden = act_ref.shape[1]
    low_ref[...] = mixed_ref[...].astype(bf16)
    if keep:
        keep["mixed_low"][...] = low_ref[...]
        done("mixed_low")
    waits[0]()
    for part, add in ((0, rows[0:1]), (1, None), (2, rows[1:2])):
        cols = slice(part * width, (part + 1) * width)
        value = dot(low_ref[...], input_ref[:, cols])
        packed_ref[:, cols] = (value if add is None else value + add).astype(bf16)
    if keep:
        done("packed")
    for p in range(tokens // SLOT):
        live = iota((2 * SLOT, SLOT), 1) < lengths_ref[p]
        here = slice(p * SLOT, (p + 1) * SLOT)
        for pair in range(PAIRS):
            at = pair * SLOT
            queries = halves(packed_ref[here, at : at + SLOT]) * (HEAD**-0.5)
            keys = packed_ref[here, width + at : width + at + SLOT]
            values = packed_ref[here, 2 * width + at : 2 * width + at + SLOT]
            top = (p * HEADS + 2 * pair) * SLOT
            scores = dot(queries, keys, NT) + bias_ref[top : top + 2 * SLOT, :]
            scores = jnp.where(live, scores, MASKED)
            expo = jnp.exp(scores - jnp.max(scores, axis=-1, keepdims=True))
            probs = (expo * (1.0 / jnp.sum(expo, axis=-1, keepdims=True))).astype(bf16)
            if keep:
                keep["probs"][top : top + 2 * SLOT, :] = probs
            attended_ref[here, at : at + SLOT] = dot(side_by_side(probs), halves(values)).astype(
                bf16
            )
    if keep:
        done("probs")
        done("attended")
    waits[1]()
    sum_ref[...] = dot(attended_ref[...], output_ref[...])
    for r in range(0, tokens, STRIP):
        strip = slice(r, r + STRIP)
        normed, inverse = normed_of(mixed_ref[strip] + sum_ref[strip] + rows[2:3])
        first = normed * gains[0:1] + rows[3:4]
        first_ref[strip] = first
        low_ref[strip] = first.astype(bf16)
        if keep:
            keep["first_norm"][strip] = normed
            keep["first_scale"][strip] = jnp.broadcast_to(inverse, (STRIP, SLOT))
            keep["first_low"][strip] = first.astype(bf16)
    if keep:
        done("first_norm")
        done("first_scale")
        done("first_low")
    waits[2]()
    for c in range(0, hidden, 2 * SLOT):
        cols = slice(c, c + 2 * SLOT)
        gate = dot(low_ref[...], up_ref[:, cols]) + up_bias_ref[:, cols].astype(f32)
        below = 0.5 + 0.5 * lax.erf(gate * 0.7071067811865476)
        act_ref[:, cols] = (gate * below).astype(bf16)
        if keep:
            density = jnp.exp(-0.5 * gate * gate) * 0.3989422804014327
            keep["slope"][:, cols] = (below + gate * density).astype(bf16)
    if keep:
        done("slope")
        done("act")
    waits[3]()
    sum_ref[...] = dot(act_ref[...], down_ref[...])
    for r in range(0, tokens, STRIP):
        strip = slice(r, r + STRIP)
        normed, inverse = normed_of(first_ref[strip] + sum_ref[strip] + rows[4:5])
        result_ref[strip] = (normed * gains[1:2] + rows[5:6]).astype(bf16)
        if keep:
            keep["second_norm"][strip] = normed
            keep["second_scale"][strip] = jnp.broadcast_to(inverse, (STRIP, SLOT))
    if keep:
        done("second_norm")
        done("second_scale")


def attention_back(p, pair, packed_ref, probs_ref, grad_ref, grad_packed_ref, width):
    here = slice(p * SLOT, (p + 1) * SLOT)
    at = pair * SLOT
    top = (p * HEADS + 2 * pair) * SLOT
    queries = halves(packed_ref[here, at : at + SLOT]) * (HEAD**-0.5)
    keys = halves(packed_ref[here, width + at : width + at + SLOT]) * (HEAD**-0.5)
    values = packed_ref[here, 2 * width + at : 2 * width + at + SLOT]
    grad = halves(grad_ref[here, at : at + SLOT])
    probs_low = probs_ref[top : top + 2 * SLOT, :]
    probs = probs_low.astype(f32)
    grad_probs = dot(grad, values, NT)
    inner = jnp.sum(probs * grad_probs, axis=-1, keepdims=True)
    grad_scores = (probs * (grad_probs - inner)).astype(bf16)
    for part, value in (
        (0, dot(side_by_side(grad_scores), keys)),
        (1, dot(grad_scores, queries, TN)),
        (2, dot(probs_low, grad, TN)),
    ):
        cols = slice(part * width + at, part * width + at + SLOT)
        grad_packed_ref[here, cols] = value.astype(bf16)
    return grad_scores


def first_kernel(
    tokens_ref,
    lengths_ref,
    flags_ref,
    order_ref,
    region_ref,
    column_ref,
    row_ref,
    rows_ref,
    gains_ref,
    up_bias_ref,
    taps_ref,
    table_ref,
    input_hbm,
    output_hbm,
    up_hbm,
    down_hbm,
    result_ref,
    mixed_ref,
    bias_ref,
    input_ref,
    output_ref,
    up_ref,
    down_ref,
    packed_ref,
    attended_ref,
    sum_ref,
    first_ref,
    low_ref,
    act_ref,
    sems,
):
    copies = copies_in(
        (
            (input_hbm, input_ref),
            (output_hbm, output_ref),
            (up_hbm, up_ref),
            (down_hbm, down_ref),
        ),
        sems,
    )
    conv_on = flags_ref[0].astype(f32)
    taps = taps_ref[...].astype(f32) * conv_on
    conv_bias = rows_ref[...].astype(f32)[6:7] * conv_on
    for p in range(order_ref.shape[0]):
        here = slice(p * SLOT, (p + 1) * SLOT)
        order = order_ref[p : p + 1, :]
        rank_hot = rank_hot_of(order)
        masks = tap_columns(order, region_ref[p : p + 1, :], lengths_ref[p])
        ordered = dot(rank_hot, tokens_ref[here], TN)
        total = jnp.zeros_like(ordered)
        for j in range(TAPS):
            total = total + taps[j : j + 1] * shifted(ordered, j - REACH) * masks[:, j : j + 1]
        mixed_ref[here] = (
            tokens_ref[here].astype(f32) + place_rows(rank_hot, total, NN) + conv_bias
        )
    bias_body(order_ref, column_ref, row_ref, table_ref, bias_ref)
    forward_body(
        (input_ref, output_ref, up_ref, down_ref),
        [copy.wait for copy in copies],
        lengths_ref,
        (rows_ref, gains_ref, up_bias_ref),
        bias_ref,
        (
            mixed_ref,
            packed_ref,
            attended_ref,
            sum_ref,
            first_ref,
            low_ref,
            act_ref,
            result_ref,
        ),
        None,
        None,
    )


KEPT = (
    ("mixed_low", 1, 0),
    ("packed", 3, 0),
    ("probs", 0, 0),
    ("attended", 1, 0),
    ("first_norm", 1, 1),
    ("first_scale", -1, 1),
    ("first_low", 1, 0),
    ("slope", 4, 0),
    ("act", 4, 0),
    ("second_norm", 1, 1),
    ("second_scale", -1, 1),
)


def kept_shapes(tokens, width, hidden):
    shapes = []
    for name, parts, wide in KEPT:
        dims = (tokens, hidden if parts == 4 else SLOT if parts < 0 else parts * width)
        if name == "probs":
            dims = (tokens * HEADS, SLOT)
        shapes.append((dims, f32 if wide else bf16))
    return shapes


def second_kernel(
    arrived_ref,
    cotangent_ref,
    lengths_ref,
    flags_ref,
    rows_ref,
    gains_ref,
    up_bias_ref,
    mixed_hbm,
    bias_hbm,
    input_hbm,
    output_hbm,
    up_hbm,
    down_hbm,
    result_ref,
    grad_in_ref,
    *rest,
):
    count = len(KEPT)
    kept_out, rest = rest[:count], rest[count:]
    kept_list, rest = rest[:count], rest[count:]
    (
        mixed_ref,
        bias_ref,
        input_ref,
        output_ref,
        up_ref,
        down_ref,
        sum_ref,
        first_ref,
        low_ref,
        gate_ref,
        grad_ref,
        grad_packed_ref,
        sems,
        kept_sems,
    ) = rest
    tokens, width = mixed_ref.shape
    hidden = gate_ref.shape[1]
    copies = copies_in(
        (
            (mixed_hbm, mixed_ref),
            (input_hbm, input_ref),
            (bias_hbm, bias_ref),
            (output_hbm, output_ref),
            (up_hbm, up_ref),
            (down_hbm, down_ref),
        ),
        sems,
    )
    names = [name for name, _, _ in KEPT]
    keep = dict(zip(names, kept_list))
    leaving = []

    def done(name):
        at = names.index(name)
        copy = pltpu.make_async_copy(kept_list[at], kept_out[at], kept_sems.at[at])
        copy.start()
        leaving.append(copy)

    copies[0].wait()
    first_section = flags_ref[0] > 0
    mixed_ref[...] = jnp.where(first_section, mixed_ref[...], arrived_ref[...].astype(f32))

    def wait_input():
        copies[1].wait()
        copies[2].wait()

    forward_body(
        (input_ref, output_ref, up_ref, down_ref),
        (wait_input, copies[3].wait, copies[4].wait, copies[5].wait),
        lengths_ref,
        (rows_ref, gains_ref, up_bias_ref),
        bias_ref,
        (
            mixed_ref,
            keep["packed"],
            keep["attended"],
            sum_ref,
            first_ref,
            low_ref,
            keep["act"],
            result_ref,
        ),
        keep,
        done,
    )
    gains = gains_ref[...].astype(f32)
    for r in range(0, tokens, STRIP):
        strip = slice(r, r + STRIP)
        grad = cotangent_ref[strip].astype(f32) * gains[1:2]
        grad_sum = norm_back(grad, keep["second_norm"][strip], keep["second_scale"][strip, :1])
        first_ref[strip] = grad_sum
        low_ref[strip] = grad_sum.astype(bf16)
    gate_body(low_ref, down_ref, keep["slope"], gate_ref)
    for c in range(0, width, 2 * SLOT):
        cols = slice(c, c + 2 * SLOT)
        sum_ref[:, cols] = first_ref[:, cols] + dot(gate_ref[...], up_ref[cols, :], NT)
    for r in range(0, tokens, STRIP):
        strip = slice(r, r + STRIP)
        grad = sum_ref[strip] * gains[0:1]
        grad_mid = norm_back(grad, keep["first_norm"][strip], keep["first_scale"][strip, :1])
        first_ref[strip] = grad_mid
        low_ref[strip] = grad_mid.astype(bf16)
    grad_ref[...] = dot(low_ref[...], output_ref[...], NT).astype(bf16)
    for p in range(tokens // SLOT):
        for pair in range(PAIRS):
            attention_back(
                p, pair, keep["packed"], keep["probs"], grad_ref, grad_packed_ref, width
            )
    for c in range(0, width, 2 * SLOT):
        cols = slice(c, c + 2 * SLOT)
        grad_in = first_ref[:, cols] + dot(grad_packed_ref[...], input_ref[cols, :], NT)
        grad_in_ref[:, cols] = grad_in.astype(bf16)
    for copy in leaving:
        copy.wait()


def gate_body(grad_ref, down_ref, slope_ref, gate_ref):
    for c in range(0, gate_ref.shape[1], 2 * SLOT):
        cols = slice(c, c + 2 * SLOT)
        value = dot(grad_ref[...], down_ref[cols, :], NT) * slope_ref[:, cols].astype(f32)
        gate_ref[:, cols] = value.astype(bf16)


class Shares:
    def __init__(self, held_ref, outs, core, sems):
        self.held, self.outs, self.core, self.sems = held_ref, outs, core, sems
        self.copies, self.sent = [], 0

    def rows_done(self, rows):
        if len(self.outs) == 1:
            if rows == self.held.shape[0]:
                self._start(self.held, self.outs[0])
            return
        share = self.outs[0].shape[1]
        while (self.sent + 1) * 2 * share <= rows:
            for out, parity in zip(self.outs, (1 - self.core, self.core)):
                start = pl.multiple_of((2 * self.sent + parity) * share, 16)
                self._start(self.held.at[pl.ds(start, share)], out.at[self.sent])
            self.sent += 1

    def _start(self, source, target):
        copy = pltpu.make_async_copy(source, target, self.sems.at[len(self.copies)])
        copy.start()
        self.copies.append(copy)

    def wait(self):
        for copy in self.copies:
            copy.wait()


def column_sum(value):
    return jnp.sum(value, axis=0, keepdims=True)


def down_kernel(
    cotangent_ref,
    arrived_ref,
    flags_ref,
    gains_ref,
    normed_ref,
    scale_ref,
    act_ref,
    *rest,
    outs,
):
    shares_out, (grad_sum_ref, small_ref, low_ref, held_ref, sems) = rest[:outs], rest[outs:]
    tokens = low_ref.shape[0]
    hidden = act_ref.shape[1]
    gains = gains_ref[...].astype(f32)
    last = flags_ref[2] > 0
    sums = [0.0, 0.0, 0.0]
    for r in range(0, tokens, STRIP):
        strip = slice(r, r + STRIP)
        grad_out = jnp.where(
            last, cotangent_ref[strip].astype(f32), arrived_ref[strip].astype(f32)
        )
        normed = normed_ref[strip]
        grad_sum = norm_back(grad_out * gains[1:2], normed, scale_ref[strip, :1])
        low = grad_sum.astype(bf16)
        grad_sum_ref[strip] = grad_sum
        low_ref[strip] = low
        sums[0] = sums[0] + column_sum(low.astype(f32))
        sums[1] = sums[1] + column_sum(grad_out)
        sums[2] = sums[2] + column_sum(grad_out * normed)
    shares = Shares(held_ref, shares_out, flags_ref[1], sems)
    step = 3 * SLOT
    for r in range(0, hidden, step):
        held_ref[r : r + step, :] = dot(act_ref[:, r : r + step], low_ref[...], TN).astype(bf16)
        shares.rows_done(r + step)
    for i, value in enumerate(sums):
        small_ref[i : i + 1, :] = value
    shares.wait()


def up_kernel(grad_sum_ref, flags_ref, slope_ref, first_low_ref, down_hbm, *rest, outs):
    shares_out, (gate_ref, small_ref, low_ref, down_ref, held_ref, sem, sems) = (
        rest[:outs],
        rest[outs:],
    )
    (copy,) = copies_in(((down_hbm, down_ref),), sem)
    low_ref[...] = grad_sum_ref[...].astype(bf16)
    copy.wait()
    gate_body(low_ref, down_ref, slope_ref, gate_ref)
    shares = Shares(held_ref, shares_out, flags_ref[1], sems)
    width, hidden = held_ref.shape
    step = 3 * SLOT
    for r in range(0, width, step):
        left = first_low_ref[:, r : r + step]
        for c in range(0, hidden, width):
            cols = slice(c, c + width)
            held_ref[r : r + step, cols] = dot(left, gate_ref[:, cols], TN).astype(bf16)
        shares.rows_done(r + step)
    for c in range(0, hidden, width):
        cols = slice(c, c + width)
        small_ref[:, cols] = column_sum(gate_ref[:, cols].astype(f32))
    shares.wait()


def backwards(every):
    shape = (2 * SLOT, 2 * SLOT)
    left, right = iota(shape, 0), iota(shape, 1)
    ends = jnp.where(left < SLOT, SLOT - 1, jnp.where(left < SLOT + B2D, 3 * SLOT - B2D - 1, 0))
    ends = jnp.where(left >= SLOT + B2D, 4 * SLOT - B2D - 1, ends)
    return dot(every, hot(left + right == ends)).astype(bf16)


def table_rows(sums):
    blank = jnp.zeros((SLOT, SLOT), f32)
    near = jnp.concatenate([sums[:SLOT, :SLOT], blank], axis=1)
    near = pltpu.roll(near, 0, 1, stride=1, stride_axis=0)
    lane = iota((B2D, SLOT), 1)
    across = jnp.where(lane < B2D, sums[SLOT : SLOT + B2D, SLOT:], 0.0)
    across = pltpu.roll(across, 0, 1, stride=1, stride_axis=0)
    down = jnp.where(lane >= B2D, sums[SLOT + B2D :, SLOT:], 0.0)
    down = pltpu.roll(down, B2D, 1, stride=1, stride_axis=0)
    return jnp.concatenate([column_sum(near), column_sum(across), column_sum(down)], axis=1)


def last_kernel(
    grad_sum_ref,
    gate_ref,
    normed_ref,
    scale_ref,
    attended_ref,
    packed_ref,
    probs_ref,
    mixed_low_ref,
    tokens_ref,
    small_down_ref,
    lengths_ref,
    flags_ref,
    order_ref,
    region_ref,
    column_ref,
    row_ref,
    gains_ref,
    taps_ref,
    up_hbm,
    output_hbm,
    input_hbm,
    *rest,
    outs,
):
    shares_out, rest = rest[:outs], rest[outs:]
    grad_in_ref, small_ref, table_ref, rest = rest[0], rest[1], rest[2], rest[3:]
    (
        up_ref,
        output_ref,
        input_ref,
        sum_ref,
        mid_ref,
        low_ref,
        grad_ref,
        grad_packed_ref,
        reach_ref,
        held_ref,
        weight_sems,
        sems,
    ) = rest
    copies = copies_in(
        ((up_hbm, up_ref), (output_hbm, output_ref), (input_hbm, input_ref)), weight_sems
    )
    tokens, width = sum_ref.shape
    pages = tokens // SLOT
    conv_on = flags_ref[0].astype(f32)
    gains = gains_ref[...].astype(f32)
    taps = taps_ref[...].astype(f32) * conv_on
    copies[0].wait()
    for c in range(0, width, 2 * SLOT):
        cols = slice(c, c + 2 * SLOT)
        sum_ref[:, cols] = grad_sum_ref[:, cols] + dot(gate_ref[...], up_ref[cols, :], NT)
    first_sum = gain_sum = branch_sum = 0.0
    for r in range(0, tokens, STRIP):
        strip = slice(r, r + STRIP)
        grad_first, normed = sum_ref[strip], normed_ref[strip]
        grad_mid = norm_back(grad_first * gains[0:1], normed, scale_ref[strip, :1])
        low = grad_mid.astype(bf16)
        mid_ref[strip] = grad_mid
        low_ref[strip] = low
        first_sum = first_sum + column_sum(grad_first)
        gain_sum = gain_sum + column_sum(grad_first * normed)
        branch_sum = branch_sum + column_sum(low.astype(f32))
    copies[1].wait()
    grad_ref[...] = dot(low_ref[...], output_ref[...], NT).astype(bf16)
    hots = [
        page_hot(order_ref[p : p + 1, :], column_ref[p : p + 1, :], row_ref[p : p + 1, :])
        for p in range(pages)
    ]
    every = backwards(jnp.concatenate(hots, axis=0))
    reach_ref[...] = jnp.zeros_like(reach_ref)
    for pair in range(PAIRS):
        scores = [
            attention_back(p, pair, packed_ref, probs_ref, grad_ref, grad_packed_ref, width)
            for p in range(pages)
        ]
        for head in range(2):
            rows = slice(head * SLOT, (head + 1) * SLOT)
            along = jnp.concatenate([dot(s[rows], h) for s, h in zip(scores, hots)], axis=0)
            sums = dot(every, along.astype(bf16), TN)
            at = 2 * pair + head
            reach_ref[at : at + 1, :] = table_rows(sums)
    shares = Shares(held_ref, shares_out, flags_ref[1], sems)
    step = 3 * SLOT
    for r in range(0, width, step):
        rows = slice(r, r + step)
        held_ref[rows, :width] = dot(attended_ref[:, rows], low_ref[...], TN).astype(bf16)
        for c in range(0, 3 * width, width):
            value = dot(mixed_low_ref[:, rows], grad_packed_ref[:, c : c + width], TN)
            held_ref[rows, width + c : 2 * width + c] = value.astype(bf16)
        shares.rows_done(r + step)
    copies[2].wait()
    for c in range(0, width, 2 * SLOT):
        cols = slice(c, c + 2 * SLOT)
        sum_ref[:, cols] = mid_ref[:, cols] + dot(grad_packed_ref[...], input_ref[cols, :], NT)
    tap_sums = [0.0] * TAPS
    mixed_sum = 0.0
    for p in range(pages):
        here = slice(p * SLOT, (p + 1) * SLOT)
        order = order_ref[p : p + 1, :]
        rank_hot = rank_hot_of(order)
        masks = tap_columns(order, region_ref[p : p + 1, :], lengths_ref[p])
        ordered = dot(rank_hot, tokens_ref[here], TN)
        grad_mixed = sum_ref[here]
        grad_order = place_rows(rank_hot, grad_mixed, TN)
        source = jnp.zeros_like(ordered)
        for j in range(TAPS):
            masked = grad_order * masks[:, j : j + 1]
            tap_sums[j] = tap_sums[j] + column_sum(masked * shifted(ordered, j - REACH))
            source = source + shifted(taps[j : j + 1] * masked, REACH - j)
        grad_in_ref[here] = grad_mixed + place_rows(rank_hot, source, NN)
        mixed_sum = mixed_sum + column_sum(grad_mixed)
    small_down = small_down_ref[...]
    rows = [
        column_sum(grad_packed_ref[:, :width].astype(f32)),
        column_sum(grad_packed_ref[:, 2 * width :].astype(f32)),
        branch_sum,
        first_sum,
        small_down[0:1],
        small_down[1:2],
        conv_on * mixed_sum,
        gain_sum,
        small_down[2:3],
    ]
    for i, value in enumerate(rows + [conv_on * value for value in tap_sums]):
        small_ref[i : i + 1, :] = value
    table_ref[...] = dot(
        bucket_places().astype(f32), reach_ref[...], NT, precision=lax.Precision.HIGHEST
    )
    shares.wait()


def kernel_call(body, name, ins, outs, scratch, flops):
    nbytes = sum(value.size * value.dtype.itemsize for value, _ in list(ins) + list(outs))
    return pl.pallas_call(
        body,
        name=name,
        out_shape=[shape for shape, _ in outs],
        in_specs=[spec for _, spec in ins],
        out_specs=[spec for _, spec in outs],
        scratch_shapes=scratch,
        compiler_params=pltpu.CompilerParams(vmem_limit_bytes=56 << 20),
        cost_estimate=pl.CostEstimate(flops=int(flops), bytes_accessed=nbytes, transcendentals=0),
    )(*[value for value, _ in ins])


def taken(value, index, axis):
    return lax.dynamic_index_in_dim(value, index, axis, keepdims=False).astype(f32)


def summed(theirs, mine):
    index = lax.axis_index("dp")
    z, y = index // 4, (index // 2) % 2
    everyone = range(16)

    def swapped(value, bits):
        return lax.ppermute(value, "dp", [(i, i ^ bits) for i in everyone])

    theirs, mine = (v.reshape((4, 2) + v.shape[1:]) for v in (theirs, mine))
    core_part = swapped(theirs, 1)
    leaving = (taken(mine, 1 - y, 1) + taken(core_part, 1 - y, 1)).astype(bf16)
    y_part = swapped(leaving, 2)
    kept = taken(mine, y, 1) + taken(core_part, y, 1) + y_part.astype(f32)
    kept = kept.astype(bf16)
    total = taken(kept, z, 0)
    for step in (1, 2, 3):
        part = lax.dynamic_index_in_dim(kept, z ^ step, 0, keepdims=False)
        total = total + swapped(part, 4 * step).astype(f32)
    return total


def local(
    tokens,
    cotangent,
    page_lengths,
    cut_order,
    cut_region,
    cell_column,
    cell_row,
    input_proj,
    output_proj,
    up_proj,
    down_proj,
    up_bias,
    bias_rows,
    gain_rows,
    conv_taps,
    bias_table,
):
    section_index = lax.axis_index("section")
    section_count = lax.axis_size("section")
    dp_index = lax.axis_index("dp")
    dp_count = lax.axis_size("dp")
    by_hops = dp_count == 16
    pages, _, width = tokens.shape
    hidden = up_proj.shape[2]
    count = pages * SLOT
    weights = [w[0] for w in (input_proj, output_proj, up_proj, down_proj)]
    input_w, output_w, up_w, down_w = weights
    rows, gains, taps = bias_rows[0], gain_rows[0], conv_taps[0]
    table = jnp.pad(bias_table[0].reshape(-1, HEADS), ((0, 0), (0, 16 - HEADS)))
    flags = jnp.stack(
        [
            (section_index == 0).astype(jnp.int32),
            (dp_index % 2).astype(jnp.int32),
            (section_index == section_count - 1).astype(jnp.int32),
        ]
    )
    tokens, cotangent = tokens.reshape(count, width), cotangent.reshape(count, width)
    work = 2 * count * (4 * width * width + 2 * width * hidden)

    def shape(dims, kind):
        return jax.ShapeDtypeStruct(dims, kind)

    def inside(*values):
        return [(v, IN_VMEM) for v in values]

    def in_place(*values):
        return [(v, IN_PLACE) for v in values]

    def scalars(*values):
        return [(v, IN_SMEM) for v in values]

    wide, low = shape((count, width), f32), shape((count, width), bf16)
    weight_scratch = [pltpu.VMEM(w.shape, w.dtype) for w in weights]
    wide_scratch = pltpu.VMEM((count, width), f32)
    low_scratch = pltpu.VMEM((count, width), bf16)
    packed_scratch = pltpu.VMEM((count, 3 * width), bf16)
    hidden_scratch = pltpu.VMEM((count, hidden), bf16)
    bias_dims = (pages * HEADS * SLOT, SLOT)

    def sems(number):
        return pltpu.SemaphoreType.DMA((number,))

    result, mixed, bias = kernel_call(
        first_kernel,
        "first",
        inside(tokens)
        + scalars(page_lengths, flags)
        + inside(cut_order, cut_region, cell_column, cell_row, rows, gains, up_bias, taps, table)
        + in_place(*weights),
        inside(low, wide, shape(bias_dims, f32)),
        weight_scratch
        + [
            packed_scratch,
            low_scratch,
            wide_scratch,
            wide_scratch,
            low_scratch,
            hidden_scratch,
            sems(4),
        ],
        work,
    )
    arrived = lax.ppermute(result, "section", [(i, i + 1) for i in range(section_count - 1)])
    shapes = kept_shapes(count, width, hidden)
    layer_out, leaving, *kept_list = kernel_call(
        second_kernel,
        "second",
        inside(arrived, cotangent)
        + scalars(page_lengths, flags)
        + inside(rows, gains, up_bias)
        + in_place(mixed, bias, *weights),
        inside(low, low) + in_place(*[shape(*s) for s in shapes]),
        [pltpu.VMEM(*s) for s in shapes]
        + [wide_scratch, pltpu.VMEM(bias_dims, f32)]
        + weight_scratch
        + [
            wide_scratch,
            wide_scratch,
            low_scratch,
            hidden_scratch,
            low_scratch,
            packed_scratch,
            sems(6),
            sems(len(KEPT)),
        ],
        2 * work,
    )
    kept = dict(zip([name for name, _, _ in KEPT], kept_list))
    arrived_grad = lax.ppermute(
        leaving, "section", [(i + 1, i) for i in range(section_count - 1)]
    )

    def share_outs(dims):
        if not by_hops:
            return in_place(shape(dims, bf16))
        half = shape((dp_count // 2, dims[0] // dp_count, dims[1]), bf16)
        return in_place(half, half)

    def over_devices(parts):
        if by_hops:
            return summed(*parts)
        return lax.psum_scatter(parts[0], "dp", scatter_dimension=0, tiled=True).astype(f32)

    outs = 2 if by_hops else 1
    share_sems = sems(dp_count if by_hops else 1)
    *down_parts, grad_sum, small_down = kernel_call(
        functools.partial(down_kernel, outs=outs),
        "down",
        inside(cotangent, arrived_grad)
        + scalars(flags)
        + inside(gains, kept["second_norm"], kept["second_scale"], kept["act"]),
        share_outs((hidden, width)) + inside(wide, shape((8, width), f32)),
        [low_scratch, pltpu.VMEM((hidden, width), bf16), share_sems],
        2 * count * width * hidden,
    )
    *up_parts, gate, small_up = kernel_call(
        functools.partial(up_kernel, outs=outs),
        "up",
        inside(grad_sum)
        + scalars(flags)
        + inside(kept["slope"], kept["first_low"])
        + in_place(down_w),
        share_outs((width, hidden)) + inside(shape((count, hidden), bf16), shape((1, hidden), f32)),
        [
            low_scratch,
            weight_scratch[3],
            pltpu.VMEM((width, hidden), bf16),
            sems(1),
            share_sems,
        ],
        4 * count * width * hidden,
    )
    *in_parts, grad_in, small_rows, small_table = kernel_call(
        functools.partial(last_kernel, outs=outs),
        "last",
        inside(
            grad_sum,
            gate,
            kept["first_norm"],
            kept["first_scale"],
            kept["attended"],
            kept["packed"],
            kept["probs"],
            kept["mixed_low"],
            tokens,
            small_down,
        )
        + scalars(page_lengths, flags)
        + inside(cut_order, cut_region, cell_column, cell_row, gains, taps)
        + in_place(up_w, output_w, input_w),
        share_outs((width, 4 * width))
        + inside(wide, shape((16, width), f32), shape((B1D + 2 * B2D, 16), f32)),
        [
            weight_scratch[2],
            weight_scratch[1],
            weight_scratch[0],
            wide_scratch,
            wide_scratch,
            low_scratch,
            low_scratch,
            packed_scratch,
            pltpu.VMEM((16, 4 * SLOT), f32),
            pltpu.VMEM((width, 4 * width), bf16),
            sems(3),
            share_sems,
        ],
        3 * work,
    )
    down_grad = over_devices(down_parts)
    up_grad = over_devices(up_parts)
    in_grad = over_devices(in_parts)
    part = width // dp_count
    small = jnp.concatenate(
        [
            small_rows.reshape(16, dp_count, part).transpose(1, 0, 2).reshape(dp_count, -1),
            small_up.reshape(dp_count, -1),
            small_table[:, :HEADS].reshape(dp_count, -1),
        ],
        axis=1,
    )
    used = small.shape[1]
    small = jnp.pad(small, ((0, 0), (0, -used % SLOT))).reshape(-1, SLOT)
    small = lax.psum_scatter(small, "dp", scatter_dimension=0, tiled=True).reshape(-1)
    small_rows = small[: 16 * part].reshape(16, part)
    up_bias_grad = small[16 * part : 16 * part + hidden // dp_count]
    table_grad = small[16 * part + hidden // dp_count : used]
    return tuple(
        value[None]
        for value in (
            layer_out.reshape(pages, SLOT, width),
            grad_in.reshape(pages, SLOT, width),
            in_grad[:, width:],
            in_grad[:, :width],
            up_grad,
            down_grad,
            up_bias_grad,
            small_rows[:7],
            small_rows[7:9],
            small_rows[9:],
            table_grad,
        )
    )


def solution(mesh):
    by_section = [P("section", None, None)] * 4
    placed = (
        P("dp", None, None),
        P("dp", None, None),
        P("dp"),
        P("dp", None),
        P("dp", None),
        P("dp", None),
        P("dp", None),
        *by_section,
        P("section", None),
        P("section", None, None),
        P("section", None, None),
        P("section", None, None),
        P("section", None),
    )
    return jax.shard_map(
        local,
        mesh=mesh,
        in_specs=placed,
        out_specs=(
            P("section", "dp", None, None),
            P("section", "dp", None, None),
            P("section", "dp", None),
            P("section", "dp", None),
            P("section", "dp", None),
            P("section", "dp", None),
            P("section", "dp"),
            P("section", None, "dp"),
            P("section", None, "dp"),
            P("section", None, "dp"),
            P("section", "dp"),
        ),
        check_vma=False,
    )
```

```python
import functools

import jax
import jax.numpy as jnp
from jax import lax
from jax.experimental import pallas as pl
from jax.experimental.pallas import tpu as pltpu
from jax.sharding import PartitionSpec as P

HEADS = 12
HEAD = 64
B1D = 32
B2D = 64
SLOT = 128
PAIRS = HEADS // 2
TAPS = 7
REACH = 3
EPSILON = 1e-05
COST = 100_000_000_000
MASKED = -1000000000.0
STRIP = 64

f32 = jnp.float32
bf16 = jnp.bfloat16
NN = ((1,), (0,))
NT = ((1,), (1,))
TN = ((0,), (0,))

IN_VMEM = pl.BlockSpec(memory_space=pltpu.VMEM)
IN_SMEM = pl.BlockSpec(memory_space=pltpu.SMEM)
IN_PLACE = pl.BlockSpec(memory_space=pl.ANY)


def dot(left, right, dims=NN, precision=None):
    return lax.dot_general(
        left, right, (dims, ((), ())), precision=precision, preferred_element_type=f32
    )


def iota(shape, axis):
    return lax.broadcasted_iota(jnp.int32, shape, axis)


def hot(mask):
    return mask.astype(f32).astype(bf16)


def identity():
    return hot(iota((SLOT, SLOT), 0) == iota((SLOT, SLOT), 1))


def rank_hot_of(order):
    return hot(order == iota((SLOT, SLOT), 0))


def page_hot(order, column, row):
    cells = iota((SLOT, SLOT), 0)
    wanted = jnp.where(cells < B2D, column, row + B2D)
    cell_hot = dot(identity(), hot(wanted == cells), NT).astype(bf16)
    return jnp.concatenate([rank_hot_of(order), cell_hot], axis=1)


def tap_columns(order, region, length):
    shape = (8, SLOT)
    order, region = jnp.broadcast_to(order, shape), jnp.broadcast_to(region, shape)
    live = (order < length).astype(jnp.int32)
    lane, tap = iota(shape, 1), iota(shape, 0)
    masks = jnp.zeros(shape, f32)
    for j in range(TAPS):
        offset = j - REACH
        shift = (-offset) % SLOT
        region_j = pltpu.roll(region, shift, 1) if shift else region
        live_j = pltpu.roll(live, shift, 1) if shift else live
        joined = (lane + offset >= 0) & (lane + offset < SLOT) & (region_j == region) & (live_j > 0)
        masks = jnp.where((tap == j) & joined, 1.0, masks)
    return dot(identity(), masks.astype(bf16), NT)


def shifted(rows, offset):
    shift = (-offset) % SLOT
    return pltpu.roll(rows, shift, 0) if shift else rows


def place_rows(rank_hot, rows, dims):
    high = rows.astype(bf16)
    low = (rows - high.astype(f32)).astype(bf16)
    return dot(rank_hot, high, dims) + dot(rank_hot, low, dims)


def bucket_places():
    shape = (B1D + 2 * B2D, 4 * SLOT)
    bucket, lane = iota(shape, 0), iota(shape, 1)
    near = jnp.clip(lane - (SLOT - 1) + B1D // 2, 0, B1D - 1)
    column = B1D + jnp.clip(lane - 2 * SLOT - (B2D - 1) + B2D // 2, 0, B2D - 1)
    row = B1D + B2D + jnp.clip(lane - 3 * SLOT - (B2D - 1) + B2D // 2, 0, B2D - 1)
    wanted = jnp.where(lane < 2 * SLOT, near, jnp.where(lane < 3 * SLOT, column, row))
    return bucket == wanted


def halves(pair):
    lane = iota((1, SLOT), 1)
    first = hot(lane < HEAD)
    second = hot(lane >= HEAD)
    return jnp.concatenate([pair * first, pair * second], axis=0)


def side_by_side(stacked):
    return jnp.concatenate([stacked[:SLOT], stacked[SLOT:]], axis=1)


def normed_of(value):
    average = jnp.mean(value, axis=-1, keepdims=True)
    centered = value - average
    spread = jnp.mean(centered * centered, axis=-1, keepdims=True)
    inverse = lax.rsqrt(spread + EPSILON)
    return centered * inverse, inverse


def norm_back(grad, normed, inverse):
    first_mean = jnp.mean(grad, axis=-1, keepdims=True)
    second_mean = jnp.mean(grad * normed, axis=-1, keepdims=True)
    return inverse * (grad - first_mean - normed * second_mean)


def copies_in(pairs, sems):
    copies = [pltpu.make_async_copy(a, b, sems.at[i]) for i, (a, b) in enumerate(pairs)]
    for copy in copies:
        copy.start()
    return copies


def table_columns(table):
    buckets = table.shape[1] // HEADS
    bucket = iota((buckets, table.shape[1]), 0) * HEADS
    lane = iota((buckets, table.shape[1]), 1)
    own = hot((lane >= bucket) & (lane < bucket + HEADS))
    lane = iota((16, table.shape[1]), 1)
    times = ((lane.astype(f32) + 0.5) * (1.0 / HEADS)).astype(jnp.int32)
    head = hot(lane - HEADS * times == iota((16, table.shape[1]), 0))
    return dot(own * table, head, NT).astype(bf16)


def bias_body(order_ref, column_ref, row_ref, table_ref, bias_ref):
    pages = order_ref.shape[0]
    hots = [
        page_hot(order_ref[p : p + 1, :], column_ref[p : p + 1, :], row_ref[p : p + 1, :])
        for p in range(pages)
    ]
    every = jnp.concatenate(hots, axis=0)
    reach = dot(table_columns(table_ref[...]), hot(bucket_places()), TN)
    lane = iota((B2D, SLOT), 1)
    for h in range(HEADS):
        row = reach[h : h + 1, :]
        near = jnp.broadcast_to(row[:, : 2 * SLOT], (SLOT, 2 * SLOT))
        near = pltpu.roll(near, SLOT + 1, 1, stride=1, stride_axis=0)[:, :SLOT]
        across = jnp.broadcast_to(row[:, 2 * SLOT : 3 * SLOT], (B2D, SLOT))
        across = pltpu.roll(across, B2D + 1, 1, stride=1, stride_axis=0)
        down = jnp.broadcast_to(row[:, 3 * SLOT :], (B2D, SLOT))
        down = pltpu.roll(down, 1, 1, stride=1, stride_axis=0)
        cells = jnp.concatenate(
            [jnp.where(lane < B2D, across, 0.0), jnp.where(lane >= B2D, down, 0.0)], axis=0
        )
        blank = jnp.zeros((SLOT, SLOT), bf16)
        grid = jnp.concatenate(
            [
                jnp.concatenate([near.astype(bf16), blank], axis=1),
                jnp.concatenate([blank, cells.astype(bf16)], axis=1),
            ],
            axis=0,
        )
        rows = dot(every, grid).astype(bf16)
        for p in range(pages):
            at = (p * HEADS + h) * SLOT
            bias_ref[at : at + SLOT, :] = dot(rows[p * SLOT : (p + 1) * SLOT], hots[p], NT)


def forward_body(weights, waits, lengths_ref, vectors, bias_ref, work, keep, done):
    input_ref, output_ref, up_ref, down_ref = weights
    rows_ref, gains_ref, up_bias_ref = vectors
    mixed_ref, packed_ref, attended_ref, sum_ref, first_ref, low_ref, act_ref, result_ref = work
    rows, gains = rows_ref[...].astype(f32), gains_ref[...].astype(f32)
    tokens, width = mixed_ref.shape
    hidden = act_ref.shape[1]
    low_ref[...] = mixed_ref[...].astype(bf16)
    if keep:
        keep["mixed_low"][...] = low_ref[...]
        done("mixed_low")
    waits[0]()
    for part, add in ((0, rows[0:1]), (1, None), (2, rows[1:2])):
        cols = slice(part * width, (part + 1) * width)
        value = dot(low_ref[...], input_ref[:, cols])
        packed_ref[:, cols] = (value if add is None else value + add).astype(bf16)
    if keep:
        done("packed")
    for p in range(tokens // SLOT):
        live = iota((2 * SLOT, SLOT), 1) < lengths_ref[p]
        here = slice(p * SLOT, (p + 1) * SLOT)
        for pair in range(PAIRS):
            at = pair * SLOT
            queries = halves(packed_ref[here, at : at + SLOT]) * (HEAD**-0.5)
            keys = packed_ref[here, width + at : width + at + SLOT]
            values = packed_ref[here, 2 * width + at : 2 * width + at + SLOT]
            top = (p * HEADS + 2 * pair) * SLOT
            scores = dot(queries, keys, NT) + bias_ref[top : top + 2 * SLOT, :]
            scores = jnp.where(live, scores, MASKED)
            expo = jnp.exp(scores - jnp.max(scores, axis=-1, keepdims=True))
            probs = (expo * (1.0 / jnp.sum(expo, axis=-1, keepdims=True))).astype(bf16)
            if keep:
                keep["probs"][top : top + 2 * SLOT, :] = probs
            attended_ref[here, at : at + SLOT] = dot(side_by_side(probs), halves(values)).astype(
                bf16
            )
    if keep:
        done("probs")
        done("attended")
    waits[1]()
    sum_ref[...] = dot(attended_ref[...], output_ref[...])
    for r in range(0, tokens, STRIP):
        strip = slice(r, r + STRIP)
        normed, inverse = normed_of(mixed_ref[strip] + sum_ref[strip] + rows[2:3])
        first = normed * gains[0:1] + rows[3:4]
        first_ref[strip] = first
        low_ref[strip] = first.astype(bf16)
        if keep:
            keep["first_norm"][strip] = normed
            keep["first_scale"][strip] = jnp.broadcast_to(inverse, (STRIP, SLOT))
            keep["first_low"][strip] = first.astype(bf16)
    if keep:
        done("first_norm")
        done("first_scale")
        done("first_low")
    waits[2]()
    for c in range(0, hidden, 2 * SLOT):
        cols = slice(c, c + 2 * SLOT)
        gate = dot(low_ref[...], up_ref[:, cols]) + up_bias_ref[:, cols].astype(f32)
        below = 0.5 + 0.5 * lax.erf(gate * 0.7071067811865476)
        act_ref[:, cols] = (gate * below).astype(bf16)
        if keep:
            density = jnp.exp(-0.5 * gate * gate) * 0.3989422804014327
            keep["slope"][:, cols] = (below + gate * density).astype(bf16)
    if keep:
        done("slope")
        done("act")
    waits[3]()
    sum_ref[...] = dot(act_ref[...], down_ref[...])
    for r in range(0, tokens, STRIP):
        strip = slice(r, r + STRIP)
        normed, inverse = normed_of(first_ref[strip] + sum_ref[strip] + rows[4:5])
        result_ref[strip] = (normed * gains[1:2] + rows[5:6]).astype(bf16)
        if keep:
            keep["second_norm"][strip] = normed
            keep["second_scale"][strip] = jnp.broadcast_to(inverse, (STRIP, SLOT))
    if keep:
        done("second_norm")
        done("second_scale")


def attention_back(p, pair, packed_ref, probs_ref, grad_ref, grad_packed_ref, width):
    here = slice(p * SLOT, (p + 1) * SLOT)
    at = pair * SLOT
    top = (p * HEADS + 2 * pair) * SLOT
    queries = halves(packed_ref[here, at : at + SLOT]) * (HEAD**-0.5)
    keys = halves(packed_ref[here, width + at : width + at + SLOT]) * (HEAD**-0.5)
    values = packed_ref[here, 2 * width + at : 2 * width + at + SLOT]
    grad = halves(grad_ref[here, at : at + SLOT])
    probs_low = probs_ref[top : top + 2 * SLOT, :]
    probs = probs_low.astype(f32)
    grad_probs = dot(grad, values, NT)
    inner = jnp.sum(probs * grad_probs, axis=-1, keepdims=True)
    grad_scores = (probs * (grad_probs - inner)).astype(bf16)
    for part, value in (
        (0, dot(side_by_side(grad_scores), keys)),
        (1, dot(grad_scores, queries, TN)),
        (2, dot(probs_low, grad, TN)),
    ):
        cols = slice(part * width + at, part * width + at + SLOT)
        grad_packed_ref[here, cols] = value.astype(bf16)
    return grad_scores


def first_kernel(
    tokens_ref,
    lengths_ref,
    order_ref,
    region_ref,
    column_ref,
    row_ref,
    rows_ref,
    gains_ref,
    up_bias_ref,
    taps_ref,
    table_ref,
    input_hbm,
    output_hbm,
    up_hbm,
    down_hbm,
    result_ref,
    mixed_ref,
    bias_ref,
    input_ref,
    output_ref,
    up_ref,
    down_ref,
    packed_ref,
    attended_ref,
    sum_ref,
    first_ref,
    low_ref,
    act_ref,
    sems,
):
    copies = copies_in(
        (
            (input_hbm, input_ref),
            (output_hbm, output_ref),
            (up_hbm, up_ref),
            (down_hbm, down_ref),
        ),
        sems,
    )
    conv_on = (lax.axis_index("section") == 0).astype(f32)
    taps = taps_ref[...].astype(f32) * conv_on
    conv_bias = rows_ref[...].astype(f32)[6:7] * conv_on
    for p in range(order_ref.shape[0]):
        here = slice(p * SLOT, (p + 1) * SLOT)
        order = order_ref[p : p + 1, :]
        rank_hot = rank_hot_of(order)
        masks = tap_columns(order, region_ref[p : p + 1, :], lengths_ref[p])
        ordered = dot(rank_hot, tokens_ref[here], TN)
        total = jnp.zeros_like(ordered)
        for j in range(TAPS):
            total = total + taps[j : j + 1] * shifted(ordered, j - REACH) * masks[:, j : j + 1]
        mixed_ref[here] = (
            tokens_ref[here].astype(f32) + place_rows(rank_hot, total, NN) + conv_bias
        )
    bias_body(order_ref, column_ref, row_ref, table_ref, bias_ref)
    forward_body(
        (input_ref, output_ref, up_ref, down_ref),
        [copy.wait for copy in copies],
        lengths_ref,
        (rows_ref, gains_ref, up_bias_ref),
        bias_ref,
        (
            mixed_ref,
            packed_ref,
            attended_ref,
            sum_ref,
            first_ref,
            low_ref,
            act_ref,
            result_ref,
        ),
        None,
        None,
    )


KEPT = (
    ("mixed_low", 1, 0),
    ("packed", 3, 0),
    ("probs", 0, 0),
    ("attended", 1, 0),
    ("first_norm", 1, 1),
    ("first_scale", -1, 1),
    ("first_low", 1, 0),
    ("slope", 4, 0),
    ("act", 4, 0),
    ("second_norm", 1, 1),
    ("second_scale", -1, 1),
)


def kept_shapes(tokens, width, hidden):
    shapes = []
    for name, parts, wide in KEPT:
        dims = (tokens, hidden if parts == 4 else SLOT if parts < 0 else parts * width)
        if name == "probs":
            dims = (tokens * HEADS, SLOT)
        shapes.append((dims, f32 if wide else bf16))
    return shapes


def second_kernel(
    arrived_ref,
    cotangent_ref,
    lengths_ref,
    rows_ref,
    gains_ref,
    up_bias_ref,
    mixed_hbm,
    bias_hbm,
    input_hbm,
    output_hbm,
    up_hbm,
    down_hbm,
    result_ref,
    grad_in_ref,
    *rest,
):
    count = len(KEPT)
    kept_out, rest = rest[:count], rest[count:]
    kept_list, rest = rest[:count], rest[count:]
    (
        mixed_ref,
        bias_ref,
        input_ref,
        output_ref,
        up_ref,
        down_ref,
        sum_ref,
        first_ref,
        low_ref,
        gate_ref,
        grad_ref,
        grad_packed_ref,
        sems,
        kept_sems,
    ) = rest
    tokens, width = mixed_ref.shape
    hidden = gate_ref.shape[1]
    copies = copies_in(
        (
            (mixed_hbm, mixed_ref),
            (input_hbm, input_ref),
            (bias_hbm, bias_ref),
            (output_hbm, output_ref),
            (up_hbm, up_ref),
            (down_hbm, down_ref),
        ),
        sems,
    )
    names = [name for name, _, _ in KEPT]
    keep = dict(zip(names, kept_list))
    leaving = []

    def done(name):
        at = names.index(name)
        copy = pltpu.make_async_copy(kept_list[at], kept_out[at], kept_sems.at[at])
        copy.start()
        leaving.append(copy)

    copies[0].wait()
    first_section = lax.axis_index("section") == 0
    mixed_ref[...] = jnp.where(first_section, mixed_ref[...], arrived_ref[...].astype(f32))

    def wait_input():
        copies[1].wait()
        copies[2].wait()

    forward_body(
        (input_ref, output_ref, up_ref, down_ref),
        (wait_input, copies[3].wait, copies[4].wait, copies[5].wait),
        lengths_ref,
        (rows_ref, gains_ref, up_bias_ref),
        bias_ref,
        (
            mixed_ref,
            keep["packed"],
            keep["attended"],
            sum_ref,
            first_ref,
            low_ref,
            keep["act"],
            result_ref,
        ),
        keep,
        done,
    )
    gains = gains_ref[...].astype(f32)
    for r in range(0, tokens, STRIP):
        strip = slice(r, r + STRIP)
        grad = cotangent_ref[strip].astype(f32) * gains[1:2]
        grad_sum = norm_back(grad, keep["second_norm"][strip], keep["second_scale"][strip, :1])
        first_ref[strip] = grad_sum
        low_ref[strip] = grad_sum.astype(bf16)
    gate_body(low_ref, down_ref, keep["slope"], gate_ref)
    for c in range(0, width, 2 * SLOT):
        cols = slice(c, c + 2 * SLOT)
        sum_ref[:, cols] = first_ref[:, cols] + dot(gate_ref[...], up_ref[cols, :], NT)
    for r in range(0, tokens, STRIP):
        strip = slice(r, r + STRIP)
        grad = sum_ref[strip] * gains[0:1]
        grad_mid = norm_back(grad, keep["first_norm"][strip], keep["first_scale"][strip, :1])
        first_ref[strip] = grad_mid
        low_ref[strip] = grad_mid.astype(bf16)
    grad_ref[...] = dot(low_ref[...], output_ref[...], NT).astype(bf16)
    for p in range(tokens // SLOT):
        for pair in range(PAIRS):
            attention_back(
                p, pair, keep["packed"], keep["probs"], grad_ref, grad_packed_ref, width
            )
    for c in range(0, width, 2 * SLOT):
        cols = slice(c, c + 2 * SLOT)
        grad_in = first_ref[:, cols] + dot(grad_packed_ref[...], input_ref[cols, :], NT)
        grad_in_ref[:, cols] = grad_in.astype(bf16)
    for copy in leaving:
        copy.wait()


def gate_body(grad_ref, down_ref, slope_ref, gate_ref):
    for c in range(0, gate_ref.shape[1], 2 * SLOT):
        cols = slice(c, c + 2 * SLOT)
        value = dot(grad_ref[...], down_ref[cols, :], NT) * slope_ref[:, cols].astype(f32)
        gate_ref[:, cols] = value.astype(bf16)


def store_shares(value, row, column, outs, cuts, share):
    rows, columns = value.shape
    value = value.astype(bf16)
    if not cuts:
        outs[0][row : row + rows, column : column + columns] = value
        return
    even = lax.axis_index("dp") % 2 == 0
    for pair in range(row // (2 * share), (row + rows) // (2 * share)):
        top = 2 * pair * share - row
        for i, (start, count, left, width) in enumerate(cuts):
            from_column, to_column = max(column, left), min(column + columns, left + width)
            if from_column >= to_column:
                continue
            cols = slice(from_column - column, to_column - column)
            first = value[top + start : top + start + count, cols]
            second = value[top + share + start : top + share + start + count, cols]
            cols = slice(from_column - left, to_column - left)
            at = pair % 2 * 4 + pair // 2
            outs[2 * i][at, :, cols] = jnp.where(even, second, first)
            outs[2 * i + 1][at, :, cols] = jnp.where(even, first, second)


def column_sum(value):
    return jnp.sum(value, axis=0, keepdims=True)


def down_kernel(
    cotangent_ref, arrived_ref, gains_ref, normed_ref, scale_ref, act_ref, *rest, outs, cuts, share
):
    shares_out, (grad_sum_ref, small_ref, low_ref) = rest[:outs], rest[outs:]
    tokens = low_ref.shape[0]
    hidden = act_ref.shape[1]
    gains = gains_ref[...].astype(f32)
    last = lax.axis_index("section") == lax.axis_size("section") - 1
    sums = [0.0, 0.0, 0.0]
    for r in range(0, tokens, STRIP):
        strip = slice(r, r + STRIP)
        grad_out = jnp.where(
            last, cotangent_ref[strip].astype(f32), arrived_ref[strip].astype(f32)
        )
        normed = normed_ref[strip]
        grad_sum = norm_back(grad_out * gains[1:2], normed, scale_ref[strip, :1])
        low = grad_sum.astype(bf16)
        grad_sum_ref[strip] = grad_sum
        low_ref[strip] = low
        sums[0] = sums[0] + column_sum(low.astype(f32))
        sums[1] = sums[1] + column_sum(grad_out)
        sums[2] = sums[2] + column_sum(grad_out * normed)
    step = 3 * SLOT
    for r in range(0, hidden, step):
        value = dot(act_ref[:, r : r + step], low_ref[...], TN)
        store_shares(value, r, 0, shares_out, cuts, share)
    for i, value in enumerate(sums):
        small_ref[i : i + 1, :] = value


def up_kernel(
    grad_sum_ref, slope_ref, first_low_ref, down_hbm, after, *rest, outs, cuts, share
):
    shares_out, (gate_ref, small_ref, low_ref, down_ref, sem) = rest[:outs], rest[outs:]
    (copy,) = copies_in(((down_hbm, down_ref),), sem)
    low_ref[...] = grad_sum_ref[...].astype(bf16)
    copy.wait()
    gate_body(low_ref, down_ref, slope_ref, gate_ref)
    width, hidden = first_low_ref.shape[1], gate_ref.shape[1]
    step = 3 * SLOT
    for r in range(0, width, step):
        left = first_low_ref[:, r : r + step]
        for c in range(0, hidden, width):
            value = dot(left, gate_ref[:, c : c + width], TN)
            store_shares(value, r, c, shares_out, cuts, share)
    for c in range(0, hidden, width):
        cols = slice(c, c + width)
        small_ref[:, cols] = column_sum(gate_ref[:, cols].astype(f32))


def backwards(every):
    shape = (2 * SLOT, 2 * SLOT)
    left, right = iota(shape, 0), iota(shape, 1)
    ends = jnp.where(left < SLOT, SLOT - 1, jnp.where(left < SLOT + B2D, 3 * SLOT - B2D - 1, 0))
    ends = jnp.where(left >= SLOT + B2D, 4 * SLOT - B2D - 1, ends)
    return dot(every, hot(left + right == ends)).astype(bf16)


def table_rows(sums):
    blank = jnp.zeros((SLOT, SLOT), f32)
    near = jnp.concatenate([sums[:SLOT, :SLOT], blank], axis=1)
    near = pltpu.roll(near, 0, 1, stride=1, stride_axis=0)
    lane = iota((B2D, SLOT), 1)
    across = jnp.where(lane < B2D, sums[SLOT : SLOT + B2D, SLOT:], 0.0)
    across = pltpu.roll(across, 0, 1, stride=1, stride_axis=0)
    down = jnp.where(lane >= B2D, sums[SLOT + B2D :, SLOT:], 0.0)
    down = pltpu.roll(down, B2D, 1, stride=1, stride_axis=0)
    return jnp.concatenate([column_sum(near), column_sum(across), column_sum(down)], axis=1)


def chain_kernel(
    grad_sum_ref,
    gate_ref,
    normed_ref,
    scale_ref,
    packed_ref,
    probs_ref,
    order_ref,
    column_ref,
    row_ref,
    gains_ref,
    up_hbm,
    output_hbm,
    after,
    mid_ref,
    low_ref,
    grad_packed_ref,
    small_ref,
    table_ref,
    up_ref,
    output_ref,
    sum_ref,
    grad_ref,
    reach_ref,
    weight_sems,
):
    copies = copies_in(((up_hbm, up_ref), (output_hbm, output_ref)), weight_sems)
    tokens, width = sum_ref.shape
    pages = tokens // SLOT
    gains = gains_ref[...].astype(f32)
    copies[0].wait()
    for c in range(0, width, 2 * SLOT):
        cols = slice(c, c + 2 * SLOT)
        sum_ref[:, cols] = grad_sum_ref[:, cols] + dot(gate_ref[...], up_ref[cols, :], NT)
    first_sum = gain_sum = branch_sum = 0.0
    for r in range(0, tokens, STRIP):
        strip = slice(r, r + STRIP)
        grad_first, normed = sum_ref[strip], normed_ref[strip]
        grad_mid = norm_back(grad_first * gains[0:1], normed, scale_ref[strip, :1])
        low = grad_mid.astype(bf16)
        mid_ref[strip] = grad_mid
        low_ref[strip] = low
        first_sum = first_sum + column_sum(grad_first)
        gain_sum = gain_sum + column_sum(grad_first * normed)
        branch_sum = branch_sum + column_sum(low.astype(f32))
    copies[1].wait()
    grad_ref[...] = dot(low_ref[...], output_ref[...], NT).astype(bf16)
    hots = [
        page_hot(order_ref[p : p + 1, :], column_ref[p : p + 1, :], row_ref[p : p + 1, :])
        for p in range(pages)
    ]
    every = backwards(jnp.concatenate(hots, axis=0))
    reach_ref[...] = jnp.zeros_like(reach_ref)
    for pair in range(PAIRS):
        scores = [
            attention_back(p, pair, packed_ref, probs_ref, grad_ref, grad_packed_ref, width)
            for p in range(pages)
        ]
        for head in range(2):
            rows = slice(head * SLOT, (head + 1) * SLOT)
            along = jnp.concatenate([dot(s[rows], h) for s, h in zip(scores, hots)], axis=0)
            sums = dot(every, along.astype(bf16), TN)
            at = 2 * pair + head
            reach_ref[at : at + 1, :] = table_rows(sums)
    for i, value in enumerate((first_sum, gain_sum, branch_sum)):
        small_ref[i : i + 1, :] = value
    table_ref[...] = dot(
        bucket_places().astype(f32), reach_ref[...], NT, precision=lax.Precision.HIGHEST
    )


def last_kernel(
    attended_ref, low_ref, mixed_low_ref, grad_packed_ref, after, *shares_out, outs, cuts, share
):
    width = low_ref.shape[1]
    step = 3 * SLOT
    for r in range(0, width, step):
        rows = slice(r, r + step)
        value = dot(attended_ref[:, rows], low_ref[...], TN)
        store_shares(value, r, 0, shares_out, cuts, share)
        for c in range(0, 3 * width, width):
            value = dot(mixed_low_ref[:, rows], grad_packed_ref[:, c : c + width], TN)
            store_shares(value, r, width + c, shares_out, cuts, share)


def input_kernel(
    mid_ref,
    grad_packed_ref,
    tokens_ref,
    small_down_ref,
    small_up_ref,
    small_chain_ref,
    table_ref,
    lengths_ref,
    order_ref,
    region_ref,
    taps_ref,
    input_hbm,
    after,
    *rest,
    outs,
    cuts,
    share,
):
    shares_out, rest = rest[:outs], rest[outs:]
    grad_in_ref, small_ref, input_ref, sum_ref, block_ref, weight_sems = rest
    copies = copies_in(((input_hbm, input_ref),), weight_sems)
    tokens, width = sum_ref.shape
    pages = tokens // SLOT
    conv_on = (lax.axis_index("section") == 0).astype(f32)
    taps = taps_ref[...].astype(f32) * conv_on
    copies[0].wait()
    for c in range(0, width, 2 * SLOT):
        cols = slice(c, c + 2 * SLOT)
        sum_ref[:, cols] = mid_ref[:, cols] + dot(grad_packed_ref[...], input_ref[cols, :], NT)
    tap_sums = [0.0] * TAPS
    mixed_sum = 0.0
    for p in range(pages):
        here = slice(p * SLOT, (p + 1) * SLOT)
        order = order_ref[p : p + 1, :]
        rank_hot = rank_hot_of(order)
        masks = tap_columns(order, region_ref[p : p + 1, :], lengths_ref[p])
        ordered = dot(rank_hot, tokens_ref[here], TN)
        grad_mixed = sum_ref[here]
        grad_order = place_rows(rank_hot, grad_mixed, TN)
        source = jnp.zeros_like(ordered)
        for j in range(TAPS):
            masked = grad_order * masks[:, j : j + 1]
            tap_sums[j] = tap_sums[j] + column_sum(masked * shifted(ordered, j - REACH))
            source = source + shifted(taps[j : j + 1] * masked, REACH - j)
        grad_in_ref[here] = grad_mixed + place_rows(rank_hot, source, NN)
        mixed_sum = mixed_sum + column_sum(grad_mixed)
    down, chain = small_down_ref[...], small_chain_ref[...]
    rows = [
        column_sum(grad_packed_ref[:, :width].astype(f32)),
        column_sum(grad_packed_ref[:, 2 * width :].astype(f32)),
        chain[2:3],
        chain[0:1],
        down[0:1],
        down[1:2],
        conv_on * mixed_sum,
        chain[1:2],
        down[2:3],
    ]
    for i, value in enumerate(rows + [conv_on * value for value in tap_sums]):
        small_ref[i : i + 1, :] = value
    if cuts:
        small_block(small_ref, small_up_ref, table_ref, block_ref, share)
        store_shares(block_ref[...], 0, 0, shares_out, cuts, share)


SMALL_SHARE = 32
SMALL_ROWS = 16


def small_block(small_ref, up_ref, table_ref, block_ref, share):
    width = small_ref.shape[1]
    shares = block_ref.shape[0] // share
    part = width // shares
    up_part = up_ref.shape[1] // shares
    buckets = (B1D + 2 * B2D) // shares
    block_ref[...] = jnp.zeros_like(block_ref)
    small, up = small_ref[...], jnp.broadcast_to(up_ref[...], (8, up_ref.shape[1]))
    for s in range(shares):
        top = s * share
        shift = (width - s * part) % width
        here = pltpu.roll(small, shift, 1) if shift else small
        block_ref[top : top + SMALL_ROWS, :] = here[:, :SLOT]
        shift = (up.shape[1] - s * up_part) % up.shape[1]
        here = pltpu.roll(up, shift, 1) if shift else up
        top += SMALL_ROWS
        block_ref[top : top + 1, :] = here[:1, :SLOT]
        block_ref[top + 1 : top + 2, :] = here[:1, SLOT : 2 * SLOT]
        top += 2
        block_ref[top : top + buckets, :] = table_ref[s * buckets : (s + 1) * buckets, :]


def place():
    index = lax.axis_index("dp")
    return index // 4, index // 2 % 2


def added(out_refs, *parts):
    rows = parts[0][0].shape[-2]
    for r in range(0, rows, 16):
        strip = slice(r, r + 16)
        total = 0.0
        for ref, at in parts:
            total = total + (ref[strip] if at is None else ref[at, strip]).astype(f32)
        ref, at = out_refs
        if at is None:
            ref[strip] = total.astype(ref.dtype)
        else:
            ref[at, strip] = total.astype(ref.dtype)


def leave_kernel(mine_ref, recv_ref, after, out_ref):
    first = 4 * (1 - place()[1])
    for k in range(4):
        added((out_ref, k), (mine_ref, first + k), (recv_ref, first + k))


def near_kernel(mine_ref, recv_ref, y_ref, after, leave_ref, keep_ref):
    z, y = place()
    for out_ref, parity in ((leave_ref, 1 - z % 2), (keep_ref, z % 2)):
        for k in range(2):
            block = 2 * k + parity
            at = 4 * y + block
            added((out_ref, k), (mine_ref, at), (recv_ref, at), (y_ref, block))


def far_kernel(keep_ref, recv_ref, after, leave_ref, own_ref):
    high = place()[0] // 2
    for out_ref, k in ((leave_ref, 1 - high), (own_ref, high)):
        added((out_ref, None), (keep_ref, k), (recv_ref, k))


def both(parts):
    return parts[0][...].astype(f32) + parts[1][...].astype(f32)


def down_end(*refs):
    out_ref = refs[-1]
    rows = refs[0].shape[0]
    out_ref[:rows] = both(refs[:2])
    out_ref[rows:] = both(refs[2:4])


def up_end(*refs):
    out_ref = refs[-1]
    columns = refs[0].shape[1]
    out_ref[:, :columns] = both(refs[:2])
    out_ref[:, columns:] = both(refs[2:4])


def last_end(*refs):
    left, right = both(refs[:2]), both(refs[2:4])
    input_ref, output_ref, bias_ref, gain_ref, tap_ref, up_ref, table_ref, block_ref = refs[7:]
    width, share = output_ref.shape[1], output_ref.shape[0]
    output_ref[...] = left[:, :width]
    input_ref[:, :width] = left[:, width:]
    input_ref[:, width:] = right
    block_ref[...] = both(refs[4:6])
    bias_ref[...] = block_ref[:7, :share]
    gain_ref[...] = block_ref[7:9, :share]
    tap_ref[...] = block_ref[9:16, :share]
    rest = up_ref.shape[1] - SLOT
    up_ref[:, :SLOT] = block_ref[SMALL_ROWS : SMALL_ROWS + 1, :]
    up_ref[:, SLOT:] = block_ref[SMALL_ROWS + 1 : SMALL_ROWS + 2, :rest]
    for i in range(table_ref.shape[1] // HEADS):
        at = SMALL_ROWS + 2 + i
        table_ref[:, i * HEADS : (i + 1) * HEADS] = block_ref[at : at + 1, :HEADS]


def kernel_call(body, name, ins, outs, scratch, flops=0, vmem=24):
    return pl.pallas_call(
        body,
        name=name,
        out_shape=[shape for shape, _ in outs],
        in_specs=[spec for _, spec in ins],
        out_specs=[spec for _, spec in outs],
        scratch_shapes=scratch,
        compiler_params=pltpu.CompilerParams(vmem_limit_bytes=vmem << 20),
        cost_estimate=pl.CostEstimate(flops=flops, bytes_accessed=0, transcendentals=0),
    )(*[value for value, _ in ins])


def near_by(value):
    return pltpu.with_memory_space_constraint(value, pltpu.VMEM)


def near_shape(dims):
    return pltpu.VMEM(dims, bf16)


class Summing:
    def __init__(self):
        self.mine, self.recv, self.crossed, self.kept, self.ends = {}, {}, {}, {}, {}

    @staticmethod
    def _swap(value, bits):
        return near_by(lax.ppermute(value, "dp", [(i, i ^ bits) for i in range(16)]))

    @staticmethod
    def _add(body, name, ins, after, outs, cost=0):
        return kernel_call(
            body,
            name,
            [(near_by(value), IN_VMEM) for value in ins] + [(after, IN_PLACE)],
            [(near_shape(dims), IN_VMEM) for dims in outs],
            [],
            cost,
            4,
        )

    def core(self, name, theirs, mine):
        self.mine[name], self.recv[name] = mine, self._swap(theirs, 1)

    def leave(self, name, after):
        mine, recv = self.mine[name], self.recv[name]
        (out,) = self._add(leave_kernel, "leave", [mine, recv], after, [(4,) + mine.shape[1:]])
        self.crossed[name] = self._swap(out, 2)
        return out

    def near(self, name, after):
        ins = [self.mine[name], self.recv[name], self.crossed[name]]
        dims = (2,) + ins[0].shape[1:]
        out, keep = self._add(near_kernel, "near", ins, after, [dims, dims], COST)
        self.kept[name] = [keep, self._swap(out, 4)]
        return out

    def far(self, name, after):
        ins = self.kept[name]
        dims = ins[0].shape[1:]
        out, own = self._add(far_kernel, "far", ins, after, [dims, dims], COST)
        self.ends[name] = [own, self._swap(out, 8)]
        return out


def local(
    tokens,
    cotangent,
    page_lengths,
    cut_order,
    cut_region,
    cell_column,
    cell_row,
    input_proj,
    output_proj,
    up_proj,
    down_proj,
    up_bias,
    bias_rows,
    gain_rows,
    conv_taps,
    bias_table,
):
    section_count = lax.axis_size("section")
    dp_count = lax.axis_size("dp")
    by_hops = dp_count == 16
    pages, _, width = tokens.shape
    hidden = up_proj.shape[2]
    count = pages * SLOT
    weights = [w[0] for w in (input_proj, output_proj, up_proj, down_proj)]
    input_w, output_w, up_w, down_w = weights
    rows, gains, taps = bias_rows[0], gain_rows[0], conv_taps[0]
    tokens, cotangent = tokens.reshape(count, width), cotangent.reshape(count, width)

    def shape(dims, kind):
        return jax.ShapeDtypeStruct(dims, kind)

    def inside(*values):
        return [(v, IN_VMEM) for v in values]

    def in_place(*values):
        return [(v, IN_PLACE) for v in values]

    def scalars(*values):
        return [(v, IN_SMEM) for v in values]

    wide, low = shape((count, width), f32), shape((count, width), bf16)
    weight_scratch = [pltpu.VMEM(w.shape, w.dtype) for w in weights]
    wide_scratch = pltpu.VMEM((count, width), f32)
    low_scratch = pltpu.VMEM((count, width), bf16)
    packed_scratch = pltpu.VMEM((count, 3 * width), bf16)
    hidden_scratch = pltpu.VMEM((count, hidden), bf16)
    bias_dims = (pages * HEADS * SLOT, SLOT)

    def sems(number):
        return pltpu.SemaphoreType.DMA((number,))

    result, mixed, bias = kernel_call(
        first_kernel,
        "first",
        inside(tokens)
        + scalars(page_lengths)
        + inside(cut_order, cut_region, cell_column, cell_row, rows, gains, up_bias, taps)
        + inside(bias_table)
        + in_place(*weights),
        inside(low, wide, shape(bias_dims, f32)),
        weight_scratch
        + [
            packed_scratch,
            low_scratch,
            wide_scratch,
            wide_scratch,
            low_scratch,
            hidden_scratch,
            sems(4),
        ],
        vmem=56,
    )
    arrived = near_by(
        lax.ppermute(result, "section", [(i, i + 1) for i in range(section_count - 1)])
    )
    shapes = kept_shapes(count, width, hidden)
    layer_out, leaving, *kept_list = kernel_call(
        second_kernel,
        "second",
        inside(arrived, cotangent)
        + scalars(page_lengths)
        + inside(rows, gains, up_bias)
        + in_place(mixed, bias, *weights),
        inside(low, low) + in_place(*[shape(*s) for s in shapes]),
        [pltpu.VMEM(*s) for s in shapes]
        + [wide_scratch, pltpu.VMEM(bias_dims, f32)]
        + weight_scratch
        + [
            wide_scratch,
            wide_scratch,
            low_scratch,
            hidden_scratch,
            low_scratch,
            packed_scratch,
            sems(6),
            sems(len(KEPT)),
        ],
        vmem=56,
    )
    kept = dict(zip([name for name, _, _ in KEPT], kept_list))
    arrived_grad = near_by(
        lax.ppermute(leaving, "section", [(i + 1, i) for i in range(section_count - 1)])
    )
    part = width // dp_count

    def cut(dims, cuts):
        share = dims[0] // dp_count
        if not by_hops:
            outs, cuts = inside(shape(dims, bf16)), ()
        else:
            halves_out = [near_shape((dp_count // 2, c[1], c[3])) for c in cuts for _ in range(2)]
            outs = inside(*halves_out)
        return outs, dict(outs=len(outs), cuts=cuts, share=share)

    half = hidden // dp_count // 2
    down_outs, down_cut = cut(
        (hidden, width), ((0, half, 0, width), (half, half, 0, width))
    )
    *down_parts, grad_sum, small_down = kernel_call(
        functools.partial(down_kernel, **down_cut),
        "down",
        inside(cotangent, arrived_grad, gains)
        + inside(kept["second_norm"], kept["second_scale"], kept["act"]),
        down_outs + inside(wide, shape((8, width), f32)),
        [low_scratch],
    )
    summing = Summing()
    after = grad_sum
    if by_hops:
        summing.core("d1", *down_parts[:2])
        summing.core("d2", *down_parts[2:])
        after = summing.leave("d1", after)
    half = hidden // 2
    up_outs, up_cut = cut(
        (width, hidden), ((0, part, 0, half), (0, part, half, half))
    )
    *up_parts, gate, small_up = kernel_call(
        functools.partial(up_kernel, **up_cut),
        "up",
        inside(grad_sum, kept["slope"], kept["first_low"]) + in_place(down_w, after),
        up_outs + inside(shape((count, hidden), bf16), shape((1, hidden), f32)),
        [
            low_scratch,
            weight_scratch[3],
            sems(1),
        ],
    )
    after = gate
    if by_hops:
        summing.core("u1", *up_parts[:2])
        summing.core("u2", *up_parts[2:])
        after = summing.leave("d2", after)
    grad_mid, grad_branch, grad_packed, small_chain, table = kernel_call(
        chain_kernel,
        "chain",
        inside(grad_sum, gate, kept["first_norm"], kept["first_scale"], kept["packed"])
        + inside(kept["probs"], cut_order, cell_column, cell_row, gains)
        + in_place(up_w, output_w, after),
        inside(wide, low, shape((count, 3 * width), bf16), shape((8, width), f32))
        + inside(shape((B1D + 2 * B2D, SLOT), f32)),
        [
            weight_scratch[2],
            weight_scratch[1],
            wide_scratch,
            low_scratch,
            pltpu.VMEM((SLOT, 4 * SLOT), f32),
            sems(2),
        ],
    )
    after = grad_mid
    if by_hops:
        after = summing.near("d1", after)
        after = summing.leave("u1", after)
    last_outs, last_cut = cut(
        (width, 4 * width), ((0, part, 0, 2 * width), (0, part, 2 * width, 2 * width))
    )
    last_parts = kernel_call(
        functools.partial(last_kernel, **last_cut),
        "last",
        inside(kept["attended"], grad_branch, kept["mixed_low"], grad_packed) + in_place(after),
        last_outs,
        [],
    )
    after = last_parts[0]
    if by_hops:
        summing.core("a1", *last_parts[:2])
        summing.core("a2", *last_parts[2:])
        after = summing.leave("u2", after)
        after = summing.near("d2", after)
        after = summing.far("d1", after)
    block = (dp_count * SMALL_SHARE, SLOT)
    small_outs, small_cut = cut(block, ((0, SMALL_SHARE, 0, SLOT),))
    *small_parts, grad_in, small_rows = kernel_call(
        functools.partial(input_kernel, **small_cut),
        "input",
        inside(grad_mid, grad_packed, tokens, small_down, small_up, small_chain, table)
        + scalars(page_lengths)
        + inside(cut_order, cut_region, taps)
        + in_place(input_w, after),
        small_outs + inside(wide, shape((16, width), f32)),
        [
            weight_scratch[0],
            wide_scratch,
            pltpu.VMEM(block, f32),
            sems(1),
        ],
    )
    if by_hops:
        summing.core("s", *small_parts)
        ends = summing.ends
        after = summing.near("u1", grad_in)
        after = summing.leave("a1", after)
        after = summing.leave("a2", after)
        after = summing.near("u2", after)
        after = summing.far("d2", after)
        after = summing.far("u1", after)
        after = summing.leave("s", after)
        (after,) = (down_grad,) = kernel_call(
            down_end,
            "down_end",
            inside(*map(near_by, ends["d1"] + ends["d2"])) + in_place(after),
            inside(shape((hidden // dp_count, width), f32)),
            [],
            vmem=4,
        )
        after = summing.far("u2", after)
        after = summing.near("a1", after)
        (after,) = (up_grad,) = kernel_call(
            up_end,
            "up_end",
            inside(*map(near_by, ends["u1"] + ends["u2"])) + in_place(after),
            inside(shape((part, hidden), f32)),
            [],
            vmem=4,
        )
        after = summing.near("a2", after)
        after = summing.far("a1", after)
        after = summing.near("s", after)
        after = summing.far("s", after)
        after = summing.far("a2", after)
        input_grad, output_grad, bias_grad, gain_grad, tap_grad, up_bias_grad, table_grad = (
            kernel_call(
                last_end,
                "last_end",
                inside(*map(near_by, ends["a1"] + ends["a2"] + ends["s"])) + in_place(after),
                inside(
                    shape((part, 3 * width), f32),
                    shape((part, width), f32),
                    shape((7, part), f32),
                    shape((2, part), f32),
                    shape((TAPS, part), f32),
                    shape((1, hidden // dp_count), f32),
                    shape((1, table.shape[0] * HEADS // dp_count), f32),
                ),
                [pltpu.VMEM((SMALL_SHARE, SLOT), f32)],
                vmem=4,
            )
        )
    else:

        def scattered(value):
            return lax.psum_scatter(value, "dp", scatter_dimension=0, tiled=True).astype(f32)

        down_grad, up_grad, last_grad = (
            scattered(parts[0]) for parts in (down_parts, up_parts, last_parts)
        )
        input_grad, output_grad = last_grad[:, width:], last_grad[:, :width]
        small = [
            small_rows.reshape(16, dp_count, part).transpose(1, 0, 2).reshape(dp_count, -1),
            small_up.reshape(dp_count, -1),
            table[:, :HEADS].reshape(dp_count, -1),
        ]
        small = jnp.concatenate(small, axis=1)
        used = small.shape[1]
        small = jnp.pad(small, ((0, 0), (0, -used % SLOT))).reshape(-1, SLOT)
        small = scattered(small).reshape(-1)
        vectors = small[: 16 * part].reshape(16, part)
        bias_grad, gain_grad, tap_grad = vectors[:7], vectors[7:9], vectors[9:]
        at = 16 * part + hidden // dp_count
        up_bias_grad, table_grad = small[None, 16 * part : at], small[None, at:used]
    return (
        layer_out.reshape(1, pages, SLOT, width),
        grad_in.reshape(1, pages, SLOT, width),
        input_grad[None],
        output_grad[None],
        up_grad[None],
        down_grad[None],
        up_bias_grad,
        bias_grad[None],
        gain_grad[None],
        tap_grad[None],
        table_grad,
    )


def solution(mesh):
    by_section = [P("section", None, None)] * 4
    placed = (
        P("dp", None, None),
        P("dp", None, None),
        P("dp"),
        P("dp", None),
        P("dp", None),
        P("dp", None),
        P("dp", None),
        *by_section,
        P("section", None),
        P("section", None, None),
        P("section", None, None),
        P("section", None, None),
        P("section", None),
    )
    return jax.shard_map(
        local,
        mesh=mesh,
        in_specs=placed,
        out_specs=(
            P("section", "dp", None, None),
            P("section", "dp", None, None),
            P("section", "dp", None),
            P("section", "dp", None),
            P("section", "dp", None),
            P("section", "dp", None),
            P("section", "dp"),
            P("section", None, "dp"),
            P("section", None, "dp"),
            P("section", None, "dp"),
            P("section", "dp"),
        ),
        check_vma=False,
    )
```

```python
import functools

import jax
import jax.numpy as jnp
from jax import lax
from jax.experimental import pallas as pl
from jax.experimental.pallas import tpu as pltpu
from jax.sharding import PartitionSpec as P

HEADS = 12
HEAD = 64
B1D = 32
B2D = 64
SLOT = 128
PAIRS = HEADS // 2
TAPS = 7
REACH = 3
EPSILON = 1e-05
COST = 100_000_000_000
LEFT_COLUMNS = 2048
MASKED = -1000000000.0
STRIP = 64

f32 = jnp.float32
bf16 = jnp.bfloat16
NN = ((1,), (0,))
NT = ((1,), (1,))
TN = ((0,), (0,))

IN_VMEM = pl.BlockSpec(memory_space=pltpu.VMEM)
IN_SMEM = pl.BlockSpec(memory_space=pltpu.SMEM)
IN_PLACE = pl.BlockSpec(memory_space=pl.ANY)


def dot(left, right, dims=NN, precision=None):
    return lax.dot_general(
        left, right, (dims, ((), ())), precision=precision, preferred_element_type=f32
    )


def iota(shape, axis):
    return lax.broadcasted_iota(jnp.int32, shape, axis)


def hot(mask):
    return mask.astype(f32).astype(bf16)


def identity():
    return hot(iota((SLOT, SLOT), 0) == iota((SLOT, SLOT), 1))


def rank_hot_of(order):
    return hot(order == iota((SLOT, SLOT), 0))


def page_hot(order, column, row):
    cells = iota((SLOT, SLOT), 0)
    wanted = jnp.where(cells < B2D, column, row + B2D)
    cell_hot = dot(identity(), hot(wanted == cells), NT).astype(bf16)
    return jnp.concatenate([rank_hot_of(order), cell_hot], axis=1)


def tap_columns(order, region, length):
    shape = (8, SLOT)
    order, region = jnp.broadcast_to(order, shape), jnp.broadcast_to(region, shape)
    live = (order < length).astype(jnp.int32)
    lane, tap = iota(shape, 1), iota(shape, 0)
    masks = jnp.zeros(shape, f32)
    for j in range(TAPS):
        offset = j - REACH
        shift = (-offset) % SLOT
        region_j = pltpu.roll(region, shift, 1) if shift else region
        live_j = pltpu.roll(live, shift, 1) if shift else live
        joined = (lane + offset >= 0) & (lane + offset < SLOT) & (region_j == region) & (live_j > 0)
        masks = jnp.where((tap == j) & joined, 1.0, masks)
    return dot(identity(), masks.astype(bf16), NT)


def shifted(rows, offset):
    shift = (-offset) % SLOT
    return pltpu.roll(rows, shift, 0) if shift else rows


def place_rows(rank_hot, rows, dims):
    high = rows.astype(bf16)
    low = (rows - high.astype(f32)).astype(bf16)
    return dot(rank_hot, high, dims) + dot(rank_hot, low, dims)


def bucket_places():
    shape = (B1D + 2 * B2D, 4 * SLOT)
    bucket, lane = iota(shape, 0), iota(shape, 1)
    near = jnp.clip(lane - (SLOT - 1) + B1D // 2, 0, B1D - 1)
    column = B1D + jnp.clip(lane - 2 * SLOT - (B2D - 1) + B2D // 2, 0, B2D - 1)
    row = B1D + B2D + jnp.clip(lane - 3 * SLOT - (B2D - 1) + B2D // 2, 0, B2D - 1)
    wanted = jnp.where(lane < 2 * SLOT, near, jnp.where(lane < 3 * SLOT, column, row))
    return bucket == wanted


def halves(pair):
    lane = iota((1, SLOT), 1)
    first = hot(lane < HEAD)
    second = hot(lane >= HEAD)
    return jnp.concatenate([pair * first, pair * second], axis=0)


def side_by_side(stacked):
    return jnp.concatenate([stacked[:SLOT], stacked[SLOT:]], axis=1)


def normed_of(value):
    average = jnp.mean(value, axis=-1, keepdims=True)
    centered = value - average
    spread = jnp.mean(centered * centered, axis=-1, keepdims=True)
    inverse = lax.rsqrt(spread + EPSILON)
    return centered * inverse, inverse


def norm_back(grad, normed, inverse):
    first_mean = jnp.mean(grad, axis=-1, keepdims=True)
    second_mean = jnp.mean(grad * normed, axis=-1, keepdims=True)
    return inverse * (grad - first_mean - normed * second_mean)


def table_columns(table):
    buckets = table.shape[1] // HEADS
    bucket = iota((buckets, table.shape[1]), 0) * HEADS
    lane = iota((buckets, table.shape[1]), 1)
    own = hot((lane >= bucket) & (lane < bucket + HEADS))
    lane = iota((16, table.shape[1]), 1)
    times = ((lane.astype(f32) + 0.5) * (1.0 / HEADS)).astype(jnp.int32)
    head = hot(lane - HEADS * times == iota((16, table.shape[1]), 0))
    return dot(own * table, head, NT).astype(bf16)


def bias_body(order_ref, column_ref, row_ref, table_ref, bias_ref):
    pages = order_ref.shape[0]
    hots = [
        page_hot(order_ref[p : p + 1, :], column_ref[p : p + 1, :], row_ref[p : p + 1, :])
        for p in range(pages)
    ]
    every = jnp.concatenate(hots, axis=0)
    reach = dot(table_columns(table_ref[...]), hot(bucket_places()), TN)
    lane = iota((B2D, SLOT), 1)
    for h in range(HEADS):
        row = reach[h : h + 1, :]
        near = jnp.broadcast_to(row[:, : 2 * SLOT], (SLOT, 2 * SLOT))
        near = pltpu.roll(near, SLOT + 1, 1, stride=1, stride_axis=0)[:, :SLOT]
        across = jnp.broadcast_to(row[:, 2 * SLOT : 3 * SLOT], (B2D, SLOT))
        across = pltpu.roll(across, B2D + 1, 1, stride=1, stride_axis=0)
        down = jnp.broadcast_to(row[:, 3 * SLOT :], (B2D, SLOT))
        down = pltpu.roll(down, 1, 1, stride=1, stride_axis=0)
        cells = jnp.concatenate(
            [jnp.where(lane < B2D, across, 0.0), jnp.where(lane >= B2D, down, 0.0)], axis=0
        )
        blank = jnp.zeros((SLOT, SLOT), bf16)
        grid = jnp.concatenate(
            [
                jnp.concatenate([near.astype(bf16), blank], axis=1),
                jnp.concatenate([blank, cells.astype(bf16)], axis=1),
            ],
            axis=0,
        )
        rows = dot(every, grid).astype(bf16)
        for p in range(pages):
            at = (p * HEADS + h) * SLOT
            bias_ref[at : at + SLOT, :] = dot(rows[p * SLOT : (p + 1) * SLOT], hots[p], NT)


def forward_body(weights, waits, lengths_ref, vectors, bias_ref, work, keep):
    input_ref, output_ref, up_ref, down_ref = weights
    rows_ref, gains_ref, up_bias_ref = vectors
    mixed_ref, packed_ref, attended_ref, sum_ref, first_ref, low_ref, act_ref, result_ref = work
    rows, gains = rows_ref[...].astype(f32), gains_ref[...].astype(f32)
    tokens, width = mixed_ref.shape
    hidden = act_ref.shape[1]
    low_ref[...] = mixed_ref[...].astype(bf16)
    if keep:
        keep["mixed_low"][...] = low_ref[...]
    waits[0]()
    for part, add in ((0, rows[0:1]), (1, None), (2, rows[1:2])):
        cols = slice(part * width, (part + 1) * width)
        value = dot(low_ref[...], input_ref[:, cols])
        packed_ref[:, cols] = (value if add is None else value + add).astype(bf16)
    for p in range(tokens // SLOT):
        live = iota((2 * SLOT, SLOT), 1) < lengths_ref[p]
        here = slice(p * SLOT, (p + 1) * SLOT)
        for pair in range(PAIRS):
            at = pair * SLOT
            queries = halves(packed_ref[here, at : at + SLOT]) * (HEAD**-0.5)
            keys = packed_ref[here, width + at : width + at + SLOT]
            values = packed_ref[here, 2 * width + at : 2 * width + at + SLOT]
            top = (p * HEADS + 2 * pair) * SLOT
            scores = dot(queries, keys, NT) + bias_ref[top : top + 2 * SLOT, :]
            scores = jnp.where(live, scores, MASKED)
            expo = jnp.exp(scores - jnp.max(scores, axis=-1, keepdims=True))
            probs = (expo * (1.0 / jnp.sum(expo, axis=-1, keepdims=True))).astype(bf16)
            if keep:
                keep["probs"][top : top + 2 * SLOT, :] = probs
            attended_ref[here, at : at + SLOT] = dot(side_by_side(probs), halves(values)).astype(
                bf16
            )
    waits[1]()
    sum_ref[...] = dot(attended_ref[...], output_ref[...])
    for r in range(0, tokens, STRIP):
        strip = slice(r, r + STRIP)
        normed, inverse = normed_of(mixed_ref[strip] + sum_ref[strip] + rows[2:3])
        first = normed * gains[0:1] + rows[3:4]
        first_ref[strip] = first
        low_ref[strip] = first.astype(bf16)
        if keep:
            keep["first_norm"][strip] = normed
            keep["first_scale"][strip] = jnp.broadcast_to(inverse, (STRIP, SLOT))
            keep["first_low"][strip] = first.astype(bf16)
    waits[2]()
    for c in range(0, hidden, 2 * SLOT):
        cols = slice(c, c + 2 * SLOT)
        gate = dot(low_ref[...], up_ref[:, cols]) + up_bias_ref[:, cols].astype(f32)
        below = 0.5 + 0.5 * lax.erf(gate * 0.7071067811865476)
        act_ref[:, cols] = (gate * below).astype(bf16)
        if keep:
            density = jnp.exp(-0.5 * gate * gate) * 0.3989422804014327
            keep["slope"][:, cols] = (below + gate * density).astype(bf16)
    waits[3]()
    sum_ref[...] = dot(act_ref[...], down_ref[...])
    for r in range(0, tokens, STRIP):
        strip = slice(r, r + STRIP)
        normed, inverse = normed_of(first_ref[strip] + sum_ref[strip] + rows[4:5])
        result_ref[strip] = (normed * gains[1:2] + rows[5:6]).astype(bf16)
        if keep:
            keep["second_norm"][strip] = normed
            keep["second_scale"][strip] = jnp.broadcast_to(inverse, (STRIP, SLOT))


def attention_back(p, pair, packed_ref, probs_ref, grad_ref, grad_packed_ref, width):
    here = slice(p * SLOT, (p + 1) * SLOT)
    at = pair * SLOT
    top = (p * HEADS + 2 * pair) * SLOT
    queries = halves(packed_ref[here, at : at + SLOT]) * (HEAD**-0.5)
    keys = halves(packed_ref[here, width + at : width + at + SLOT]) * (HEAD**-0.5)
    values = packed_ref[here, 2 * width + at : 2 * width + at + SLOT]
    grad = halves(grad_ref[here, at : at + SLOT])
    probs_low = probs_ref[top : top + 2 * SLOT, :]
    probs = probs_low.astype(f32)
    grad_probs = dot(grad, values, NT)
    inner = jnp.sum(probs * grad_probs, axis=-1, keepdims=True)
    grad_scores = (probs * (grad_probs - inner)).astype(bf16)
    for part, value in (
        (0, dot(side_by_side(grad_scores), keys)),
        (1, dot(grad_scores, queries, TN)),
        (2, dot(probs_low, grad, TN)),
    ):
        cols = slice(part * width + at, part * width + at + SLOT)
        grad_packed_ref[here, cols] = value.astype(bf16)
    return grad_scores


def first_kernel(lengths_ref, *rest):
    ins, weight_ins, rest = rest[:10], rest[10:14], rest[14:]
    result_ref, mixed_ref, bias_ref, *weights = rest[:7]
    packed_ref, attended_ref, sum_ref, first_ref, low_ref, act_ref = rest[7:13]
    held, sems = rest[13:23], rest[23]
    small = [pltpu.make_async_copy(a, b, sems.at[i]) for i, (a, b) in enumerate(zip(ins, held))]
    copies = [
        pltpu.make_async_copy(a, b, sems.at[len(small) + i])
        for i, (a, b) in enumerate(zip(weight_ins, weights))
    ]
    for copy in small:
        copy.start()
    copies[0].start()
    for copy in small:
        copy.wait()
    tokens_ref, order_ref, region_ref, column_ref, row_ref = held[:5]
    rows_ref, gains_ref, up_bias_ref, taps_ref, table_ref = held[5:]
    conv_on = (lax.axis_index("section") == 0).astype(f32)
    taps = taps_ref[...].astype(f32) * conv_on
    conv_bias = rows_ref[...].astype(f32)[6:7] * conv_on
    for p in range(order_ref.shape[0]):
        here = slice(p * SLOT, (p + 1) * SLOT)
        order = order_ref[p : p + 1, :]
        rank_hot = rank_hot_of(order)
        masks = tap_columns(order, region_ref[p : p + 1, :], lengths_ref[p])
        ordered = dot(rank_hot, tokens_ref[here], TN)
        total = jnp.zeros_like(ordered)
        for j in range(TAPS):
            total = total + taps[j : j + 1] * shifted(ordered, j - REACH) * masks[:, j : j + 1]
        mixed_ref[here] = (
            tokens_ref[here].astype(f32) + place_rows(rank_hot, total, NN) + conv_bias
        )
    copies[1].start()
    copies[2].start()
    bias_body(order_ref, column_ref, row_ref, table_ref, bias_ref)

    def wait_input():
        copies[0].wait()
        copies[3].start()

    forward_body(
        weights,
        [wait_input] + [copy.wait for copy in copies[1:]],
        lengths_ref,
        (rows_ref, gains_ref, up_bias_ref),
        bias_ref,
        (
            mixed_ref,
            packed_ref,
            attended_ref,
            sum_ref,
            first_ref,
            low_ref,
            act_ref,
            result_ref,
        ),
        None,
    )


KEPT = (
    ("mixed_low", 1, 0),
    ("packed", 3, 0),
    ("probs", 0, 0),
    ("attended", 1, 0),
    ("first_norm", 1, 1),
    ("first_scale", -1, 1),
    ("first_low", 1, 0),
    ("slope", 4, 0),
    ("act", 4, 0),
    ("second_norm", 1, 1),
    ("second_scale", -1, 1),
)


def kept_shapes(tokens, width, hidden):
    shapes = []
    for name, parts, wide in KEPT:
        dims = (tokens, hidden if parts == 4 else SLOT if parts < 0 else parts * width)
        if name == "probs":
            dims = (tokens * HEADS, SLOT)
        shapes.append((dims, f32 if wide else bf16))
    return shapes


def second_kernel(
    arrived_ref,
    cotangent_ref,
    lengths_ref,
    rows_ref,
    gains_ref,
    up_bias_ref,
    mixed_in_ref,
    bias_ref,
    input_ref,
    output_ref,
    up_ref,
    down_ref,
    result_ref,
    grad_in_ref,
    *rest,
):
    kept_list, rest = rest[: len(KEPT)], rest[len(KEPT) :]
    mixed_ref, sum_ref, first_ref, low_ref, gate_ref, grad_ref, grad_packed_ref = rest
    tokens, width = mixed_ref.shape
    keep = dict(zip([name for name, _, _ in KEPT], kept_list))
    first_section = lax.axis_index("section") == 0
    mixed_ref[...] = jnp.where(first_section, mixed_in_ref[...], arrived_ref[...].astype(f32))
    forward_body(
        (input_ref, output_ref, up_ref, down_ref),
        [lambda: None] * 4,
        lengths_ref,
        (rows_ref, gains_ref, up_bias_ref),
        bias_ref,
        (
            mixed_ref,
            keep["packed"],
            keep["attended"],
            sum_ref,
            first_ref,
            low_ref,
            keep["act"],
            result_ref,
        ),
        keep,
    )
    gains = gains_ref[...].astype(f32)
    for r in range(0, tokens, STRIP):
        strip = slice(r, r + STRIP)
        grad = cotangent_ref[strip].astype(f32) * gains[1:2]
        grad_sum = norm_back(grad, keep["second_norm"][strip], keep["second_scale"][strip, :1])
        first_ref[strip] = grad_sum
        low_ref[strip] = grad_sum.astype(bf16)
    gate_body(low_ref, down_ref, keep["slope"], gate_ref)
    for c in range(0, width, 2 * SLOT):
        cols = slice(c, c + 2 * SLOT)
        sum_ref[:, cols] = first_ref[:, cols] + dot(gate_ref[...], up_ref[cols, :], NT)
    for r in range(0, tokens, STRIP):
        strip = slice(r, r + STRIP)
        grad = sum_ref[strip] * gains[0:1]
        grad_mid = norm_back(grad, keep["first_norm"][strip], keep["first_scale"][strip, :1])
        first_ref[strip] = grad_mid
        low_ref[strip] = grad_mid.astype(bf16)
    grad_ref[...] = dot(low_ref[...], output_ref[...], NT).astype(bf16)
    for p in range(tokens // SLOT):
        for pair in range(PAIRS):
            attention_back(
                p, pair, keep["packed"], keep["probs"], grad_ref, grad_packed_ref, width
            )
    for c in range(0, width, 2 * SLOT):
        cols = slice(c, c + 2 * SLOT)
        grad_in = first_ref[:, cols] + dot(grad_packed_ref[...], input_ref[cols, :], NT)
        grad_in_ref[:, cols] = grad_in.astype(bf16)


def gate_body(grad_ref, down_ref, slope_ref, gate_ref):
    for c in range(0, gate_ref.shape[1], 2 * SLOT):
        cols = slice(c, c + 2 * SLOT)
        value = dot(grad_ref[...], down_ref[cols, :], NT) * slope_ref[:, cols].astype(f32)
        gate_ref[:, cols] = value.astype(bf16)


def store_shares(value, row, column, outs, cuts, share):
    rows, columns = value.shape
    value = value.astype(bf16)
    if not cuts:
        outs[0][row : row + rows, column : column + columns] = value
        return
    even = lax.axis_index("dp") % 2 == 0
    for pair in range(row // (2 * share), (row + rows) // (2 * share)):
        top = 2 * pair * share - row
        for i, (start, count, left, width) in enumerate(cuts):
            from_column, to_column = max(column, left), min(column + columns, left + width)
            if from_column >= to_column:
                continue
            cols = slice(from_column - column, to_column - column)
            first = value[top + start : top + start + count, cols]
            second = value[top + share + start : top + share + start + count, cols]
            cols = slice(from_column - left, to_column - left)
            at = pair % 2 * 4 + pair // 2
            outs[2 * i][at, :, cols] = jnp.where(even, second, first)
            outs[2 * i + 1][at, :, cols] = jnp.where(even, first, second)


def column_sum(value):
    return jnp.sum(value, axis=0, keepdims=True)


def down_kernel(
    cotangent_ref, arrived_ref, gains_ref, normed_ref, scale_ref, act_ref, *rest, outs, cuts, share
):
    shares_out, (grad_sum_ref, small_ref, low_ref) = rest[:outs], rest[outs:]
    tokens = low_ref.shape[0]
    hidden = act_ref.shape[1]
    gains = gains_ref[...].astype(f32)
    last = lax.axis_index("section") == lax.axis_size("section") - 1
    sums = [0.0, 0.0, 0.0]
    for r in range(0, tokens, STRIP):
        strip = slice(r, r + STRIP)
        grad_out = jnp.where(
            last, cotangent_ref[strip].astype(f32), arrived_ref[strip].astype(f32)
        )
        normed = normed_ref[strip]
        grad_sum = norm_back(grad_out * gains[1:2], normed, scale_ref[strip, :1])
        low = grad_sum.astype(bf16)
        grad_sum_ref[strip] = grad_sum
        low_ref[strip] = low
        sums[0] = sums[0] + column_sum(low.astype(f32))
        sums[1] = sums[1] + column_sum(grad_out)
        sums[2] = sums[2] + column_sum(grad_out * normed)
    step = 3 * SLOT
    for r in range(0, hidden, step):
        value = dot(act_ref[:, r : r + step], low_ref[...], TN)
        store_shares(value, r, 0, shares_out, cuts, share)
    for i, value in enumerate(sums):
        small_ref[i : i + 1, :] = value


def up_kernel(
    grad_sum_ref, slope_ref, first_low_ref, down_ref, after, *rest, outs, cuts, share
):
    shares_out, (gate_ref, small_ref, low_ref) = rest[:outs], rest[outs:]
    low_ref[...] = grad_sum_ref[...].astype(bf16)
    gate_body(low_ref, down_ref, slope_ref, gate_ref)
    width, hidden = first_low_ref.shape[1], gate_ref.shape[1]
    step = 3 * SLOT
    for r in range(0, width, step):
        left = first_low_ref[:, r : r + step]
        for c in range(0, hidden, width):
            value = dot(left, gate_ref[:, c : c + width], TN)
            store_shares(value, r, c, shares_out, cuts, share)
    for c in range(0, hidden, width):
        cols = slice(c, c + width)
        small_ref[:, cols] = column_sum(gate_ref[:, cols].astype(f32))


def backwards(every):
    shape = (2 * SLOT, 2 * SLOT)
    left, right = iota(shape, 0), iota(shape, 1)
    ends = jnp.where(left < SLOT, SLOT - 1, jnp.where(left < SLOT + B2D, 3 * SLOT - B2D - 1, 0))
    ends = jnp.where(left >= SLOT + B2D, 4 * SLOT - B2D - 1, ends)
    return dot(every, hot(left + right == ends)).astype(bf16)


def table_rows(sums):
    blank = jnp.zeros((SLOT, SLOT), f32)
    near = jnp.concatenate([sums[:SLOT, :SLOT], blank], axis=1)
    near = pltpu.roll(near, 0, 1, stride=1, stride_axis=0)
    lane = iota((B2D, SLOT), 1)
    across = jnp.where(lane < B2D, sums[SLOT : SLOT + B2D, SLOT:], 0.0)
    across = pltpu.roll(across, 0, 1, stride=1, stride_axis=0)
    down = jnp.where(lane >= B2D, sums[SLOT + B2D :, SLOT:], 0.0)
    down = pltpu.roll(down, B2D, 1, stride=1, stride_axis=0)
    return jnp.concatenate([column_sum(near), column_sum(across), column_sum(down)], axis=1)


def chain_kernel(
    grad_sum_ref,
    gate_ref,
    normed_ref,
    scale_ref,
    packed_ref,
    probs_ref,
    order_ref,
    column_ref,
    row_ref,
    gains_ref,
    up_ref,
    output_ref,
    after,
    mid_ref,
    low_ref,
    grad_packed_ref,
    small_ref,
    table_ref,
    sum_ref,
    grad_ref,
    reach_ref,
):
    tokens, width = sum_ref.shape
    pages = tokens // SLOT
    gains = gains_ref[...].astype(f32)
    for c in range(0, width, 2 * SLOT):
        cols = slice(c, c + 2 * SLOT)
        sum_ref[:, cols] = grad_sum_ref[:, cols] + dot(gate_ref[...], up_ref[cols, :], NT)
    first_sum = gain_sum = branch_sum = 0.0
    for r in range(0, tokens, STRIP):
        strip = slice(r, r + STRIP)
        grad_first, normed = sum_ref[strip], normed_ref[strip]
        grad_mid = norm_back(grad_first * gains[0:1], normed, scale_ref[strip, :1])
        low = grad_mid.astype(bf16)
        mid_ref[strip] = grad_mid
        low_ref[strip] = low
        first_sum = first_sum + column_sum(grad_first)
        gain_sum = gain_sum + column_sum(grad_first * normed)
        branch_sum = branch_sum + column_sum(low.astype(f32))
    grad_ref[...] = dot(low_ref[...], output_ref[...], NT).astype(bf16)
    hots = [
        page_hot(order_ref[p : p + 1, :], column_ref[p : p + 1, :], row_ref[p : p + 1, :])
        for p in range(pages)
    ]
    every = backwards(jnp.concatenate(hots, axis=0))
    reach_ref[...] = jnp.zeros_like(reach_ref)
    for pair in range(PAIRS):
        scores = [
            attention_back(p, pair, packed_ref, probs_ref, grad_ref, grad_packed_ref, width)
            for p in range(pages)
        ]
        for head in range(2):
            rows = slice(head * SLOT, (head + 1) * SLOT)
            along = jnp.concatenate([dot(s[rows], h) for s, h in zip(scores, hots)], axis=0)
            sums = dot(every, along.astype(bf16), TN)
            at = 2 * pair + head
            reach_ref[at : at + 1, :] = table_rows(sums)
    for i, value in enumerate((first_sum, gain_sum, branch_sum)):
        small_ref[i : i + 1, :] = value
    table_ref[...] = dot(
        bucket_places().astype(f32), reach_ref[...], NT, precision=lax.Precision.HIGHEST
    )


def last_kernel(
    attended_ref,
    low_ref,
    mixed_low_ref,
    grad_packed_ref,
    block_ref,
    after,
    *shares_out,
    outs,
    cuts,
    share,
):
    width = low_ref.shape[1]
    step = 3 * SLOT
    for r in range(0, width, step):
        rows = slice(r, r + step)
        value = dot(attended_ref[:, rows], low_ref[...], TN)
        store_shares(value, r, 0, shares_out, cuts, share)
        for c in range(0, 3 * width, width):
            value = dot(mixed_low_ref[:, rows], grad_packed_ref[:, c : c + width], TN)
            store_shares(value, r, width + c, shares_out, cuts, share)
        if cuts:
            store_shares(block_ref[rows], r, 4 * width, shares_out, cuts, share)


def input_kernel(
    mid_ref,
    grad_packed_ref,
    tokens_ref,
    small_down_ref,
    small_up_ref,
    small_chain_ref,
    table_ref,
    lengths_ref,
    order_ref,
    region_ref,
    taps_ref,
    input_ref,
    after,
    grad_in_ref,
    small_ref,
    block_ref,
    sum_ref,
    *,
    share,
):
    tokens, width = sum_ref.shape
    pages = tokens // SLOT
    conv_on = (lax.axis_index("section") == 0).astype(f32)
    taps = taps_ref[...].astype(f32) * conv_on
    for c in range(0, width, 2 * SLOT):
        cols = slice(c, c + 2 * SLOT)
        sum_ref[:, cols] = mid_ref[:, cols] + dot(grad_packed_ref[...], input_ref[cols, :], NT)
    tap_sums = [0.0] * TAPS
    mixed_sum = 0.0
    for p in range(pages):
        here = slice(p * SLOT, (p + 1) * SLOT)
        order = order_ref[p : p + 1, :]
        rank_hot = rank_hot_of(order)
        masks = tap_columns(order, region_ref[p : p + 1, :], lengths_ref[p])
        ordered = dot(rank_hot, tokens_ref[here], TN)
        grad_mixed = sum_ref[here]
        grad_order = place_rows(rank_hot, grad_mixed, TN)
        source = jnp.zeros_like(ordered)
        for j in range(TAPS):
            masked = grad_order * masks[:, j : j + 1]
            tap_sums[j] = tap_sums[j] + column_sum(masked * shifted(ordered, j - REACH))
            source = source + shifted(taps[j : j + 1] * masked, REACH - j)
        grad_in_ref[here] = grad_mixed + place_rows(rank_hot, source, NN)
        mixed_sum = mixed_sum + column_sum(grad_mixed)
    down, chain = small_down_ref[...], small_chain_ref[...]
    rows = [
        column_sum(grad_packed_ref[:, :width].astype(f32)),
        column_sum(grad_packed_ref[:, 2 * width :].astype(f32)),
        chain[2:3],
        chain[0:1],
        down[0:1],
        down[1:2],
        conv_on * mixed_sum,
        chain[1:2],
        down[2:3],
    ]
    for i, value in enumerate(rows + [conv_on * value for value in tap_sums]):
        small_ref[i : i + 1, :] = value
    if share:
        small_block(small_ref, small_up_ref, table_ref, block_ref, share)


SMALL_ROWS = 16


def small_block(small_ref, up_ref, table_ref, block_ref, share):
    width = small_ref.shape[1]
    shares = block_ref.shape[0] // share
    part = width // shares
    up_part = up_ref.shape[1] // shares
    buckets = (B1D + 2 * B2D) // shares
    block_ref[...] = jnp.zeros_like(block_ref)
    small, up = small_ref[...], jnp.broadcast_to(up_ref[...], (8, up_ref.shape[1]))
    for s in range(shares):
        top = s * share
        shift = (width - s * part) % width
        here = pltpu.roll(small, shift, 1) if shift else small
        block_ref[top : top + SMALL_ROWS, :] = here[:, :SLOT]
        shift = (up.shape[1] - s * up_part) % up.shape[1]
        here = pltpu.roll(up, shift, 1) if shift else up
        top += SMALL_ROWS
        block_ref[top : top + 1, :] = here[:1, :SLOT]
        block_ref[top + 1 : top + 2, :] = here[:1, SLOT : 2 * SLOT]
        top += 2
        block_ref[top : top + buckets, :] = table_ref[s * buckets : (s + 1) * buckets, :]


def place():
    index = lax.axis_index("dp")
    return index // 4, index // 2 % 2


def added(out_ref, out_at, parts, window=None):
    rows = out_ref.shape[-2]
    for r in range(0, rows, 16):
        strip = slice(r, r + 16)
        total = 0.0
        for ref, at, windowed in parts:
            if windowed:
                row, _, column, columns = window
                value = ref[at, row + r : row + r + 16, column : column + columns]
            else:
                value = ref[at, strip]
            total = total + value.astype(f32)
        if out_at is None:
            out_ref[strip] = total.astype(bf16)
        else:
            out_ref[out_at, strip] = total.astype(bf16)


def leave_kernel(mine_ref, recv_ref, after, out_ref, *, window):
    first = 4 * (1 - place()[1])
    for k in range(4):
        parts = ((mine_ref, first + k, True), (recv_ref, first + k, True))
        added(out_ref, k, parts, window)


def near_kernel(mine_ref, recv_ref, y_ref, after, leave_ref, keep_ref, *, window):
    z, y = place()
    for out_ref, parity in ((leave_ref, 1 - z % 2), (keep_ref, z % 2)):
        for k in range(2):
            block = 2 * k + parity
            at = 4 * y + block
            parts = ((mine_ref, at, True), (recv_ref, at, True), (y_ref, block, False))
            added(out_ref, k, parts, window)


def far_kernel(keep_ref, recv_ref, *rest):
    leave_ref, own_ref = rest[-2:]
    high = place()[0] // 2
    for out_ref, k in ((leave_ref, 1 - high), (own_ref, high)):
        added(out_ref, None, ((keep_ref, k, False), (recv_ref, k, False)))


def both(parts):
    return parts[0][...].astype(f32) + parts[1][...].astype(f32)


def down_end(*refs):
    out_ref = refs[-1]
    rows = refs[0].shape[0]
    out_ref[:rows] = both(refs[:2])
    out_ref[rows:] = both(refs[2:4])


def up_end(*refs):
    out_ref = refs[-1]
    columns = refs[0].shape[1]
    out_ref[:, :columns] = both(refs[:2])
    out_ref[:, columns:] = both(refs[2:4])


def last_end(*refs):
    left_width = refs[0].shape[1]
    input_ref, output_ref, bias_ref, gain_ref, tap_ref, up_ref, table_ref = refs[5:12]
    sum_ref, block_ref = refs[12:]
    sum_ref[:, :left_width] = both(refs[:2])
    sum_ref[:, left_width:] = both(refs[2:4])
    width, share = output_ref.shape[1], output_ref.shape[0]
    output_ref[...] = sum_ref[:, :width]
    input_ref[...] = sum_ref[:, width : 4 * width]
    block_ref[...] = sum_ref[:, 4 * width :]
    bias_ref[...] = block_ref[:7, :share]
    gain_ref[...] = block_ref[7:9, :share]
    tap_ref[...] = block_ref[9:16, :share]
    rest = up_ref.shape[1] - SLOT
    up_ref[:, :SLOT] = block_ref[SMALL_ROWS : SMALL_ROWS + 1, :]
    up_ref[:, SLOT:] = block_ref[SMALL_ROWS + 1 : SMALL_ROWS + 2, :rest]
    for i in range(table_ref.shape[1] // HEADS):
        at = SMALL_ROWS + 2 + i
        table_ref[:, i * HEADS : (i + 1) * HEADS] = block_ref[at : at + 1, :HEADS]


def kernel_call(body, name, ins, outs, scratch, flops=0, vmem=16):
    return pl.pallas_call(
        body,
        name=name,
        out_shape=[shape for shape, _ in outs],
        in_specs=[spec for _, spec in ins],
        out_specs=[spec for _, spec in outs],
        scratch_shapes=scratch,
        compiler_params=pltpu.CompilerParams(vmem_limit_bytes=vmem << 20),
        cost_estimate=pl.CostEstimate(flops=flops, bytes_accessed=0, transcendentals=0),
    )(*[value for value, _ in ins])


def near_by(value):
    return pltpu.with_memory_space_constraint(value, pltpu.VMEM)


def in_hbm(value):
    return pltpu.with_memory_space_constraint(value, pltpu.HBM)


def near_shape(dims, kind=bf16):
    return pltpu.VMEM(dims, kind)


class Summing:
    def __init__(self):
        self.pairs, self.windows, self.crossed, self.kept, self.ends = {}, {}, {}, {}, {}

    @staticmethod
    def _swap(value, bits):
        return near_by(lax.ppermute(value, "dp", [(i, i ^ bits) for i in range(16)]))

    @staticmethod
    def _add(body, name, ins, after, outs, cost=0):
        return kernel_call(
            body,
            name,
            [(near_by(value), IN_VMEM) for value in ins] + [(after, IN_PLACE)],
            [(near_shape(dims), IN_VMEM) for dims in outs],
            [],
            cost,
            4,
        )

    def core(self, theirs, mine, **windows):
        recv = self._swap(theirs, 1)
        for name, window in windows.items():
            self.pairs[name], self.windows[name] = [mine, recv], window

    def leave(self, name, after):
        window = self.windows[name]
        body = functools.partial(leave_kernel, window=window)
        dims = (4, window[1], window[3])
        (out,) = self._add(body, "leave", self.pairs[name], after, [dims])
        self.crossed[name] = self._swap(out, 2)
        return out

    def near(self, name, after):
        window = self.windows[name]
        body = functools.partial(near_kernel, window=window)
        dims = (2, window[1], window[3])
        ins = self.pairs[name] + [self.crossed[name]]
        out, keep = self._add(body, "near", ins, after, [dims, dims], COST)
        self.kept[name] = [keep, self._swap(out, 4)]
        return out

    def far(self, name, after, earlier=None):
        ins = self.kept[name]
        dims = ins[0].shape[1:]
        body = far_kernel
        if earlier:
            ins = ins + self.ends[earlier][1:]
        out, own = self._add(body, "far", ins, after, [dims, dims], COST)
        self.ends[name] = [own, self._swap(out, 8)]
        return out


def local(
    tokens,
    cotangent,
    page_lengths,
    cut_order,
    cut_region,
    cell_column,
    cell_row,
    input_proj,
    output_proj,
    up_proj,
    down_proj,
    up_bias,
    bias_rows,
    gain_rows,
    conv_taps,
    bias_table,
):
    section_count = lax.axis_size("section")
    dp_count = lax.axis_size("dp")
    by_hops = dp_count == 16
    pages, _, width = tokens.shape
    hidden = up_proj.shape[2]
    count = pages * SLOT
    weights = [w[0] for w in (input_proj, output_proj, up_proj, down_proj)]
    rows, gains, taps = bias_rows[0], gain_rows[0], conv_taps[0]
    tokens, cotangent = tokens.reshape(count, width), cotangent.reshape(count, width)

    def shape(dims, kind):
        return jax.ShapeDtypeStruct(dims, kind)

    def inside(*values):
        return [(v, IN_VMEM) for v in values]

    def in_place(*values):
        return [(v, IN_PLACE) for v in values]

    def scalars(*values):
        return [(v, IN_SMEM) for v in values]

    wide, low = shape((count, width), f32), shape((count, width), bf16)
    wide_scratch = pltpu.VMEM((count, width), f32)
    low_scratch = pltpu.VMEM((count, width), bf16)
    packed_scratch = pltpu.VMEM((count, 3 * width), bf16)
    hidden_scratch = pltpu.VMEM((count, hidden), bf16)
    bias_dims = (pages * HEADS * SLOT, SLOT)

    def sems(number):
        return pltpu.SemaphoreType.DMA((number,))

    first_ins = [tokens, cut_order, cut_region, cell_column, cell_row, rows, gains, up_bias]
    first_ins += [taps, bias_table]
    result, mixed, bias, *near_weights = kernel_call(
        first_kernel,
        "first",
        scalars(in_hbm(page_lengths)) + in_place(*map(in_hbm, first_ins + weights)),
        inside(low, near_shape((count, width), f32), near_shape(bias_dims, f32))
        + inside(*[near_shape(w.shape) for w in weights]),
        [
            packed_scratch,
            low_scratch,
            wide_scratch,
            wide_scratch,
            low_scratch,
            hidden_scratch,
            *[pltpu.VMEM(v.shape, v.dtype) for v in first_ins],
            sems(len(first_ins) + len(weights)),
        ],
    )
    input_w, output_w, up_w, down_w = near_weights = list(map(near_by, near_weights))
    arrived = near_by(
        lax.ppermute(result, "section", [(i, i + 1) for i in range(section_count - 1)])
    )
    shapes = kept_shapes(count, width, hidden)
    layer_out, leaving, *kept_list = kernel_call(
        second_kernel,
        "second",
        inside(arrived, cotangent)
        + scalars(page_lengths)
        + inside(rows, gains, up_bias)
        + inside(*map(near_by, (mixed, bias, *near_weights))),
        inside(low, near_shape((count, width)), *[near_shape(*s) for s in shapes]),
        [
            wide_scratch,
            wide_scratch,
            wide_scratch,
            low_scratch,
            hidden_scratch,
            low_scratch,
            packed_scratch,
        ],
    )
    kept = dict(zip([name for name, _, _ in KEPT], map(near_by, kept_list)))
    arrived_grad = near_by(
        lax.ppermute(leaving, "section", [(i + 1, i) for i in range(section_count - 1)])
    )
    part = width // dp_count

    def cut(dims, cuts):
        share = dims[0] // dp_count
        if not by_hops:
            outs, cuts = inside(shape(dims, bf16)), ()
        else:
            halves_out = [near_shape((dp_count // 2, c[1], c[3])) for c in cuts for _ in range(2)]
            outs = inside(*halves_out)
        return outs, dict(outs=len(outs), cuts=cuts, share=share)

    half = hidden // dp_count // 2
    down_outs, down_cut = cut(
        (hidden, width), ((0, half, 0, width), (half, half, 0, width))
    )
    *down_parts, grad_sum, small_down = kernel_call(
        functools.partial(down_kernel, **down_cut),
        "down",
        inside(cotangent, arrived_grad, gains)
        + inside(kept["second_norm"], kept["second_scale"], kept["act"]),
        down_outs + inside(wide, shape((8, width), f32)),
        [low_scratch],
    )
    summing = Summing()
    after = grad_sum
    if by_hops:
        piece = (0, half, 0, width)
        summing.core(*down_parts[:2], d1=piece)
        summing.core(*down_parts[2:], d2=piece)
        after = summing.leave("d1", after)
    half = hidden // 2
    up_outs, up_cut = cut(
        (width, hidden), ((0, part, 0, hidden),)
    )
    *up_parts, gate, small_up = kernel_call(
        functools.partial(up_kernel, **up_cut),
        "up",
        inside(grad_sum, kept["slope"], kept["first_low"], down_w) + in_place(after),
        up_outs + inside(shape((count, hidden), bf16), shape((1, hidden), f32)),
        [low_scratch],
    )
    after = gate
    if by_hops:
        summing.core(*up_parts, u1=(0, part, 0, half), u2=(0, part, half, half))
        after = summing.leave("d2", after)
    grad_mid, grad_branch, grad_packed, small_chain, table = kernel_call(
        chain_kernel,
        "chain",
        inside(grad_sum, gate, kept["first_norm"], kept["first_scale"], kept["packed"])
        + inside(kept["probs"], cut_order, cell_column, cell_row, gains)
        + inside(up_w, output_w)
        + in_place(after),
        inside(wide, low, shape((count, 3 * width), bf16), shape((8, width), f32))
        + inside(shape((B1D + 2 * B2D, SLOT), f32)),
        [wide_scratch, low_scratch, pltpu.VMEM((SLOT, 4 * SLOT), f32)],
    )
    after = grad_mid
    if by_hops:
        after = summing.near("d1", after)
        after = summing.leave("u1", after)
    grad_in, small_rows, block = kernel_call(
        functools.partial(input_kernel, share=part if by_hops else 0),
        "input",
        inside(grad_mid, grad_packed, tokens, small_down, small_up, small_chain, table)
        + scalars(page_lengths)
        + inside(cut_order, cut_region, taps, input_w)
        + in_place(after),
        inside(wide, shape((16, width), f32), near_shape((width, SLOT), f32)),
        [wide_scratch],
    )
    after = grad_in
    if by_hops:
        after = summing.near("d2", after)
        after = summing.far("d1", after)
    columns = 4 * width + (SLOT if by_hops else 0)
    last_outs, last_cut = cut((width, columns), ((0, part, 0, columns),))
    last_parts = kernel_call(
        functools.partial(last_kernel, **last_cut),
        "last",
        inside(kept["attended"], grad_branch, kept["mixed_low"], grad_packed, near_by(block))
        + in_place(after),
        last_outs,
        [],
    )
    after = last_parts[0]
    if by_hops:
        left = LEFT_COLUMNS
        summing.core(
            *last_parts, a1=(0, part, 0, left), a2=(0, part, left, columns - left)
        )
        ends = summing.ends
        after = summing.leave("u2", after)
        after = summing.near("u1", after)
        after = summing.far("d2", after, "d1")
        after = summing.leave("a1", after)
        after = summing.near("u2", after)
        after = summing.far("u1", after)
        (after,) = (down_grad,) = kernel_call(
            down_end,
            "down_end",
            inside(*map(near_by, ends["d1"] + ends["d2"])) + in_place(after),
            inside(shape((hidden // dp_count, width), f32)),
            [],
            vmem=4,
        )
        after = summing.leave("a2", after)
        after = summing.near("a1", after)
        after = summing.far("u2", after, "u1")
        after = summing.near("a2", after)
        after = summing.far("a1", after)
        (after,) = (up_grad,) = kernel_call(
            up_end,
            "up_end",
            inside(*map(near_by, ends["u1"] + ends["u2"])) + in_place(after),
            inside(shape((part, hidden), f32)),
            [],
            vmem=4,
        )
        after = summing.far("a2", after)
        input_grad, output_grad, bias_grad, gain_grad, tap_grad, up_bias_grad, table_grad = (
            kernel_call(
                last_end,
                "last_end",
                inside(*map(near_by, ends["a1"] + ends["a2"])) + in_place(after),
                inside(
                    shape((part, 3 * width), f32),
                    shape((part, width), f32),
                    shape((7, part), f32),
                    shape((2, part), f32),
                    shape((TAPS, part), f32),
                    shape((1, hidden // dp_count), f32),
                    shape((1, table.shape[0] * HEADS // dp_count), f32),
                ),
                [pltpu.VMEM((part, columns), f32), pltpu.VMEM((part, SLOT), f32)],
                vmem=4,
            )
        )
    else:

        def scattered(value):
            return lax.psum_scatter(value, "dp", scatter_dimension=0, tiled=True).astype(f32)

        down_grad, up_grad, last_grad = (
            scattered(parts[0]) for parts in (down_parts, up_parts, last_parts)
        )
        input_grad, output_grad = last_grad[:, width:], last_grad[:, :width]
        small = [
            small_rows.reshape(16, dp_count, part).transpose(1, 0, 2).reshape(dp_count, -1),
            small_up.reshape(dp_count, -1),
            table[:, :HEADS].reshape(dp_count, -1),
        ]
        small = jnp.concatenate(small, axis=1)
        used = small.shape[1]
        small = jnp.pad(small, ((0, 0), (0, -used % SLOT))).reshape(-1, SLOT)
        small = scattered(small).reshape(-1)
        vectors = small[: 16 * part].reshape(16, part)
        bias_grad, gain_grad, tap_grad = vectors[:7], vectors[7:9], vectors[9:]
        at = 16 * part + hidden // dp_count
        up_bias_grad, table_grad = small[None, 16 * part : at], small[None, at:used]
    return (
        layer_out.reshape(1, pages, SLOT, width),
        grad_in.reshape(1, pages, SLOT, width),
        input_grad[None],
        output_grad[None],
        up_grad[None],
        down_grad[None],
        up_bias_grad,
        bias_grad[None],
        gain_grad[None],
        tap_grad[None],
        table_grad,
    )


def solution(mesh):
    by_section = [P("section", None, None)] * 4
    placed = (
        P("dp", None, None),
        P("dp", None, None),
        P("dp"),
        P("dp", None),
        P("dp", None),
        P("dp", None),
        P("dp", None),
        *by_section,
        P("section", None),
        P("section", None, None),
        P("section", None, None),
        P("section", None, None),
        P("section", None),
    )
    return jax.shard_map(
        local,
        mesh=mesh,
        in_specs=placed,
        out_specs=(
            P("section", "dp", None, None),
            P("section", "dp", None, None),
            P("section", "dp", None),
            P("section", "dp", None),
            P("section", "dp", None),
            P("section", "dp", None),
            P("section", "dp"),
            P("section", None, "dp"),
            P("section", None, "dp"),
            P("section", None, "dp"),
            P("section", "dp"),
        ),
        check_vma=False,
    )
```

```python
import functools

import jax
import jax.numpy as jnp
from jax import lax
from jax.experimental import pallas as pl
from jax.experimental.pallas import tpu as pltpu
from jax.sharding import PartitionSpec as P

HEADS = 12
HEAD = 64
B1D = 32
B2D = 64
SLOT = 128
PAIRS = HEADS // 2
TAPS = 7
REACH = 3
EPSILON = 1e-05
COST = 20_000_000_000
MASKED = -1000000000.0
STRIP = 64

f32 = jnp.float32
bf16 = jnp.bfloat16
NN = ((1,), (0,))
NT = ((1,), (1,))
TN = ((0,), (0,))

IN_VMEM = pl.BlockSpec(memory_space=pltpu.VMEM)
IN_SMEM = pl.BlockSpec(memory_space=pltpu.SMEM)
IN_PLACE = pl.BlockSpec(memory_space=pl.ANY)


def dot(left, right, dims=NN, precision=None):
    return lax.dot_general(
        left, right, (dims, ((), ())), precision=precision, preferred_element_type=f32
    )


def iota(shape, axis):
    return lax.broadcasted_iota(jnp.int32, shape, axis)


def hot(mask):
    return mask.astype(f32).astype(bf16)


def identity():
    return hot(iota((SLOT, SLOT), 0) == iota((SLOT, SLOT), 1))


def rank_hot_of(order):
    return hot(order == iota((SLOT, SLOT), 0))


def page_hot(order, column, row):
    cells = iota((SLOT, SLOT), 0)
    wanted = jnp.where(cells < B2D, column, row + B2D)
    cell_hot = dot(identity(), hot(wanted == cells), NT).astype(bf16)
    return jnp.concatenate([rank_hot_of(order), cell_hot], axis=1)


def tap_columns(order, region, length):
    shape = (8, SLOT)
    order, region = jnp.broadcast_to(order, shape), jnp.broadcast_to(region, shape)
    live = (order < length).astype(jnp.int32)
    lane, tap = iota(shape, 1), iota(shape, 0)
    masks = jnp.zeros(shape, f32)
    for j in range(TAPS):
        offset = j - REACH
        shift = (-offset) % SLOT
        region_j = pltpu.roll(region, shift, 1) if shift else region
        live_j = pltpu.roll(live, shift, 1) if shift else live
        joined = (lane + offset >= 0) & (lane + offset < SLOT) & (region_j == region) & (live_j > 0)
        masks = jnp.where((tap == j) & joined, 1.0, masks)
    return dot(identity(), masks.astype(bf16), NT)


def shifted(rows, offset):
    shift = (-offset) % SLOT
    return pltpu.roll(rows, shift, 0) if shift else rows


def place_rows(rank_hot, rows, dims):
    high = rows.astype(bf16)
    low = (rows - high.astype(f32)).astype(bf16)
    return dot(rank_hot, high, dims) + dot(rank_hot, low, dims)


def bucket_places():
    shape = (B1D + 2 * B2D, 4 * SLOT)
    bucket, lane = iota(shape, 0), iota(shape, 1)
    near = jnp.clip(lane - (SLOT - 1) + B1D // 2, 0, B1D - 1)
    column = B1D + jnp.clip(lane - 2 * SLOT - (B2D - 1) + B2D // 2, 0, B2D - 1)
    row = B1D + B2D + jnp.clip(lane - 3 * SLOT - (B2D - 1) + B2D // 2, 0, B2D - 1)
    wanted = jnp.where(lane < 2 * SLOT, near, jnp.where(lane < 3 * SLOT, column, row))
    return bucket == wanted


def halves(pair):
    lane = iota((1, SLOT), 1)
    first = hot(lane < HEAD)
    second = hot(lane >= HEAD)
    return jnp.concatenate([pair * first, pair * second], axis=0)


def side_by_side(stacked):
    return jnp.concatenate([stacked[:SLOT], stacked[SLOT:]], axis=1)


def normed_of(value):
    average = jnp.mean(value, axis=-1, keepdims=True)
    centered = value - average
    spread = jnp.mean(centered * centered, axis=-1, keepdims=True)
    inverse = lax.rsqrt(spread + EPSILON)
    return centered * inverse, inverse


def norm_back(grad, normed, inverse):
    first_mean = jnp.mean(grad, axis=-1, keepdims=True)
    second_mean = jnp.mean(grad * normed, axis=-1, keepdims=True)
    return inverse * (grad - first_mean - normed * second_mean)


def table_columns(table):
    buckets = table.shape[1] // HEADS
    bucket = iota((buckets, table.shape[1]), 0) * HEADS
    lane = iota((buckets, table.shape[1]), 1)
    own = hot((lane >= bucket) & (lane < bucket + HEADS))
    lane = iota((16, table.shape[1]), 1)
    times = ((lane.astype(f32) + 0.5) * (1.0 / HEADS)).astype(jnp.int32)
    head = hot(lane - HEADS * times == iota((16, table.shape[1]), 0))
    return dot(own * table, head, NT).astype(bf16)


def bias_body(order_ref, column_ref, row_ref, table_ref, bias_ref):
    pages = order_ref.shape[0]
    hots = [
        page_hot(order_ref[p : p + 1, :], column_ref[p : p + 1, :], row_ref[p : p + 1, :])
        for p in range(pages)
    ]
    every = jnp.concatenate(hots, axis=0)
    reach = dot(table_columns(table_ref[...]), hot(bucket_places()), TN)
    lane = iota((B2D, SLOT), 1)
    for h in range(HEADS):
        row = reach[h : h + 1, :]
        near = jnp.broadcast_to(row[:, : 2 * SLOT], (SLOT, 2 * SLOT))
        near = pltpu.roll(near, SLOT + 1, 1, stride=1, stride_axis=0)[:, :SLOT]
        across = jnp.broadcast_to(row[:, 2 * SLOT : 3 * SLOT], (B2D, SLOT))
        across = pltpu.roll(across, B2D + 1, 1, stride=1, stride_axis=0)
        down = jnp.broadcast_to(row[:, 3 * SLOT :], (B2D, SLOT))
        down = pltpu.roll(down, 1, 1, stride=1, stride_axis=0)
        cells = jnp.concatenate(
            [jnp.where(lane < B2D, across, 0.0), jnp.where(lane >= B2D, down, 0.0)], axis=0
        )
        blank = jnp.zeros((SLOT, SLOT), bf16)
        grid = jnp.concatenate(
            [
                jnp.concatenate([near.astype(bf16), blank], axis=1),
                jnp.concatenate([blank, cells.astype(bf16)], axis=1),
            ],
            axis=0,
        )
        rows = dot(every, grid).astype(bf16)
        for p in range(pages):
            at = (p * HEADS + h) * SLOT
            bias_ref[at : at + SLOT, :] = dot(rows[p * SLOT : (p + 1) * SLOT], hots[p], NT)


def forward_body(weights, waits, lengths_ref, vectors, bias_ref, work, keep):
    input_ref, output_ref, up_ref, down_ref = weights
    rows_ref, gains_ref, up_bias_ref = vectors
    mixed_ref, packed_ref, attended_ref, sum_ref, first_ref, low_ref, act_ref, result_ref = work
    rows, gains = rows_ref[...].astype(f32), gains_ref[...].astype(f32)
    tokens, width = mixed_ref.shape
    hidden = act_ref.shape[1]
    low_ref[...] = mixed_ref[...].astype(bf16)
    if keep:
        keep["mixed_low"][...] = low_ref[...]
    waits[0]()
    for part, add in ((0, rows[0:1]), (1, None), (2, rows[1:2])):
        cols = slice(part * width, (part + 1) * width)
        value = dot(low_ref[...], input_ref[:, cols])
        packed_ref[:, cols] = (value if add is None else value + add).astype(bf16)
    for p in range(tokens // SLOT):
        live = iota((2 * SLOT, SLOT), 1) < lengths_ref[p]
        here = slice(p * SLOT, (p + 1) * SLOT)
        for pair in range(PAIRS):
            at = pair * SLOT
            queries = halves(packed_ref[here, at : at + SLOT]) * (HEAD**-0.5)
            keys = packed_ref[here, width + at : width + at + SLOT]
            values = packed_ref[here, 2 * width + at : 2 * width + at + SLOT]
            top = (p * HEADS + 2 * pair) * SLOT
            scores = dot(queries, keys, NT) + bias_ref[top : top + 2 * SLOT, :]
            scores = jnp.where(live, scores, MASKED)
            expo = jnp.exp(scores - jnp.max(scores, axis=-1, keepdims=True))
            probs = (expo * (1.0 / jnp.sum(expo, axis=-1, keepdims=True))).astype(bf16)
            if keep:
                keep["probs"][top : top + 2 * SLOT, :] = probs
            attended_ref[here, at : at + SLOT] = dot(side_by_side(probs), halves(values)).astype(
                bf16
            )
    waits[1]()
    sum_ref[...] = dot(attended_ref[...], output_ref[...])
    for r in range(0, tokens, STRIP):
        strip = slice(r, r + STRIP)
        normed, inverse = normed_of(mixed_ref[strip] + sum_ref[strip] + rows[2:3])
        first = normed * gains[0:1] + rows[3:4]
        first_ref[strip] = first
        low_ref[strip] = first.astype(bf16)
        if keep:
            keep["first_norm"][strip] = normed
            keep["first_scale"][strip] = jnp.broadcast_to(inverse, (STRIP, SLOT))
            keep["first_low"][strip] = first.astype(bf16)
    waits[2]()
    for c in range(0, hidden, 2 * SLOT):
        cols = slice(c, c + 2 * SLOT)
        gate = dot(low_ref[...], up_ref[:, cols]) + up_bias_ref[:, cols].astype(f32)
        below = 0.5 + 0.5 * lax.erf(gate * 0.7071067811865476)
        act_ref[:, cols] = (gate * below).astype(bf16)
        if keep:
            density = jnp.exp(-0.5 * gate * gate) * 0.3989422804014327
            keep["slope"][:, cols] = (below + gate * density).astype(bf16)
    waits[3]()
    sum_ref[...] = dot(act_ref[...], down_ref[...])
    for r in range(0, tokens, STRIP):
        strip = slice(r, r + STRIP)
        normed, inverse = normed_of(first_ref[strip] + sum_ref[strip] + rows[4:5])
        result_ref[strip] = (normed * gains[1:2] + rows[5:6]).astype(bf16)
        if keep:
            keep["second_norm"][strip] = normed
            keep["second_scale"][strip] = jnp.broadcast_to(inverse, (STRIP, SLOT))


def attention_back(p, pair, packed_ref, probs_ref, grad_ref, grad_packed_ref, width):
    here = slice(p * SLOT, (p + 1) * SLOT)
    at = pair * SLOT
    top = (p * HEADS + 2 * pair) * SLOT
    queries = halves(packed_ref[here, at : at + SLOT]) * (HEAD**-0.5)
    keys = halves(packed_ref[here, width + at : width + at + SLOT]) * (HEAD**-0.5)
    values = packed_ref[here, 2 * width + at : 2 * width + at + SLOT]
    grad = halves(grad_ref[here, at : at + SLOT])
    probs_low = probs_ref[top : top + 2 * SLOT, :]
    probs = probs_low.astype(f32)
    grad_probs = dot(grad, values, NT)
    inner = jnp.sum(probs * grad_probs, axis=-1, keepdims=True)
    grad_scores = (probs * (grad_probs - inner)).astype(bf16)
    for part, value in (
        (0, dot(side_by_side(grad_scores), keys)),
        (1, dot(grad_scores, queries, TN)),
        (2, dot(probs_low, grad, TN)),
    ):
        cols = slice(part * width + at, part * width + at + SLOT)
        grad_packed_ref[here, cols] = value.astype(bf16)
    return grad_scores


def first_kernel(lengths_ref, *rest):
    ins, weight_ins, rest = rest[:10], rest[10:14], rest[14:]
    result_ref, mixed_ref, bias_ref, *weights = rest[:7]
    packed_ref, attended_ref, sum_ref, first_ref, low_ref, act_ref = rest[7:13]
    held, sems = rest[13:23], rest[23]
    small = [pltpu.make_async_copy(a, b, sems.at[i]) for i, (a, b) in enumerate(zip(ins, held))]
    copies = [
        pltpu.make_async_copy(a, b, sems.at[len(small) + i])
        for i, (a, b) in enumerate(zip(weight_ins, weights))
    ]
    for copy in small:
        copy.start()
    copies[0].start()
    for copy in small:
        copy.wait()
    tokens_ref, order_ref, region_ref, column_ref, row_ref = held[:5]
    rows_ref, gains_ref, up_bias_ref, taps_ref, table_ref = held[5:]
    conv_on = (lax.axis_index("section") == 0).astype(f32)
    taps = taps_ref[...].astype(f32) * conv_on
    conv_bias = rows_ref[...].astype(f32)[6:7] * conv_on
    for p in range(order_ref.shape[0]):
        here = slice(p * SLOT, (p + 1) * SLOT)
        order = order_ref[p : p + 1, :]
        rank_hot = rank_hot_of(order)
        masks = tap_columns(order, region_ref[p : p + 1, :], lengths_ref[p])
        ordered = dot(rank_hot, tokens_ref[here], TN)
        total = jnp.zeros_like(ordered)
        for j in range(TAPS):
            total = total + taps[j : j + 1] * shifted(ordered, j - REACH) * masks[:, j : j + 1]
        mixed_ref[here] = (
            tokens_ref[here].astype(f32) + place_rows(rank_hot, total, NN) + conv_bias
        )
    copies[1].start()
    copies[2].start()
    bias_body(order_ref, column_ref, row_ref, table_ref, bias_ref)

    def wait_input():
        copies[0].wait()
        copies[3].start()

    forward_body(
        weights,
        [wait_input] + [copy.wait for copy in copies[1:]],
        lengths_ref,
        (rows_ref, gains_ref, up_bias_ref),
        bias_ref,
        (
            mixed_ref,
            packed_ref,
            attended_ref,
            sum_ref,
            first_ref,
            low_ref,
            act_ref,
            result_ref,
        ),
        None,
    )


KEPT = (
    ("mixed_low", 1, 0),
    ("packed", 3, 0),
    ("probs", 0, 0),
    ("attended", 1, 0),
    ("first_norm", 1, 1),
    ("first_scale", -1, 1),
    ("first_low", 1, 0),
    ("slope", 4, 0),
    ("act", 4, 0),
    ("second_norm", 1, 1),
    ("second_scale", -1, 1),
)


def kept_shapes(tokens, width, hidden):
    shapes = []
    for name, parts, wide in KEPT:
        dims = (tokens, hidden if parts == 4 else SLOT if parts < 0 else parts * width)
        if name == "probs":
            dims = (tokens * HEADS, SLOT)
        shapes.append((dims, f32 if wide else bf16))
    return shapes


def second_kernel(
    arrived_ref,
    cotangent_ref,
    lengths_ref,
    rows_ref,
    gains_ref,
    up_bias_ref,
    mixed_in_ref,
    bias_ref,
    input_ref,
    output_ref,
    up_ref,
    down_ref,
    result_ref,
    grad_in_ref,
    *rest,
):
    kept_list, rest = rest[: len(KEPT)], rest[len(KEPT) :]
    mixed_ref, sum_ref, first_ref, low_ref, gate_ref, grad_ref, grad_packed_ref = rest
    tokens, width = mixed_ref.shape
    keep = dict(zip([name for name, _, _ in KEPT], kept_list))
    first_section = lax.axis_index("section") == 0
    mixed_ref[...] = jnp.where(first_section, mixed_in_ref[...], arrived_ref[...].astype(f32))
    forward_body(
        (input_ref, output_ref, up_ref, down_ref),
        [lambda: None] * 4,
        lengths_ref,
        (rows_ref, gains_ref, up_bias_ref),
        bias_ref,
        (
            mixed_ref,
            keep["packed"],
            keep["attended"],
            sum_ref,
            first_ref,
            low_ref,
            keep["act"],
            result_ref,
        ),
        keep,
    )
    gains = gains_ref[...].astype(f32)
    for r in range(0, tokens, STRIP):
        strip = slice(r, r + STRIP)
        grad = cotangent_ref[strip].astype(f32) * gains[1:2]
        grad_sum = norm_back(grad, keep["second_norm"][strip], keep["second_scale"][strip, :1])
        first_ref[strip] = grad_sum
        low_ref[strip] = grad_sum.astype(bf16)
    gate_body(low_ref, down_ref, keep["slope"], gate_ref)
    for c in range(0, width, 2 * SLOT):
        cols = slice(c, c + 2 * SLOT)
        sum_ref[:, cols] = first_ref[:, cols] + dot(gate_ref[...], up_ref[cols, :], NT)
    for r in range(0, tokens, STRIP):
        strip = slice(r, r + STRIP)
        grad = sum_ref[strip] * gains[0:1]
        grad_mid = norm_back(grad, keep["first_norm"][strip], keep["first_scale"][strip, :1])
        first_ref[strip] = grad_mid
        low_ref[strip] = grad_mid.astype(bf16)
    grad_ref[...] = dot(low_ref[...], output_ref[...], NT).astype(bf16)
    for p in range(tokens // SLOT):
        for pair in range(PAIRS):
            attention_back(
                p, pair, keep["packed"], keep["probs"], grad_ref, grad_packed_ref, width
            )
    for c in range(0, width, 2 * SLOT):
        cols = slice(c, c + 2 * SLOT)
        grad_in = first_ref[:, cols] + dot(grad_packed_ref[...], input_ref[cols, :], NT)
        grad_in_ref[:, cols] = grad_in.astype(bf16)


def gate_body(grad_ref, down_ref, slope_ref, gate_ref):
    for c in range(0, gate_ref.shape[1], 2 * SLOT):
        cols = slice(c, c + 2 * SLOT)
        value = dot(grad_ref[...], down_ref[cols, :], NT) * slope_ref[:, cols].astype(f32)
        gate_ref[:, cols] = value.astype(bf16)


def store_shares(value, row, column, outs, cuts, share):
    rows, columns = value.shape
    value = value.astype(bf16)
    if not cuts:
        outs[0][row : row + rows, column : column + columns] = value
        return
    even = lax.axis_index("dp") % 2 == 0
    for pair in range(row // (2 * share), (row + rows) // (2 * share)):
        top = 2 * pair * share - row
        for i, (start, count, left, width) in enumerate(cuts):
            from_column, to_column = max(column, left), min(column + columns, left + width)
            if from_column >= to_column:
                continue
            cols = slice(from_column - column, to_column - column)
            first = value[top + start : top + start + count, cols]
            second = value[top + share + start : top + share + start + count, cols]
            cols = slice(from_column - left, to_column - left)
            at = pair % 2 * 4 + pair // 2
            outs[2 * i][at, :, cols] = jnp.where(even, second, first)
            outs[2 * i + 1][at, :, cols] = jnp.where(even, first, second)


def column_sum(value):
    return jnp.sum(value, axis=0, keepdims=True)


def feed_kernel(
    cotangent_ref,
    arrived_ref,
    gains_ref,
    normed_ref,
    scale_ref,
    act_ref,
    slope_ref,
    first_low_ref,
    down_ref,
    *rest,
    down_cut,
    up_cut,
):
    down_out, rest = rest[: down_cut["outs"]], rest[down_cut["outs"] :]
    up_out, rest = rest[: up_cut["outs"]], rest[up_cut["outs"] :]
    grad_sum_ref, gate_ref, small_ref, small_up_ref, low_ref = rest
    tokens, width = low_ref.shape
    hidden = act_ref.shape[1]
    gains = gains_ref[...].astype(f32)
    last = lax.axis_index("section") == lax.axis_size("section") - 1
    sums = [0.0, 0.0, 0.0]
    for r in range(0, tokens, STRIP):
        strip = slice(r, r + STRIP)
        grad_out = jnp.where(
            last, cotangent_ref[strip].astype(f32), arrived_ref[strip].astype(f32)
        )
        normed = normed_ref[strip]
        grad_sum = norm_back(grad_out * gains[1:2], normed, scale_ref[strip, :1])
        low = grad_sum.astype(bf16)
        grad_sum_ref[strip] = grad_sum
        low_ref[strip] = low
        sums[0] = sums[0] + column_sum(low.astype(f32))
        sums[1] = sums[1] + column_sum(grad_out)
        sums[2] = sums[2] + column_sum(grad_out * normed)
    step = 3 * SLOT
    for r in range(0, hidden, step):
        value = dot(act_ref[:, r : r + step], low_ref[...], TN)
        store_shares(value, r, 0, down_out, down_cut["cuts"], down_cut["share"])
    for i, value in enumerate(sums):
        small_ref[i : i + 1, :] = value
    gate_body(low_ref, down_ref, slope_ref, gate_ref)
    for r in range(0, width, step):
        left = first_low_ref[:, r : r + step]
        for c in range(0, hidden, width):
            value = dot(left, gate_ref[:, c : c + width], TN)
            store_shares(value, r, c, up_out, up_cut["cuts"], up_cut["share"])
    for c in range(0, hidden, width):
        cols = slice(c, c + width)
        small_up_ref[:, cols] = column_sum(gate_ref[:, cols].astype(f32))


def backwards(every):
    shape = (2 * SLOT, 2 * SLOT)
    left, right = iota(shape, 0), iota(shape, 1)
    ends = jnp.where(left < SLOT, SLOT - 1, jnp.where(left < SLOT + B2D, 3 * SLOT - B2D - 1, 0))
    ends = jnp.where(left >= SLOT + B2D, 4 * SLOT - B2D - 1, ends)
    return dot(every, hot(left + right == ends)).astype(bf16)


def table_rows(sums):
    blank = jnp.zeros((SLOT, SLOT), f32)
    near = jnp.concatenate([sums[:SLOT, :SLOT], blank], axis=1)
    near = pltpu.roll(near, 0, 1, stride=1, stride_axis=0)
    lane = iota((B2D, SLOT), 1)
    across = jnp.where(lane < B2D, sums[SLOT : SLOT + B2D, SLOT:], 0.0)
    across = pltpu.roll(across, 0, 1, stride=1, stride_axis=0)
    down = jnp.where(lane >= B2D, sums[SLOT + B2D :, SLOT:], 0.0)
    down = pltpu.roll(down, B2D, 1, stride=1, stride_axis=0)
    return jnp.concatenate([column_sum(near), column_sum(across), column_sum(down)], axis=1)


def chain_kernel(
    grad_sum_ref,
    gate_ref,
    normed_ref,
    scale_ref,
    packed_ref,
    probs_ref,
    order_ref,
    column_ref,
    row_ref,
    gains_ref,
    up_ref,
    output_ref,
    after,
    mid_ref,
    low_ref,
    grad_packed_ref,
    small_ref,
    table_ref,
    sum_ref,
    grad_ref,
    reach_ref,
):
    tokens, width = sum_ref.shape
    pages = tokens // SLOT
    gains = gains_ref[...].astype(f32)
    for c in range(0, width, 2 * SLOT):
        cols = slice(c, c + 2 * SLOT)
        sum_ref[:, cols] = grad_sum_ref[:, cols] + dot(gate_ref[...], up_ref[cols, :], NT)
    first_sum = gain_sum = branch_sum = 0.0
    for r in range(0, tokens, STRIP):
        strip = slice(r, r + STRIP)
        grad_first, normed = sum_ref[strip], normed_ref[strip]
        grad_mid = norm_back(grad_first * gains[0:1], normed, scale_ref[strip, :1])
        low = grad_mid.astype(bf16)
        mid_ref[strip] = grad_mid
        low_ref[strip] = low
        first_sum = first_sum + column_sum(grad_first)
        gain_sum = gain_sum + column_sum(grad_first * normed)
        branch_sum = branch_sum + column_sum(low.astype(f32))
    grad_ref[...] = dot(low_ref[...], output_ref[...], NT).astype(bf16)
    hots = [
        page_hot(order_ref[p : p + 1, :], column_ref[p : p + 1, :], row_ref[p : p + 1, :])
        for p in range(pages)
    ]
    every = backwards(jnp.concatenate(hots, axis=0))
    reach_ref[...] = jnp.zeros_like(reach_ref)
    for pair in range(PAIRS):
        scores = [
            attention_back(p, pair, packed_ref, probs_ref, grad_ref, grad_packed_ref, width)
            for p in range(pages)
        ]
        for head in range(2):
            rows = slice(head * SLOT, (head + 1) * SLOT)
            along = jnp.concatenate([dot(s[rows], h) for s, h in zip(scores, hots)], axis=0)
            sums = dot(every, along.astype(bf16), TN)
            at = 2 * pair + head
            reach_ref[at : at + 1, :] = table_rows(sums)
    for i, value in enumerate((first_sum, gain_sum, branch_sum)):
        small_ref[i : i + 1, :] = value
    table_ref[...] = dot(
        bucket_places().astype(f32), reach_ref[...], NT, precision=lax.Precision.HIGHEST
    )


def last_kernel(
    attended_ref,
    low_ref,
    mixed_low_ref,
    grad_packed_ref,
    block_ref,
    after,
    *shares_out,
    outs,
    cuts,
    share,
):
    width = low_ref.shape[1]
    step = 3 * SLOT
    for r in range(0, width, step):
        rows = slice(r, r + step)
        value = dot(attended_ref[:, rows], low_ref[...], TN)
        store_shares(value, r, 0, shares_out, cuts, share)
        for c in range(0, 3 * width, width):
            value = dot(mixed_low_ref[:, rows], grad_packed_ref[:, c : c + width], TN)
            store_shares(value, r, width + c, shares_out, cuts, share)
        if cuts:
            store_shares(block_ref[rows], r, 4 * width, shares_out, cuts, share)


def input_kernel(
    mid_ref,
    grad_packed_ref,
    tokens_ref,
    small_down_ref,
    small_up_ref,
    small_chain_ref,
    table_ref,
    lengths_ref,
    order_ref,
    region_ref,
    taps_ref,
    input_ref,
    after,
    grad_in_ref,
    small_ref,
    block_ref,
    sum_ref,
    *,
    share,
):
    tokens, width = sum_ref.shape
    pages = tokens // SLOT
    conv_on = (lax.axis_index("section") == 0).astype(f32)
    taps = taps_ref[...].astype(f32) * conv_on
    for c in range(0, width, 2 * SLOT):
        cols = slice(c, c + 2 * SLOT)
        sum_ref[:, cols] = mid_ref[:, cols] + dot(grad_packed_ref[...], input_ref[cols, :], NT)
    tap_sums = [0.0] * TAPS
    mixed_sum = 0.0
    for p in range(pages):
        here = slice(p * SLOT, (p + 1) * SLOT)
        order = order_ref[p : p + 1, :]
        rank_hot = rank_hot_of(order)
        masks = tap_columns(order, region_ref[p : p + 1, :], lengths_ref[p])
        ordered = dot(rank_hot, tokens_ref[here], TN)
        grad_mixed = sum_ref[here]
        grad_order = place_rows(rank_hot, grad_mixed, TN)
        source = jnp.zeros_like(ordered)
        for j in range(TAPS):
            masked = grad_order * masks[:, j : j + 1]
            tap_sums[j] = tap_sums[j] + column_sum(masked * shifted(ordered, j - REACH))
            source = source + shifted(taps[j : j + 1] * masked, REACH - j)
        grad_in_ref[here] = grad_mixed + place_rows(rank_hot, source, NN)
        mixed_sum = mixed_sum + column_sum(grad_mixed)
    down, chain = small_down_ref[...], small_chain_ref[...]
    rows = [
        column_sum(grad_packed_ref[:, :width].astype(f32)),
        column_sum(grad_packed_ref[:, 2 * width :].astype(f32)),
        chain[2:3],
        chain[0:1],
        down[0:1],
        down[1:2],
        conv_on * mixed_sum,
        chain[1:2],
        down[2:3],
    ]
    for i, value in enumerate(rows + [conv_on * value for value in tap_sums]):
        small_ref[i : i + 1, :] = value
    if share:
        small_block(small_ref, small_up_ref, table_ref, block_ref, share)


SMALL_ROWS = 16


def small_block(small_ref, up_ref, table_ref, block_ref, share):
    width = small_ref.shape[1]
    shares = block_ref.shape[0] // share
    part = width // shares
    up_part = up_ref.shape[1] // shares
    buckets = (B1D + 2 * B2D) // shares
    block_ref[...] = jnp.zeros_like(block_ref)
    small, up = small_ref[...], jnp.broadcast_to(up_ref[...], (8, up_ref.shape[1]))
    for s in range(shares):
        top = s * share
        shift = (width - s * part) % width
        here = pltpu.roll(small, shift, 1) if shift else small
        block_ref[top : top + SMALL_ROWS, :] = here[:, :SLOT]
        shift = (up.shape[1] - s * up_part) % up.shape[1]
        here = pltpu.roll(up, shift, 1) if shift else up
        top += SMALL_ROWS
        block_ref[top : top + 1, :] = here[:1, :SLOT]
        block_ref[top + 1 : top + 2, :] = here[:1, SLOT : 2 * SLOT]
        top += 2
        block_ref[top : top + buckets, :] = table_ref[s * buckets : (s + 1) * buckets, :]


def place():
    index = lax.axis_index("dp")
    return index // 4, index // 2 % 2


def added(out_ref, out_at, parts, window=None):
    rows = out_ref.shape[-2]
    for r in range(0, rows, 16):
        strip = slice(r, r + 16)
        total = 0.0
        for ref, at, windowed in parts:
            if windowed:
                row, _, column, columns = window
                value = ref[at, row + r : row + r + 16, column : column + columns]
            else:
                value = ref[at, strip]
            total = total + value.astype(f32)
        if out_at is None:
            out_ref[strip] = total.astype(bf16)
        else:
            out_ref[out_at, strip] = total.astype(bf16)


def fetched(recv_hbm, first, window, scratch, sems):
    row, rows, column, columns = window
    copies = []
    for k in range(4):
        source = recv_hbm.at[first + k, pl.ds(row, rows), pl.ds(column, columns)]
        copies.append(pltpu.make_async_copy(source, scratch.at[k], sems.at[k]))
        copies[-1].start()
    return copies


def leave_kernel(mine_ref, recv_ref, *rest, window, fetch):
    first = 4 * (1 - place()[1])
    if fetch:
        out_ref, scratch, sems = rest[-3:]
        copies = fetched(recv_ref, first, window, scratch, sems)
    else:
        out_ref = rest[-1]
    for k in range(4):
        other = (recv_ref, first + k, True)
        if fetch:
            copies[k].wait()
            other = (scratch, k, False)
        added(out_ref, k, ((mine_ref, first + k, True), other), window)


def near_kernel(mine_ref, recv_ref, y_ref, after, leave_ref, keep_ref, *rest, window, fetch):
    z, y = place()
    if fetch:
        scratch, sems = rest
        for copy in fetched(recv_ref, 4 * y, window, scratch, sems):
            copy.wait()
    for out_ref, parity in ((leave_ref, 1 - z % 2), (keep_ref, z % 2)):
        for k in range(2):
            block = 2 * k + parity
            at = 4 * y + block
            other = (scratch, block, False) if fetch else (recv_ref, at, True)
            added(out_ref, k, ((mine_ref, at, True), other, (y_ref, block, False)), window)


def far_kernel(keep_ref, recv_ref, *rest):
    leave_ref, own_ref = rest[-2:]
    high = place()[0] // 2
    for out_ref, k in ((leave_ref, 1 - high), (own_ref, high)):
        added(out_ref, None, ((keep_ref, k, False), (recv_ref, k, False)))


def near_first_kernel(mine_ref, recv_ref, after, leave_ref, keep_ref):
    z, _ = place()
    for out_ref, parity in ((leave_ref, 1 - z % 2), (keep_ref, z % 2)):
        for k in range(4):
            at = 2 * k + parity
            added(out_ref, k, ((mine_ref, at, False), (recv_ref, at, False)))


def far_first_kernel(keep_ref, recv_ref, after, leave_ref, stay_ref):
    high = place()[0] // 2
    for out_ref, k in ((leave_ref, 1 - high), (stay_ref, high)):
        for y in range(2):
            at = 2 * y + k
            added(out_ref, y, ((keep_ref, at, False), (recv_ref, at, False)))


def cross_kernel(keep_ref, recv_ref, after, leave_ref, own_ref):
    y = place()[1]
    for out_ref, at in ((leave_ref, 1 - y), (own_ref, y)):
        added(out_ref, None, ((keep_ref, at, False), (recv_ref, at, False)))


def both(parts):
    return parts[0][...].astype(f32) + parts[1][...].astype(f32)


def down_end(*refs):
    out_ref, token_ref = refs[-2:]
    token_ref[...] = jnp.zeros_like(token_ref)
    rows = refs[0].shape[0]
    out_ref[:rows] = both(refs[:2])
    out_ref[rows:] = both(refs[2:4])


def up_end(*refs):
    out_ref, token_ref = refs[-2:]
    token_ref[...] = jnp.zeros_like(token_ref)
    columns = refs[0].shape[1]
    out_ref[:, :columns] = both(refs[:2])
    out_ref[:, columns:] = both(refs[2:4])


def last_end(*refs):
    sum_ref, block_ref = refs[-2:]
    input_ref, output_ref, bias_ref, gain_ref, tap_ref, up_ref, table_ref = refs[-9:-2]
    column = 0
    for i in range(0, len(refs) - 10, 2):
        columns = refs[i].shape[1]
        sum_ref[:, column : column + columns] = both(refs[i : i + 2])
        column += columns
    width, share = output_ref.shape[1], output_ref.shape[0]
    output_ref[...] = sum_ref[:, :width]
    input_ref[...] = sum_ref[:, width : 4 * width]
    block_ref[...] = sum_ref[:, 4 * width :]
    bias_ref[...] = block_ref[:7, :share]
    gain_ref[...] = block_ref[7:9, :share]
    tap_ref[...] = block_ref[9:16, :share]
    rest = up_ref.shape[1] - SLOT
    up_ref[:, :SLOT] = block_ref[SMALL_ROWS : SMALL_ROWS + 1, :]
    up_ref[:, SLOT:] = block_ref[SMALL_ROWS + 1 : SMALL_ROWS + 2, :rest]
    for i in range(table_ref.shape[1] // HEADS):
        at = SMALL_ROWS + 2 + i
        table_ref[:, i * HEADS : (i + 1) * HEADS] = block_ref[at : at + 1, :HEADS]


def kernel_call(body, name, ins, outs, scratch, flops=0, vmem=10):
    return pl.pallas_call(
        body,
        name=name,
        out_shape=[shape for shape, _ in outs],
        in_specs=[spec for _, spec in ins],
        out_specs=[spec for _, spec in outs],
        scratch_shapes=scratch,
        compiler_params=pltpu.CompilerParams(vmem_limit_bytes=vmem << 20),
        cost_estimate=pl.CostEstimate(flops=flops, bytes_accessed=0, transcendentals=0),
    )(*[value for value, _ in ins])


def near_by(value):
    return pltpu.with_memory_space_constraint(value, pltpu.VMEM)


def in_hbm(value):
    return pltpu.with_memory_space_constraint(value, pltpu.HBM)


def near_shape(dims, kind=bf16):
    return pltpu.VMEM(dims, kind)


class Summing:
    def __init__(self):
        self.pairs, self.windows, self.crossed, self.kept, self.ends = {}, {}, {}, {}, {}
        self.fetch = {}

    @staticmethod
    def _swap(value, bits):
        return near_by(lax.ppermute(value, "dp", [(i, i ^ bits) for i in range(16)]))

    @staticmethod
    def _add(body, name, ins, after, outs, cost=0, earlier=(), scratch=(), fetch=False):
        specs = [IN_VMEM] * len(ins)
        if fetch:
            specs[1] = IN_PLACE
        return kernel_call(
            body,
            name,
            [(near_by(value), spec) for value, spec in zip(ins, specs)]
            + [(value, IN_PLACE) for value in (after, *earlier)],
            [(near_shape(dims), IN_VMEM) for dims in outs],
            list(scratch),
            cost,
            4,
        )

    def core(self, theirs, mine, fetch=False, **windows):
        recv = self._swap(theirs, 1)
        for name, window in windows.items():
            self.pairs[name], self.windows[name] = [mine, recv], window
            self.fetch[name] = fetch

    def _fetching(self, name, body):
        window, fetch = self.windows[name], self.fetch[name]
        dims = (4, window[1], window[3])
        scratch = [pltpu.VMEM(dims, bf16), pltpu.SemaphoreType.DMA((4,))] if fetch else []
        body = functools.partial(body, window=window, fetch=fetch)
        return body, dict(scratch=scratch, fetch=fetch), dims

    def leave(self, name, after, earlier=None):
        body, more, dims = self._fetching(name, leave_kernel)
        earlier = [self.crossed[earlier]] if earlier else []
        (out,) = self._add(body, "leave", self.pairs[name], after, [dims], 0, earlier, **more)
        self.crossed[name] = self._swap(out, 2)
        return out

    def near(self, name, after):
        body, more, dims = self._fetching(name, near_kernel)
        dims = (2,) + dims[1:]
        ins = self.pairs[name] + [self.crossed[name]]
        out, keep = self._add(body, "near", ins, after, [dims, dims], COST, **more)
        self.kept[name] = [keep, self._swap(out, 4)]
        return out

    def far(self, name, after, earlier=()):
        ins = self.kept[name]
        dims = ins[0].shape[1:]
        earlier = [self.ends[other][1] for other in earlier]
        out, own = self._add(far_kernel, "far", ins, after, [dims, dims], COST, earlier)
        self.ends[name] = [own, self._swap(out, 8)]
        return out

    def near_first(self, name, after):
        ins = self.pairs[name]
        dims = (4,) + ins[0].shape[1:]
        out, keep = self._add(near_first_kernel, "near_first", ins, after, [dims, dims], COST)
        self.kept[name] = [keep, self._swap(out, 4)]
        return out

    def far_first(self, name, after):
        ins = self.kept[name]
        dims = (2,) + ins[0].shape[1:]
        out, stay = self._add(far_first_kernel, "far_first", ins, after, [dims, dims], COST)
        self.kept[name] = [stay, self._swap(out, 8)]
        return out

    def cross(self, name, after):
        ins = self.kept[name]
        dims = ins[0].shape[1:]
        out, own = self._add(cross_kernel, "cross", ins, after, [dims, dims], COST)
        self.ends[name] = [own, self._swap(out, 2)]
        return out


def local(
    tokens,
    cotangent,
    page_lengths,
    cut_order,
    cut_region,
    cell_column,
    cell_row,
    input_proj,
    output_proj,
    up_proj,
    down_proj,
    up_bias,
    bias_rows,
    gain_rows,
    conv_taps,
    bias_table,
):
    section_count = lax.axis_size("section")
    dp_count = lax.axis_size("dp")
    by_hops = dp_count == 16
    pages, _, width = tokens.shape
    hidden = up_proj.shape[2]
    count = pages * SLOT
    weights = [w[0] for w in (input_proj, output_proj, up_proj, down_proj)]
    rows, gains, taps = bias_rows[0], gain_rows[0], conv_taps[0]
    tokens, cotangent = tokens.reshape(count, width), cotangent.reshape(count, width)

    def shape(dims, kind):
        return jax.ShapeDtypeStruct(dims, kind)

    def inside(*values):
        return [(v, IN_VMEM) for v in values]

    def in_place(*values):
        return [(v, IN_PLACE) for v in values]

    def scalars(*values):
        return [(v, IN_SMEM) for v in values]

    wide, low = shape((count, width), f32), shape((count, width), bf16)
    wide_scratch = pltpu.VMEM((count, width), f32)
    low_scratch = pltpu.VMEM((count, width), bf16)
    packed_scratch = pltpu.VMEM((count, 3 * width), bf16)
    hidden_scratch = pltpu.VMEM((count, hidden), bf16)
    bias_dims = (pages * HEADS * SLOT, SLOT)

    def sems(number):
        return pltpu.SemaphoreType.DMA((number,))

    first_ins = [tokens, cut_order, cut_region, cell_column, cell_row, rows, gains, up_bias]
    first_ins += [taps, bias_table]
    result, mixed, bias, *near_weights = kernel_call(
        first_kernel,
        "first",
        scalars(in_hbm(page_lengths)) + in_place(*map(in_hbm, first_ins + weights)),
        inside(low, near_shape((count, width), f32), near_shape(bias_dims, f32))
        + inside(*[near_shape(w.shape) for w in weights]),
        [
            packed_scratch,
            low_scratch,
            wide_scratch,
            wide_scratch,
            low_scratch,
            hidden_scratch,
            *[pltpu.VMEM(v.shape, v.dtype) for v in first_ins],
            sems(len(first_ins) + len(weights)),
        ],
    )
    input_w, output_w, up_w, down_w = near_weights = list(map(near_by, near_weights))
    arrived = near_by(
        lax.ppermute(result, "section", [(i, i + 1) for i in range(section_count - 1)])
    )
    shapes = kept_shapes(count, width, hidden)
    layer_out, leaving, *kept_list = kernel_call(
        second_kernel,
        "second",
        inside(arrived, cotangent)
        + scalars(page_lengths)
        + inside(rows, gains, up_bias)
        + inside(*map(near_by, (mixed, bias, *near_weights))),
        inside(low, near_shape((count, width)), *[near_shape(*s) for s in shapes]),
        [
            wide_scratch,
            wide_scratch,
            wide_scratch,
            low_scratch,
            hidden_scratch,
            low_scratch,
            packed_scratch,
        ],
    )
    kept = dict(zip([name for name, _, _ in KEPT], map(near_by, kept_list)))
    arrived_grad = near_by(
        lax.ppermute(leaving, "section", [(i + 1, i) for i in range(section_count - 1)])
    )
    part = width // dp_count

    def cut(dims, cuts):
        share = dims[0] // dp_count
        if not by_hops:
            outs, cuts = inside(shape(dims, bf16)), ()
        else:
            halves_out = [near_shape((dp_count // 2, c[1], c[3])) for c in cuts for _ in range(2)]
            outs = inside(*halves_out)
        return outs, dict(outs=len(outs), cuts=cuts, share=share)

    half = hidden // dp_count // 2
    down_outs, down_cut = cut((hidden, width), ((0, half, 0, width), (half, half, 0, width)))
    up_outs, up_cut = cut((width, hidden), ((0, part, 0, hidden),))
    feed = kernel_call(
        functools.partial(feed_kernel, down_cut=down_cut, up_cut=up_cut),
        "feed",
        inside(cotangent, arrived_grad, gains)
        + inside(kept["second_norm"], kept["second_scale"], kept["act"])
        + inside(kept["slope"], kept["first_low"], down_w),
        down_outs
        + up_outs
        + inside(wide, shape((count, hidden), bf16))
        + inside(shape((8, width), f32), shape((1, hidden), f32)),
        [low_scratch],
    )
    down_parts, feed = feed[: len(down_outs)], feed[len(down_outs) :]
    up_parts, feed = feed[: len(up_outs)], feed[len(up_outs) :]
    grad_sum, gate, small_down, small_up = feed
    summing = Summing()
    after = grad_sum
    if by_hops:
        piece = (0, half, 0, width)
        side = hidden // 2
        summing.core(*down_parts[:2], d1=piece)
        summing.core(*down_parts[2:], d2=piece)
        summing.core(*up_parts, u1=(0, part, 0, side), u2=(0, part, side, side))
        after = summing.leave("d1", after)
        after = summing.near_first("d2", after)
        after = summing.leave("u1", after)
    grad_mid, grad_branch, grad_packed, small_chain, table = kernel_call(
        chain_kernel,
        "chain",
        inside(grad_sum, gate, kept["first_norm"], kept["first_scale"], kept["packed"])
        + inside(kept["probs"], cut_order, cell_column, cell_row, gains)
        + inside(up_w, output_w)
        + in_place(after),
        inside(wide, low, shape((count, 3 * width), bf16), shape((8, width), f32))
        + inside(shape((B1D + 2 * B2D, SLOT), f32)),
        [wide_scratch, low_scratch, pltpu.VMEM((SLOT, 4 * SLOT), f32)],
    )
    after = grad_mid
    if by_hops:
        after = summing.near("d1", after)
        after = summing.leave("u2", after)
    grad_in, small_rows, block = kernel_call(
        functools.partial(input_kernel, share=part if by_hops else 0),
        "input",
        inside(grad_mid, grad_packed, tokens, small_down, small_up, small_chain, table)
        + scalars(page_lengths)
        + inside(cut_order, cut_region, taps, input_w)
        + in_place(after),
        inside(wide, shape((16, width), f32), near_shape((width, SLOT), f32)),
        [wide_scratch],
    )
    after = block
    columns = 4 * width + (SLOT if by_hops else 0)
    last_outs, last_cut = cut((width, columns), ((0, part, 0, columns),))
    last_parts = kernel_call(
        functools.partial(last_kernel, **last_cut),
        "last",
        inside(kept["attended"], grad_branch, kept["mixed_low"], grad_packed, near_by(block))
        + in_place(after),
        last_outs,
        [],
    )
    after = last_parts[0]
    if by_hops:
        token = near_shape((8, SLOT), f32)
        windows, column = {}, 0
        for name, end in (("a1", 2 * width), ("a2", 3 * width + 2 * SLOT), ("a3", columns)):
            windows[name], column = (0, part, column, end - column), end
        summing.core(*last_parts, fetch=True, **windows)
        ends = summing.ends
        after = summing.far_first("d2", after)
        after = summing.near("u1", after)
        after = summing.far("d1", after)
        after = summing.leave("a1", after, "u2")
        after = summing.near("u2", after)
        after = summing.cross("d2", after)
        after = summing.far("u1", after, ["d1"])
        after = summing.leave("a2", after)
        after = summing.near("a1", after)
        after = summing.far("u2", after)
        down_grad, after = kernel_call(
            down_end,
            "down_end",
            inside(*map(near_by, ends["d1"] + ends["d2"])) + in_place(after),
            inside(shape((hidden // dp_count, width), f32), token),
            [],
            vmem=4,
        )
        after = summing.leave("a3", after)
        after = summing.near("a2", after)
        after = summing.far("a1", after, ["u1"])
        up_grad, after = kernel_call(
            up_end,
            "up_end",
            inside(*map(near_by, ends["u1"] + ends["u2"])) + in_place(after),
            inside(shape((part, hidden), f32), token),
            [],
            vmem=4,
        )
        after = summing.near("a3", after)
        after = summing.far("a2", after)
        after = summing.far("a3", after)
        input_grad, output_grad, bias_grad, gain_grad, tap_grad, up_bias_grad, table_grad = (
            kernel_call(
                last_end,
                "last_end",
                inside(*map(near_by, ends["a1"] + ends["a2"] + ends["a3"])) + in_place(after),
                inside(
                    shape((part, 3 * width), f32),
                    shape((part, width), f32),
                    shape((7, part), f32),
                    shape((2, part), f32),
                    shape((TAPS, part), f32),
                    shape((1, hidden // dp_count), f32),
                    shape((1, table.shape[0] * HEADS // dp_count), f32),
                ),
                [pltpu.VMEM((part, columns), f32), pltpu.VMEM((part, SLOT), f32)],
                vmem=4,
            )
        )
    else:

        def scattered(value):
            return lax.psum_scatter(value, "dp", scatter_dimension=0, tiled=True).astype(f32)

        down_grad, up_grad, last_grad = (
            scattered(parts[0]) for parts in (down_parts, up_parts, last_parts)
        )
        input_grad, output_grad = last_grad[:, width:], last_grad[:, :width]
        small = [
            small_rows.reshape(16, dp_count, part).transpose(1, 0, 2).reshape(dp_count, -1),
            small_up.reshape(dp_count, -1),
            table[:, :HEADS].reshape(dp_count, -1),
        ]
        small = jnp.concatenate(small, axis=1)
        used = small.shape[1]
        small = jnp.pad(small, ((0, 0), (0, -used % SLOT))).reshape(-1, SLOT)
        small = scattered(small).reshape(-1)
        vectors = small[: 16 * part].reshape(16, part)
        bias_grad, gain_grad, tap_grad = vectors[:7], vectors[7:9], vectors[9:]
        at = 16 * part + hidden // dp_count
        up_bias_grad, table_grad = small[None, 16 * part : at], small[None, at:used]
    return (
        layer_out.reshape(1, pages, SLOT, width),
        grad_in.reshape(1, pages, SLOT, width),
        input_grad[None],
        output_grad[None],
        up_grad[None],
        down_grad[None],
        up_bias_grad,
        bias_grad[None],
        gain_grad[None],
        tap_grad[None],
        table_grad,
    )


def solution(mesh):
    by_section = [P("section", None, None)] * 4
    placed = (
        P("dp", None, None),
        P("dp", None, None),
        P("dp"),
        P("dp", None),
        P("dp", None),
        P("dp", None),
        P("dp", None),
        *by_section,
        P("section", None),
        P("section", None, None),
        P("section", None, None),
        P("section", None, None),
        P("section", None),
    )
    return jax.shard_map(
        local,
        mesh=mesh,
        in_specs=placed,
        out_specs=(
            P("section", "dp", None, None),
            P("section", "dp", None, None),
            P("section", "dp", None),
            P("section", "dp", None),
            P("section", "dp", None),
            P("section", "dp", None),
            P("section", "dp"),
            P("section", None, "dp"),
            P("section", None, "dp"),
            P("section", None, "dp"),
            P("section", "dp"),
        ),
        check_vma=False,
    )
```

```python
import functools

import jax
import jax.numpy as jnp
from jax import lax
from jax.experimental import pallas as pl
from jax.experimental.pallas import tpu as pltpu
from jax.sharding import PartitionSpec as P

HEADS = 12
HEAD = 64
B1D = 32
B2D = 64
SLOT = 128
PAIRS = HEADS // 2
TAPS = 7
REACH = 3
EPSILON = 1e-05
COST = 20_000_000_000
MASKED = -1000000000.0
STRIP = 64

f32 = jnp.float32
bf16 = jnp.bfloat16
NN = ((1,), (0,))
NT = ((1,), (1,))
TN = ((0,), (0,))

IN_VMEM = pl.BlockSpec(memory_space=pltpu.VMEM)
IN_SMEM = pl.BlockSpec(memory_space=pltpu.SMEM)
IN_PLACE = pl.BlockSpec(memory_space=pl.ANY)


def dot(left, right, dims=NN, precision=None):
    return lax.dot_general(
        left, right, (dims, ((), ())), precision=precision, preferred_element_type=f32
    )


def iota(shape, axis):
    return lax.broadcasted_iota(jnp.int32, shape, axis)


def hot(mask):
    return mask.astype(f32).astype(bf16)


def identity():
    return hot(iota((SLOT, SLOT), 0) == iota((SLOT, SLOT), 1))


def rank_hot_of(order):
    return hot(order == iota((SLOT, SLOT), 0))


def page_hot(order, column, row):
    cells = iota((SLOT, SLOT), 0)
    wanted = jnp.where(cells < B2D, column, row + B2D)
    cell_hot = dot(identity(), hot(wanted == cells), NT).astype(bf16)
    return jnp.concatenate([rank_hot_of(order), cell_hot], axis=1)


def tap_columns(order, region, length):
    shape = (8, SLOT)
    order, region = jnp.broadcast_to(order, shape), jnp.broadcast_to(region, shape)
    live = (order < length).astype(jnp.int32)
    lane, tap = iota(shape, 1), iota(shape, 0)
    masks = jnp.zeros(shape, f32)
    for j in range(TAPS):
        offset = j - REACH
        shift = (-offset) % SLOT
        region_j = pltpu.roll(region, shift, 1) if shift else region
        live_j = pltpu.roll(live, shift, 1) if shift else live
        joined = (lane + offset >= 0) & (lane + offset < SLOT) & (region_j == region) & (live_j > 0)
        masks = jnp.where((tap == j) & joined, 1.0, masks)
    return dot(identity(), masks.astype(bf16), NT)


def shifted(rows, offset):
    shift = (-offset) % SLOT
    return pltpu.roll(rows, shift, 0) if shift else rows


def place_rows(rank_hot, rows, dims):
    high = rows.astype(bf16)
    low = (rows - high.astype(f32)).astype(bf16)
    return dot(rank_hot, high, dims) + dot(rank_hot, low, dims)


def bucket_places():
    shape = (B1D + 2 * B2D, 4 * SLOT)
    bucket, lane = iota(shape, 0), iota(shape, 1)
    near = jnp.clip(lane - (SLOT - 1) + B1D // 2, 0, B1D - 1)
    column = B1D + jnp.clip(lane - 2 * SLOT - (B2D - 1) + B2D // 2, 0, B2D - 1)
    row = B1D + B2D + jnp.clip(lane - 3 * SLOT - (B2D - 1) + B2D // 2, 0, B2D - 1)
    wanted = jnp.where(lane < 2 * SLOT, near, jnp.where(lane < 3 * SLOT, column, row))
    return bucket == wanted


def halves(pair):
    lane = iota((1, SLOT), 1)
    first = hot(lane < HEAD)
    second = hot(lane >= HEAD)
    return jnp.concatenate([pair * first, pair * second], axis=0)


def side_by_side(stacked):
    return jnp.concatenate([stacked[:SLOT], stacked[SLOT:]], axis=1)


def normed_of(value):
    average = jnp.mean(value, axis=-1, keepdims=True)
    centered = value - average
    spread = jnp.mean(centered * centered, axis=-1, keepdims=True)
    inverse = lax.rsqrt(spread + EPSILON)
    return centered * inverse, inverse


def norm_back(grad, normed, inverse):
    first_mean = jnp.mean(grad, axis=-1, keepdims=True)
    second_mean = jnp.mean(grad * normed, axis=-1, keepdims=True)
    return inverse * (grad - first_mean - normed * second_mean)


def table_columns(table):
    buckets = table.shape[1] // HEADS
    bucket = iota((buckets, table.shape[1]), 0) * HEADS
    lane = iota((buckets, table.shape[1]), 1)
    own = hot((lane >= bucket) & (lane < bucket + HEADS))
    lane = iota((16, table.shape[1]), 1)
    times = ((lane.astype(f32) + 0.5) * (1.0 / HEADS)).astype(jnp.int32)
    head = hot(lane - HEADS * times == iota((16, table.shape[1]), 0))
    return dot(own * table, head, NT).astype(bf16)


def bias_body(order_ref, column_ref, row_ref, table_ref, bias_ref):
    pages = order_ref.shape[0]
    hots = [
        page_hot(order_ref[p : p + 1, :], column_ref[p : p + 1, :], row_ref[p : p + 1, :])
        for p in range(pages)
    ]
    every = jnp.concatenate(hots, axis=0)
    reach = dot(table_columns(table_ref[...]), hot(bucket_places()), TN)
    lane = iota((B2D, SLOT), 1)
    for h in range(HEADS):
        row = reach[h : h + 1, :]
        near = jnp.broadcast_to(row[:, : 2 * SLOT], (SLOT, 2 * SLOT))
        near = pltpu.roll(near, SLOT + 1, 1, stride=1, stride_axis=0)[:, :SLOT]
        across = jnp.broadcast_to(row[:, 2 * SLOT : 3 * SLOT], (B2D, SLOT))
        across = pltpu.roll(across, B2D + 1, 1, stride=1, stride_axis=0)
        down = jnp.broadcast_to(row[:, 3 * SLOT :], (B2D, SLOT))
        down = pltpu.roll(down, 1, 1, stride=1, stride_axis=0)
        cells = jnp.concatenate(
            [jnp.where(lane < B2D, across, 0.0), jnp.where(lane >= B2D, down, 0.0)], axis=0
        )
        blank = jnp.zeros((SLOT, SLOT), bf16)
        grid = jnp.concatenate(
            [
                jnp.concatenate([near.astype(bf16), blank], axis=1),
                jnp.concatenate([blank, cells.astype(bf16)], axis=1),
            ],
            axis=0,
        )
        rows = dot(every, grid).astype(bf16)
        for p in range(pages):
            at = (p * HEADS + h) * SLOT
            bias_ref[at : at + SLOT, :] = dot(rows[p * SLOT : (p + 1) * SLOT], hots[p], NT)


def forward_body(weights, waits, lengths_ref, vectors, bias_ref, work, keep):
    input_ref, output_ref, up_ref, down_ref = weights
    rows_ref, gains_ref, up_bias_ref = vectors
    mixed_ref, packed_ref, attended_ref, sum_ref, first_ref, low_ref, act_ref, result_ref = work
    rows, gains = rows_ref[...].astype(f32), gains_ref[...].astype(f32)
    tokens, width = mixed_ref.shape
    hidden = act_ref.shape[1]
    low_ref[...] = mixed_ref[...].astype(bf16)
    if keep:
        keep["mixed_low"][...] = low_ref[...]
    waits[0]()
    for part, add in ((0, rows[0:1]), (1, None), (2, rows[1:2])):
        cols = slice(part * width, (part + 1) * width)
        value = dot(low_ref[...], input_ref[:, cols])
        packed_ref[:, cols] = (value if add is None else value + add).astype(bf16)
    for p in range(tokens // SLOT):
        live = iota((2 * SLOT, SLOT), 1) < lengths_ref[p]
        here = slice(p * SLOT, (p + 1) * SLOT)
        for pair in range(PAIRS):
            at = pair * SLOT
            queries = halves(packed_ref[here, at : at + SLOT]) * (HEAD**-0.5)
            keys = packed_ref[here, width + at : width + at + SLOT]
            values = packed_ref[here, 2 * width + at : 2 * width + at + SLOT]
            top = (p * HEADS + 2 * pair) * SLOT
            scores = dot(queries, keys, NT) + bias_ref[top : top + 2 * SLOT, :]
            scores = jnp.where(live, scores, MASKED)
            expo = jnp.exp(scores - jnp.max(scores, axis=-1, keepdims=True))
            probs = (expo * (1.0 / jnp.sum(expo, axis=-1, keepdims=True))).astype(bf16)
            if keep:
                keep["probs"][top : top + 2 * SLOT, :] = probs
            attended_ref[here, at : at + SLOT] = dot(side_by_side(probs), halves(values)).astype(
                bf16
            )
    waits[1]()
    sum_ref[...] = dot(attended_ref[...], output_ref[...])
    for r in range(0, tokens, STRIP):
        strip = slice(r, r + STRIP)
        normed, inverse = normed_of(mixed_ref[strip] + sum_ref[strip] + rows[2:3])
        first = normed * gains[0:1] + rows[3:4]
        first_ref[strip] = first
        low_ref[strip] = first.astype(bf16)
        if keep:
            keep["first_norm"][strip] = normed
            keep["first_scale"][strip] = jnp.broadcast_to(inverse, (STRIP, SLOT))
            keep["first_low"][strip] = first.astype(bf16)
    waits[2]()
    for c in range(0, hidden, 2 * SLOT):
        cols = slice(c, c + 2 * SLOT)
        gate = dot(low_ref[...], up_ref[:, cols]) + up_bias_ref[:, cols].astype(f32)
        below = 0.5 + 0.5 * lax.erf(gate * 0.7071067811865476)
        act_ref[:, cols] = (gate * below).astype(bf16)
        if keep:
            density = jnp.exp(-0.5 * gate * gate) * 0.3989422804014327
            keep["slope"][:, cols] = (below + gate * density).astype(bf16)
    waits[3]()
    sum_ref[...] = dot(act_ref[...], down_ref[...])
    for r in range(0, tokens, STRIP):
        strip = slice(r, r + STRIP)
        normed, inverse = normed_of(first_ref[strip] + sum_ref[strip] + rows[4:5])
        result_ref[strip] = (normed * gains[1:2] + rows[5:6]).astype(bf16)
        if keep:
            keep["second_norm"][strip] = normed
            keep["second_scale"][strip] = jnp.broadcast_to(inverse, (STRIP, SLOT))


def attention_back(p, pair, packed_ref, probs_ref, grad_ref, grad_packed_ref, width):
    here = slice(p * SLOT, (p + 1) * SLOT)
    at = pair * SLOT
    top = (p * HEADS + 2 * pair) * SLOT
    queries = halves(packed_ref[here, at : at + SLOT]) * (HEAD**-0.5)
    keys = halves(packed_ref[here, width + at : width + at + SLOT]) * (HEAD**-0.5)
    values = packed_ref[here, 2 * width + at : 2 * width + at + SLOT]
    grad = halves(grad_ref[here, at : at + SLOT])
    probs_low = probs_ref[top : top + 2 * SLOT, :]
    probs = probs_low.astype(f32)
    grad_probs = dot(grad, values, NT)
    inner = jnp.sum(probs * grad_probs, axis=-1, keepdims=True)
    grad_scores = (probs * (grad_probs - inner)).astype(bf16)
    for part, value in (
        (0, dot(side_by_side(grad_scores), keys)),
        (1, dot(grad_scores, queries, TN)),
        (2, dot(probs_low, grad, TN)),
    ):
        cols = slice(part * width + at, part * width + at + SLOT)
        grad_packed_ref[here, cols] = value.astype(bf16)
    return grad_scores


def first_kernel(lengths_ref, *rest):
    ins, weight_ins, rest = rest[:10], rest[10:14], rest[14:]
    result_ref, mixed_ref, bias_ref, *weights = rest[:7]
    packed_ref, attended_ref, sum_ref, first_ref, low_ref, act_ref = rest[7:13]
    held, sems = rest[13:23], rest[23]
    small = [pltpu.make_async_copy(a, b, sems.at[i]) for i, (a, b) in enumerate(zip(ins, held))]
    copies = [
        pltpu.make_async_copy(a, b, sems.at[len(small) + i])
        for i, (a, b) in enumerate(zip(weight_ins, weights))
    ]
    for copy in small:
        copy.start()
    copies[0].start()
    for copy in small:
        copy.wait()
    tokens_ref, order_ref, region_ref, column_ref, row_ref = held[:5]
    rows_ref, gains_ref, up_bias_ref, taps_ref, table_ref = held[5:]
    conv_on = (lax.axis_index("section") == 0).astype(f32)
    taps = taps_ref[...].astype(f32) * conv_on
    conv_bias = rows_ref[...].astype(f32)[6:7] * conv_on
    for p in range(order_ref.shape[0]):
        here = slice(p * SLOT, (p + 1) * SLOT)
        order = order_ref[p : p + 1, :]
        rank_hot = rank_hot_of(order)
        masks = tap_columns(order, region_ref[p : p + 1, :], lengths_ref[p])
        ordered = dot(rank_hot, tokens_ref[here], TN)
        total = jnp.zeros_like(ordered)
        for j in range(TAPS):
            total = total + taps[j : j + 1] * shifted(ordered, j - REACH) * masks[:, j : j + 1]
        mixed_ref[here] = (
            tokens_ref[here].astype(f32) + place_rows(rank_hot, total, NN) + conv_bias
        )
    copies[1].start()
    copies[2].start()
    bias_body(order_ref, column_ref, row_ref, table_ref, bias_ref)

    def wait_input():
        copies[0].wait()
        copies[3].start()

    forward_body(
        weights,
        [wait_input] + [copy.wait for copy in copies[1:]],
        lengths_ref,
        (rows_ref, gains_ref, up_bias_ref),
        bias_ref,
        (
            mixed_ref,
            packed_ref,
            attended_ref,
            sum_ref,
            first_ref,
            low_ref,
            act_ref,
            result_ref,
        ),
        None,
    )


KEPT = (
    ("mixed_low", 1, 0),
    ("packed", 3, 0),
    ("probs", 0, 0),
    ("attended", 1, 0),
    ("first_norm", 1, 1),
    ("first_scale", -1, 1),
    ("first_low", 1, 0),
    ("slope", 4, 0),
    ("act", 4, 0),
    ("second_norm", 1, 1),
    ("second_scale", -1, 1),
)


def kept_shapes(tokens, width, hidden):
    shapes = []
    for name, parts, wide in KEPT:
        dims = (tokens, hidden if parts == 4 else SLOT if parts < 0 else parts * width)
        if name == "probs":
            dims = (tokens * HEADS, SLOT)
        shapes.append((dims, f32 if wide else bf16))
    return shapes


def second_kernel(
    arrived_ref,
    cotangent_ref,
    lengths_ref,
    rows_ref,
    gains_ref,
    up_bias_ref,
    mixed_in_ref,
    bias_ref,
    input_ref,
    output_ref,
    up_ref,
    down_ref,
    result_ref,
    grad_in_ref,
    *rest,
):
    kept_list, rest = rest[: len(KEPT)], rest[len(KEPT) :]
    mixed_ref, sum_ref, first_ref, low_ref, gate_ref, grad_ref, grad_packed_ref = rest
    tokens, width = mixed_ref.shape
    keep = dict(zip([name for name, _, _ in KEPT], kept_list))
    first_section = lax.axis_index("section") == 0
    mixed_ref[...] = jnp.where(first_section, mixed_in_ref[...], arrived_ref[...].astype(f32))
    forward_body(
        (input_ref, output_ref, up_ref, down_ref),
        [lambda: None] * 4,
        lengths_ref,
        (rows_ref, gains_ref, up_bias_ref),
        bias_ref,
        (
            mixed_ref,
            keep["packed"],
            keep["attended"],
            sum_ref,
            first_ref,
            low_ref,
            keep["act"],
            result_ref,
        ),
        keep,
    )
    gains = gains_ref[...].astype(f32)
    for r in range(0, tokens, STRIP):
        strip = slice(r, r + STRIP)
        grad = cotangent_ref[strip].astype(f32) * gains[1:2]
        grad_sum = norm_back(grad, keep["second_norm"][strip], keep["second_scale"][strip, :1])
        first_ref[strip] = grad_sum
        low_ref[strip] = grad_sum.astype(bf16)
    gate_body(low_ref, down_ref, keep["slope"], gate_ref)
    for c in range(0, width, 2 * SLOT):
        cols = slice(c, c + 2 * SLOT)
        sum_ref[:, cols] = first_ref[:, cols] + dot(gate_ref[...], up_ref[cols, :], NT)
    for r in range(0, tokens, STRIP):
        strip = slice(r, r + STRIP)
        grad = sum_ref[strip] * gains[0:1]
        grad_mid = norm_back(grad, keep["first_norm"][strip], keep["first_scale"][strip, :1])
        first_ref[strip] = grad_mid
        low_ref[strip] = grad_mid.astype(bf16)
    grad_ref[...] = dot(low_ref[...], output_ref[...], NT).astype(bf16)
    for p in range(tokens // SLOT):
        for pair in range(PAIRS):
            attention_back(
                p, pair, keep["packed"], keep["probs"], grad_ref, grad_packed_ref, width
            )
    for c in range(0, width, 2 * SLOT):
        cols = slice(c, c + 2 * SLOT)
        grad_in = first_ref[:, cols] + dot(grad_packed_ref[...], input_ref[cols, :], NT)
        grad_in_ref[:, cols] = grad_in.astype(bf16)


def gate_body(grad_ref, down_ref, slope_ref, gate_ref):
    for c in range(0, gate_ref.shape[1], 2 * SLOT):
        cols = slice(c, c + 2 * SLOT)
        value = dot(grad_ref[...], down_ref[cols, :], NT) * slope_ref[:, cols].astype(f32)
        gate_ref[:, cols] = value.astype(bf16)


def store_shares(value, row, column, outs, cuts, share):
    rows, columns = value.shape
    value = value.astype(bf16)
    if not cuts:
        outs[0][row : row + rows, column : column + columns] = value
        return
    even = lax.axis_index("dp") % 2 == 0
    for pair in range(row // (2 * share), (row + rows) // (2 * share)):
        top = 2 * pair * share - row
        for i, (start, count, left, width) in enumerate(cuts):
            from_column, to_column = max(column, left), min(column + columns, left + width)
            if from_column >= to_column:
                continue
            cols = slice(from_column - column, to_column - column)
            first = value[top + start : top + start + count, cols]
            second = value[top + share + start : top + share + start + count, cols]
            cols = slice(from_column - left, to_column - left)
            at = pair % 2 * 4 + pair // 2
            outs[2 * i][at, :, cols] = jnp.where(even, second, first)
            outs[2 * i + 1][at, :, cols] = jnp.where(even, first, second)


def column_sum(value):
    return jnp.sum(value, axis=0, keepdims=True)


def feed_kernel(
    cotangent_ref, arrived_ref, gains_ref, normed_ref, scale_ref, act_ref, *rest, outs, cuts, share
):
    shares_out, (grad_sum_ref, low_ref, small_ref) = rest[:outs], rest[outs:]
    tokens = low_ref.shape[0]
    hidden = act_ref.shape[1]
    gains = gains_ref[...].astype(f32)
    last = lax.axis_index("section") == lax.axis_size("section") - 1
    sums = [0.0, 0.0, 0.0]
    for r in range(0, tokens, STRIP):
        strip = slice(r, r + STRIP)
        grad_out = jnp.where(
            last, cotangent_ref[strip].astype(f32), arrived_ref[strip].astype(f32)
        )
        normed = normed_ref[strip]
        grad_sum = norm_back(grad_out * gains[1:2], normed, scale_ref[strip, :1])
        low = grad_sum.astype(bf16)
        grad_sum_ref[strip] = grad_sum
        low_ref[strip] = low
        sums[0] = sums[0] + column_sum(low.astype(f32))
        sums[1] = sums[1] + column_sum(grad_out)
        sums[2] = sums[2] + column_sum(grad_out * normed)
    step = 3 * SLOT
    for r in range(0, hidden, step):
        value = dot(act_ref[:, r : r + step], low_ref[...], TN)
        store_shares(value, r, 0, shares_out, cuts, share)
    for i, value in enumerate(sums):
        small_ref[i : i + 1, :] = value


def gate_kernel(low_ref, slope_ref, first_low_ref, down_ref, after, *rest, outs, cuts, share):
    shares_out, (gate_ref, small_ref) = rest[:outs], rest[outs:]
    gate_body(low_ref, down_ref, slope_ref, gate_ref)
    width, hidden = first_low_ref.shape[1], gate_ref.shape[1]
    step = 3 * SLOT
    for r in range(0, width, step):
        left = first_low_ref[:, r : r + step]
        for c in range(0, hidden, width):
            value = dot(left, gate_ref[:, c : c + width], TN)
            store_shares(value, r, c, shares_out, cuts, share)
    for c in range(0, hidden, width):
        cols = slice(c, c + width)
        small_ref[:, cols] = column_sum(gate_ref[:, cols].astype(f32))


def backwards(every):
    shape = (2 * SLOT, 2 * SLOT)
    left, right = iota(shape, 0), iota(shape, 1)
    ends = jnp.where(left < SLOT, SLOT - 1, jnp.where(left < SLOT + B2D, 3 * SLOT - B2D - 1, 0))
    ends = jnp.where(left >= SLOT + B2D, 4 * SLOT - B2D - 1, ends)
    return dot(every, hot(left + right == ends)).astype(bf16)


def table_rows(sums):
    blank = jnp.zeros((SLOT, SLOT), f32)
    near = jnp.concatenate([sums[:SLOT, :SLOT], blank], axis=1)
    near = pltpu.roll(near, 0, 1, stride=1, stride_axis=0)
    lane = iota((B2D, SLOT), 1)
    across = jnp.where(lane < B2D, sums[SLOT : SLOT + B2D, SLOT:], 0.0)
    across = pltpu.roll(across, 0, 1, stride=1, stride_axis=0)
    down = jnp.where(lane >= B2D, sums[SLOT + B2D :, SLOT:], 0.0)
    down = pltpu.roll(down, B2D, 1, stride=1, stride_axis=0)
    return jnp.concatenate([column_sum(near), column_sum(across), column_sum(down)], axis=1)


def chain_kernel(
    grad_sum_ref,
    gate_ref,
    normed_ref,
    scale_ref,
    packed_ref,
    probs_ref,
    order_ref,
    column_ref,
    row_ref,
    gains_ref,
    up_ref,
    output_ref,
    after,
    mid_ref,
    low_ref,
    grad_packed_ref,
    small_ref,
    table_ref,
    sum_ref,
    grad_ref,
    reach_ref,
):
    tokens, width = sum_ref.shape
    pages = tokens // SLOT
    gains = gains_ref[...].astype(f32)
    for c in range(0, width, 2 * SLOT):
        cols = slice(c, c + 2 * SLOT)
        sum_ref[:, cols] = grad_sum_ref[:, cols] + dot(gate_ref[...], up_ref[cols, :], NT)
    first_sum = gain_sum = branch_sum = 0.0
    for r in range(0, tokens, STRIP):
        strip = slice(r, r + STRIP)
        grad_first, normed = sum_ref[strip], normed_ref[strip]
        grad_mid = norm_back(grad_first * gains[0:1], normed, scale_ref[strip, :1])
        low = grad_mid.astype(bf16)
        mid_ref[strip] = grad_mid
        low_ref[strip] = low
        first_sum = first_sum + column_sum(grad_first)
        gain_sum = gain_sum + column_sum(grad_first * normed)
        branch_sum = branch_sum + column_sum(low.astype(f32))
    grad_ref[...] = dot(low_ref[...], output_ref[...], NT).astype(bf16)
    hots = [
        page_hot(order_ref[p : p + 1, :], column_ref[p : p + 1, :], row_ref[p : p + 1, :])
        for p in range(pages)
    ]
    every = backwards(jnp.concatenate(hots, axis=0))
    reach_ref[...] = jnp.zeros_like(reach_ref)
    for pair in range(PAIRS):
        scores = [
            attention_back(p, pair, packed_ref, probs_ref, grad_ref, grad_packed_ref, width)
            for p in range(pages)
        ]
        for head in range(2):
            rows = slice(head * SLOT, (head + 1) * SLOT)
            along = jnp.concatenate([dot(s[rows], h) for s, h in zip(scores, hots)], axis=0)
            sums = dot(every, along.astype(bf16), TN)
            at = 2 * pair + head
            reach_ref[at : at + 1, :] = table_rows(sums)
    for i, value in enumerate((first_sum, gain_sum, branch_sum)):
        small_ref[i : i + 1, :] = value
    table_ref[...] = dot(
        bucket_places().astype(f32), reach_ref[...], NT, precision=lax.Precision.HIGHEST
    )


def last_kernel(
    attended_ref,
    low_ref,
    mixed_low_ref,
    grad_packed_ref,
    block_ref,
    after,
    *shares_out,
    outs,
    cuts,
    share,
):
    width = low_ref.shape[1]
    step = 3 * SLOT
    for r in range(0, width, step):
        rows = slice(r, r + step)
        value = dot(attended_ref[:, rows], low_ref[...], TN)
        store_shares(value, r, 0, shares_out, cuts, share)
        for c in range(0, 3 * width, width):
            value = dot(mixed_low_ref[:, rows], grad_packed_ref[:, c : c + width], TN)
            store_shares(value, r, width + c, shares_out, cuts, share)
        if cuts:
            store_shares(block_ref[rows], r, 4 * width, shares_out, cuts, share)


def input_kernel(
    mid_ref,
    grad_packed_ref,
    tokens_ref,
    small_down_ref,
    small_up_ref,
    small_chain_ref,
    table_ref,
    lengths_ref,
    order_ref,
    region_ref,
    taps_ref,
    input_ref,
    after,
    grad_in_ref,
    small_ref,
    block_ref,
    sum_ref,
    *,
    share,
):
    tokens, width = sum_ref.shape
    pages = tokens // SLOT
    conv_on = (lax.axis_index("section") == 0).astype(f32)
    taps = taps_ref[...].astype(f32) * conv_on
    for c in range(0, width, 2 * SLOT):
        cols = slice(c, c + 2 * SLOT)
        sum_ref[:, cols] = mid_ref[:, cols] + dot(grad_packed_ref[...], input_ref[cols, :], NT)
    tap_sums = [0.0] * TAPS
    mixed_sum = 0.0
    for p in range(pages):
        here = slice(p * SLOT, (p + 1) * SLOT)
        order = order_ref[p : p + 1, :]
        rank_hot = rank_hot_of(order)
        masks = tap_columns(order, region_ref[p : p + 1, :], lengths_ref[p])
        ordered = dot(rank_hot, tokens_ref[here], TN)
        grad_mixed = sum_ref[here]
        grad_order = place_rows(rank_hot, grad_mixed, TN)
        source = jnp.zeros_like(ordered)
        for j in range(TAPS):
            masked = grad_order * masks[:, j : j + 1]
            tap_sums[j] = tap_sums[j] + column_sum(masked * shifted(ordered, j - REACH))
            source = source + shifted(taps[j : j + 1] * masked, REACH - j)
        grad_in_ref[here] = grad_mixed + place_rows(rank_hot, source, NN)
        mixed_sum = mixed_sum + column_sum(grad_mixed)
    down, chain = small_down_ref[...], small_chain_ref[...]
    rows = [
        column_sum(grad_packed_ref[:, :width].astype(f32)),
        column_sum(grad_packed_ref[:, 2 * width :].astype(f32)),
        chain[2:3],
        chain[0:1],
        down[0:1],
        down[1:2],
        conv_on * mixed_sum,
        chain[1:2],
        down[2:3],
    ]
    for i, value in enumerate(rows + [conv_on * value for value in tap_sums]):
        small_ref[i : i + 1, :] = value
    if share:
        small_block(small_ref, small_up_ref, table_ref, block_ref, share)


SMALL_ROWS = 16


def small_block(small_ref, up_ref, table_ref, block_ref, share):
    width = small_ref.shape[1]
    shares = block_ref.shape[0] // share
    part = width // shares
    up_part = up_ref.shape[1] // shares
    buckets = (B1D + 2 * B2D) // shares
    block_ref[...] = jnp.zeros_like(block_ref)
    small, up = small_ref[...], jnp.broadcast_to(up_ref[...], (8, up_ref.shape[1]))
    for s in range(shares):
        top = s * share
        shift = (width - s * part) % width
        here = pltpu.roll(small, shift, 1) if shift else small
        block_ref[top : top + SMALL_ROWS, :] = here[:, :SLOT]
        shift = (up.shape[1] - s * up_part) % up.shape[1]
        here = pltpu.roll(up, shift, 1) if shift else up
        top += SMALL_ROWS
        block_ref[top : top + 1, :] = here[:1, :SLOT]
        block_ref[top + 1 : top + 2, :] = here[:1, SLOT : 2 * SLOT]
        top += 2
        block_ref[top : top + buckets, :] = table_ref[s * buckets : (s + 1) * buckets, :]


def place():
    index = lax.axis_index("dp")
    return index // 4, index // 2 % 2


def added(out_ref, out_at, parts, window=None):
    rows = out_ref.shape[-2]
    for r in range(0, rows, 16):
        strip = slice(r, r + 16)
        total = 0.0
        for ref, at, windowed in parts:
            if windowed:
                row, _, column, columns = window
                value = ref[at, row + r : row + r + 16, column : column + columns]
            else:
                value = ref[at, strip]
            total = total + value.astype(f32)
        if out_at is None:
            out_ref[strip] = total.astype(bf16)
        else:
            out_ref[out_at, strip] = total.astype(bf16)


def fetched(recv_hbm, first, window, scratch, sems):
    row, rows, column, columns = window
    copies = []
    for k in range(4):
        source = recv_hbm.at[first + k, pl.ds(row, rows), pl.ds(column, columns)]
        copies.append(pltpu.make_async_copy(source, scratch.at[k], sems.at[k]))
        copies[-1].start()
    return copies


def leave_kernel(mine_ref, recv_ref, *rest, window, fetch):
    first = 4 * (1 - place()[1])
    if fetch:
        out_ref, scratch, sems = rest[-3:]
        copies = fetched(recv_ref, first, window, scratch, sems)
    else:
        out_ref = rest[-1]
    for k in range(4):
        other = (recv_ref, first + k, True)
        if fetch:
            copies[k].wait()
            other = (scratch, k, False)
        added(out_ref, k, ((mine_ref, first + k, True), other), window)


def near_kernel(mine_ref, recv_ref, y_ref, after, leave_ref, keep_ref, *rest, window, fetch):
    z, y = place()
    if fetch:
        scratch, sems = rest
        for copy in fetched(recv_ref, 4 * y, window, scratch, sems):
            copy.wait()
    for out_ref, parity in ((leave_ref, 1 - z % 2), (keep_ref, z % 2)):
        for k in range(2):
            block = 2 * k + parity
            at = 4 * y + block
            other = (scratch, block, False) if fetch else (recv_ref, at, True)
            added(out_ref, k, ((mine_ref, at, True), other, (y_ref, block, False)), window)


def far_kernel(keep_ref, recv_ref, *rest):
    leave_ref, own_ref = rest[-2:]
    high = place()[0] // 2
    for out_ref, k in ((leave_ref, 1 - high), (own_ref, high)):
        added(out_ref, None, ((keep_ref, k, False), (recv_ref, k, False)))


def near_first_kernel(mine_ref, recv_ref, after, leave_ref, keep_ref):
    z, _ = place()
    for out_ref, parity in ((leave_ref, 1 - z % 2), (keep_ref, z % 2)):
        for k in range(4):
            at = 2 * k + parity
            added(out_ref, k, ((mine_ref, at, False), (recv_ref, at, False)))


def far_first_kernel(keep_ref, recv_ref, after, leave_ref, stay_ref):
    high = place()[0] // 2
    for out_ref, k in ((leave_ref, 1 - high), (stay_ref, high)):
        for y in range(2):
            at = 2 * y + k
            added(out_ref, y, ((keep_ref, at, False), (recv_ref, at, False)))


def cross_kernel(keep_ref, recv_ref, after, leave_ref, own_ref):
    y = place()[1]
    for out_ref, at in ((leave_ref, 1 - y), (own_ref, y)):
        added(out_ref, None, ((keep_ref, at, False), (recv_ref, at, False)))


def both(parts):
    return parts[0][...].astype(f32) + parts[1][...].astype(f32)


def down_end(*refs):
    out_ref, token_ref = refs[-2:]
    token_ref[...] = jnp.zeros_like(token_ref)
    rows = refs[0].shape[0]
    out_ref[:rows] = both(refs[:2])
    out_ref[rows:] = both(refs[2:4])


def up_end(*refs):
    out_ref, token_ref = refs[-2:]
    token_ref[...] = jnp.zeros_like(token_ref)
    columns = refs[0].shape[1]
    out_ref[:, :columns] = both(refs[:2])
    out_ref[:, columns:] = both(refs[2:4])


def last_end(*refs):
    sum_ref, block_ref = refs[-2:]
    input_ref, output_ref, bias_ref, gain_ref, tap_ref, up_ref, table_ref = refs[-9:-2]
    column = 0
    for i in range(0, len(refs) - 10, 2):
        columns = refs[i].shape[1]
        sum_ref[:, column : column + columns] = both(refs[i : i + 2])
        column += columns
    width, share = output_ref.shape[1], output_ref.shape[0]
    output_ref[...] = sum_ref[:, :width]
    input_ref[...] = sum_ref[:, width : 4 * width]
    block_ref[...] = sum_ref[:, 4 * width :]
    for i in range(7):
        bias_ref[i] = block_ref[i : i + 1, :share]
        tap_ref[i] = block_ref[9 + i : 10 + i, :share]
    gain_ref[...] = block_ref[7:9, :share]
    rest = up_ref.shape[1] - SLOT
    up_ref[:, :SLOT] = block_ref[SMALL_ROWS : SMALL_ROWS + 1, :]
    up_ref[:, SLOT:] = block_ref[SMALL_ROWS + 1 : SMALL_ROWS + 2, :rest]
    for i in range(table_ref.shape[1] // HEADS):
        at = SMALL_ROWS + 2 + i
        table_ref[:, i * HEADS : (i + 1) * HEADS] = block_ref[at : at + 1, :HEADS]


def kernel_call(body, name, ins, outs, scratch, flops=0, vmem=10):
    return pl.pallas_call(
        body,
        name=name,
        out_shape=[shape for shape, _ in outs],
        in_specs=[spec for _, spec in ins],
        out_specs=[spec for _, spec in outs],
        scratch_shapes=scratch,
        compiler_params=pltpu.CompilerParams(vmem_limit_bytes=vmem << 20),
        cost_estimate=pl.CostEstimate(flops=flops, bytes_accessed=0, transcendentals=0),
    )(*[value for value, _ in ins])


def near_by(value):
    return pltpu.with_memory_space_constraint(value, pltpu.VMEM)


def in_hbm(value):
    return pltpu.with_memory_space_constraint(value, pltpu.HBM)


def near_shape(dims, kind=bf16):
    return pltpu.VMEM(dims, kind)


class Summing:
    def __init__(self):
        self.pairs, self.windows, self.crossed, self.kept, self.ends = {}, {}, {}, {}, {}
        self.fetch = {}

    @staticmethod
    def _swap(value, bits):
        return near_by(lax.ppermute(value, "dp", [(i, i ^ bits) for i in range(16)]))

    @staticmethod
    def _add(body, name, ins, after, outs, cost=0, earlier=(), scratch=(), fetch=False):
        specs = [IN_VMEM] * len(ins)
        if fetch:
            specs[1] = IN_PLACE
        return kernel_call(
            body,
            name,
            [(near_by(value), spec) for value, spec in zip(ins, specs)]
            + [(value, IN_PLACE) for value in (after, *earlier)],
            [(near_shape(dims), IN_VMEM) for dims in outs],
            list(scratch),
            cost,
            4,
        )

    def core(self, theirs, mine, fetch=False, **windows):
        recv = self._swap(theirs, 1)
        for name, window in windows.items():
            self.pairs[name], self.windows[name] = [mine, recv], window
            self.fetch[name] = fetch

    def _fetching(self, name, body):
        window, fetch = self.windows[name], self.fetch[name]
        dims = (4, window[1], window[3])
        scratch = [pltpu.VMEM(dims, bf16), pltpu.SemaphoreType.DMA((4,))] if fetch else []
        body = functools.partial(body, window=window, fetch=fetch)
        return body, dict(scratch=scratch, fetch=fetch), dims

    def leave(self, name, after, earlier=None):
        body, more, dims = self._fetching(name, leave_kernel)
        earlier = [self.crossed[earlier]] if earlier else []
        (out,) = self._add(body, "leave", self.pairs[name], after, [dims], 0, earlier, **more)
        self.crossed[name] = self._swap(out, 2)
        return out

    def near(self, name, after):
        body, more, dims = self._fetching(name, near_kernel)
        dims = (2,) + dims[1:]
        ins = self.pairs[name] + [self.crossed[name]]
        out, keep = self._add(body, "near", ins, after, [dims, dims], COST, **more)
        self.kept[name] = [keep, self._swap(out, 4)]
        return out

    def far(self, name, after, earlier=()):
        ins = self.kept[name]
        dims = ins[0].shape[1:]
        earlier = [self.ends[other][1] for other in earlier]
        out, own = self._add(far_kernel, "far", ins, after, [dims, dims], COST, earlier)
        self.ends[name] = [own, self._swap(out, 8)]
        return out

    def near_first(self, name, after):
        ins = self.pairs[name]
        dims = (4,) + ins[0].shape[1:]
        out, keep = self._add(near_first_kernel, "near_first", ins, after, [dims, dims], COST)
        self.kept[name] = [keep, self._swap(out, 4)]
        return out

    def far_first(self, name, after):
        ins = self.kept[name]
        dims = (2,) + ins[0].shape[1:]
        out, stay = self._add(far_first_kernel, "far_first", ins, after, [dims, dims], COST)
        self.kept[name] = [stay, self._swap(out, 8)]
        return out

    def cross(self, name, after):
        ins = self.kept[name]
        dims = ins[0].shape[1:]
        out, own = self._add(cross_kernel, "cross", ins, after, [dims, dims], COST)
        self.ends[name] = [own, self._swap(out, 2)]
        return out


def local(
    tokens,
    cotangent,
    page_lengths,
    cut_order,
    cut_region,
    cell_column,
    cell_row,
    input_proj,
    output_proj,
    up_proj,
    down_proj,
    up_bias,
    bias_rows,
    gain_rows,
    conv_taps,
    bias_table,
):
    section_count = lax.axis_size("section")
    dp_count = lax.axis_size("dp")
    by_hops = dp_count == 16
    pages, _, width = tokens.shape
    hidden = up_proj.shape[2]
    count = pages * SLOT
    weights = [w[0] for w in (input_proj, output_proj, up_proj, down_proj)]
    rows, gains, taps = bias_rows[0], gain_rows[0], conv_taps[0]
    tokens, cotangent = tokens.reshape(count, width), cotangent.reshape(count, width)

    def shape(dims, kind):
        return jax.ShapeDtypeStruct(dims, kind)

    def inside(*values):
        return [(v, IN_VMEM) for v in values]

    def in_place(*values):
        return [(v, IN_PLACE) for v in values]

    def scalars(*values):
        return [(v, IN_SMEM) for v in values]

    wide, low = shape((count, width), f32), shape((count, width), bf16)
    wide_scratch = pltpu.VMEM((count, width), f32)
    low_scratch = pltpu.VMEM((count, width), bf16)
    packed_scratch = pltpu.VMEM((count, 3 * width), bf16)
    hidden_scratch = pltpu.VMEM((count, hidden), bf16)
    bias_dims = (pages * HEADS * SLOT, SLOT)

    def sems(number):
        return pltpu.SemaphoreType.DMA((number,))

    first_ins = [tokens, cut_order, cut_region, cell_column, cell_row, rows, gains, up_bias]
    first_ins += [taps, bias_table]
    result, mixed, bias, *near_weights = kernel_call(
        first_kernel,
        "first",
        scalars(in_hbm(page_lengths)) + in_place(*map(in_hbm, first_ins + weights)),
        inside(low, near_shape((count, width), f32), near_shape(bias_dims, f32))
        + inside(*[near_shape(w.shape) for w in weights]),
        [
            packed_scratch,
            low_scratch,
            wide_scratch,
            wide_scratch,
            low_scratch,
            hidden_scratch,
            *[pltpu.VMEM(v.shape, v.dtype) for v in first_ins],
            sems(len(first_ins) + len(weights)),
        ],
    )
    input_w, output_w, up_w, down_w = near_weights = list(map(near_by, near_weights))
    arrived = near_by(
        lax.ppermute(result, "section", [(i, i + 1) for i in range(section_count - 1)])
    )
    shapes = kept_shapes(count, width, hidden)
    layer_out, leaving, *kept_list = kernel_call(
        second_kernel,
        "second",
        inside(arrived, cotangent)
        + scalars(page_lengths)
        + inside(rows, gains, up_bias)
        + inside(*map(near_by, (mixed, bias, *near_weights))),
        inside(low, near_shape((count, width)), *[near_shape(*s) for s in shapes]),
        [
            wide_scratch,
            wide_scratch,
            wide_scratch,
            low_scratch,
            hidden_scratch,
            low_scratch,
            packed_scratch,
        ],
    )
    kept = dict(zip([name for name, _, _ in KEPT], map(near_by, kept_list)))
    arrived_grad = near_by(
        lax.ppermute(leaving, "section", [(i + 1, i) for i in range(section_count - 1)])
    )
    part = width // dp_count

    def cut(dims, cuts):
        share = dims[0] // dp_count
        if not by_hops:
            outs, cuts = inside(shape(dims, bf16)), ()
        else:
            halves_out = [near_shape((dp_count // 2, c[1], c[3])) for c in cuts for _ in range(2)]
            outs = inside(*halves_out)
        return outs, dict(outs=len(outs), cuts=cuts, share=share)

    half = hidden // dp_count // 2
    down_outs, down_cut = cut((hidden, width), ((0, half, 0, width), (half, half, 0, width)))
    up_outs, up_cut = cut((width, hidden), ((0, part, 0, hidden),))
    *down_parts, grad_sum, grad_low, small_down = kernel_call(
        functools.partial(feed_kernel, **down_cut),
        "feed",
        inside(cotangent, arrived_grad, gains)
        + inside(kept["second_norm"], kept["second_scale"], kept["act"]),
        down_outs + inside(wide, low, shape((8, width), f32)),
        [],
    )
    *up_parts, gate, small_up = kernel_call(
        functools.partial(gate_kernel, **up_cut),
        "gate",
        inside(grad_low, kept["slope"], kept["first_low"], down_w) + in_place(small_down),
        up_outs + inside(shape((count, hidden), bf16), shape((1, hidden), f32)),
        [],
    )
    summing = Summing()
    after = small_up
    if by_hops:
        piece = (0, half, 0, width)
        side = hidden // 2
        summing.core(*down_parts[:2], d1=piece)
        summing.core(*down_parts[2:], d2=piece)
        summing.core(*up_parts, u1=(0, part, 0, side), u2=(0, part, side, side))
        after = summing.leave("d1", after)
        after = summing.near_first("d2", after)
        after = summing.leave("u1", after)
    grad_mid, grad_branch, grad_packed, small_chain, table = kernel_call(
        chain_kernel,
        "chain",
        inside(grad_sum, gate, kept["first_norm"], kept["first_scale"], kept["packed"])
        + inside(kept["probs"], cut_order, cell_column, cell_row, gains)
        + inside(up_w, output_w)
        + in_place(after),
        inside(wide, low, shape((count, 3 * width), bf16), shape((8, width), f32))
        + inside(shape((B1D + 2 * B2D, SLOT), f32)),
        [wide_scratch, low_scratch, pltpu.VMEM((SLOT, 4 * SLOT), f32)],
    )
    after = grad_mid
    if by_hops:
        after = summing.near("d1", after)
        after = summing.far_first("d2", after)
        after = summing.leave("u2", after)
    grad_in, small_rows, block = kernel_call(
        functools.partial(input_kernel, share=part if by_hops else 0),
        "input",
        inside(grad_mid, grad_packed, tokens, small_down, small_up, small_chain, table)
        + scalars(page_lengths)
        + inside(cut_order, cut_region, taps, input_w)
        + in_place(after),
        inside(wide, shape((16, width), f32), near_shape((width, SLOT), f32)),
        [wide_scratch],
    )
    after = block
    columns = 4 * width + (SLOT if by_hops else 0)
    last_outs, last_cut = cut((width, columns), ((0, part, 0, columns),))
    last_parts = kernel_call(
        functools.partial(last_kernel, **last_cut),
        "last",
        inside(kept["attended"], grad_branch, kept["mixed_low"], grad_packed, near_by(block))
        + in_place(after),
        last_outs,
        [],
    )
    after = last_parts[0]
    if by_hops:
        token = near_shape((8, SLOT), f32)
        windows, column = {}, 0
        for name, end in (("a1", 2 * width), ("a2", 3 * width + 2 * SLOT), ("a3", columns)):
            windows[name], column = (0, part, column, end - column), end
        summing.core(*last_parts, fetch=True, **windows)
        ends = summing.ends
        after = summing.near("u1", after)
        after = summing.far("d1", after)
        after = summing.cross("d2", after)
        after = summing.leave("a1", after, "u2")
        after = summing.near("u2", after)
        after = summing.far("u1", after, ["d1"])
        after = summing.leave("a2", after)
        down_grad, after = kernel_call(
            down_end,
            "down_end",
            inside(*map(near_by, ends["d1"] + ends["d2"])) + in_place(after),
            inside(shape((hidden // dp_count, width), f32), token),
            [],
            vmem=4,
        )
        after = summing.far("u2", after)
        after = summing.near("a1", after)
        after = summing.leave("a3", after)
        after = summing.near("a2", after)
        after = summing.far("a1", after)
        up_grad, after = kernel_call(
            up_end,
            "up_end",
            inside(*map(near_by, ends["u1"] + ends["u2"])) + in_place(after),
            inside(shape((part, hidden), f32), token),
            [],
            vmem=4,
        )
        after = summing.near("a3", after)
        after = summing.far("a2", after)
        after = summing.far("a3", after)
        input_grad, output_grad, bias_grad, gain_grad, tap_grad, up_bias_grad, table_grad = (
            kernel_call(
                last_end,
                "last_end",
                inside(*map(near_by, ends["a1"] + ends["a2"] + ends["a3"])) + in_place(after),
                inside(
                    shape((part, 3 * width), f32),
                    shape((part, width), f32),
                    shape((7, 1, part), f32),
                    shape((2, part), f32),
                    shape((TAPS, 1, part), f32),
                    shape((1, hidden // dp_count), f32),
                    shape((1, table.shape[0] * HEADS // dp_count), f32),
                ),
                [pltpu.VMEM((part, columns), f32), pltpu.VMEM((part, SLOT), f32)],
                vmem=4,
            )
        )
    else:

        def scattered(value):
            return lax.psum_scatter(value, "dp", scatter_dimension=0, tiled=True).astype(f32)

        down_grad, up_grad, last_grad = (
            scattered(parts[0]) for parts in (down_parts, up_parts, last_parts)
        )
        input_grad, output_grad = last_grad[:, width:], last_grad[:, :width]
        small = [
            small_rows.reshape(16, dp_count, part).transpose(1, 0, 2).reshape(dp_count, -1),
            small_up.reshape(dp_count, -1),
            table[:, :HEADS].reshape(dp_count, -1),
        ]
        small = jnp.concatenate(small, axis=1)
        used = small.shape[1]
        small = jnp.pad(small, ((0, 0), (0, -used % SLOT))).reshape(-1, SLOT)
        small = scattered(small).reshape(-1)
        vectors = small[: 16 * part].reshape(16, part)
        bias_grad, tap_grad = vectors[:7, None], vectors[9:, None]
        gain_grad = vectors[7:9]
        at = 16 * part + hidden // dp_count
        up_bias_grad, table_grad = small[None, 16 * part : at], small[None, at:used]
    return (
        layer_out.reshape(1, pages, SLOT, width),
        grad_in.reshape(1, pages, SLOT, width),
        input_grad[None],
        output_grad[None],
        up_grad[None],
        down_grad[None],
        up_bias_grad,
        bias_grad.transpose(1, 0, 2),
        gain_grad[None],
        tap_grad.transpose(1, 0, 2),
        table_grad,
    )


def solution(mesh):
    by_section = [P("section", None, None)] * 4
    placed = (
        P("dp", None, None),
        P("dp", None, None),
        P("dp"),
        P("dp", None),
        P("dp", None),
        P("dp", None),
        P("dp", None),
        *by_section,
        P("section", None),
        P("section", None, None),
        P("section", None, None),
        P("section", None, None),
        P("section", None),
    )
    return jax.shard_map(
        local,
        mesh=mesh,
        in_specs=placed,
        out_specs=(
            P("section", "dp", None, None),
            P("section", "dp", None, None),
            P("section", "dp", None),
            P("section", "dp", None),
            P("section", "dp", None),
            P("section", "dp", None),
            P("section", "dp"),
            P("section", None, "dp"),
            P("section", None, "dp"),
            P("section", None, "dp"),
            P("section", "dp"),
        ),
        check_vma=False,
    )
```

```python
import functools

import jax
import jax.numpy as jnp
from jax import lax
from jax.experimental import pallas as pl
from jax.experimental.pallas import tpu as pltpu
from jax.sharding import PartitionSpec as P

HEADS = 12
HEAD = 64
B1D = 32
B2D = 64
SLOT = 128
PAIRS = HEADS // 2
TAPS = 7
REACH = 3
EPSILON = 1e-05
COST = 20_000_000_000
MASKED = -1000000000.0
STRIP = 64

f32 = jnp.float32
bf16 = jnp.bfloat16
NN = ((1,), (0,))
NT = ((1,), (1,))
TN = ((0,), (0,))

IN_VMEM = pl.BlockSpec(memory_space=pltpu.VMEM)
IN_SMEM = pl.BlockSpec(memory_space=pltpu.SMEM)
IN_PLACE = pl.BlockSpec(memory_space=pl.ANY)


def dot(left, right, dims=NN, precision=None):
    return lax.dot_general(
        left, right, (dims, ((), ())), precision=precision, preferred_element_type=f32
    )


def iota(shape, axis):
    return lax.broadcasted_iota(jnp.int32, shape, axis)


def hot(mask):
    return mask.astype(f32).astype(bf16)


def identity():
    return hot(iota((SLOT, SLOT), 0) == iota((SLOT, SLOT), 1))


def rank_hot_of(order):
    return hot(order == iota((SLOT, SLOT), 0))


def page_hot(order, column, row):
    cells = iota((SLOT, SLOT), 0)
    wanted = jnp.where(cells < B2D, column, row + B2D)
    cell_hot = dot(identity(), hot(wanted == cells), NT).astype(bf16)
    return jnp.concatenate([rank_hot_of(order), cell_hot], axis=1)


def tap_columns(order, region, length):
    shape = (8, SLOT)
    order, region = jnp.broadcast_to(order, shape), jnp.broadcast_to(region, shape)
    live = (order < length).astype(jnp.int32)
    lane, tap = iota(shape, 1), iota(shape, 0)
    masks = jnp.zeros(shape, f32)
    for j in range(TAPS):
        offset = j - REACH
        shift = (-offset) % SLOT
        region_j = pltpu.roll(region, shift, 1) if shift else region
        live_j = pltpu.roll(live, shift, 1) if shift else live
        joined = (lane + offset >= 0) & (lane + offset < SLOT) & (region_j == region) & (live_j > 0)
        masks = jnp.where((tap == j) & joined, 1.0, masks)
    return dot(identity(), masks.astype(bf16), NT)


def shifted(rows, offset):
    shift = (-offset) % SLOT
    return pltpu.roll(rows, shift, 0) if shift else rows


def place_rows(rank_hot, rows, dims):
    high = rows.astype(bf16)
    low = (rows - high.astype(f32)).astype(bf16)
    return dot(rank_hot, high, dims) + dot(rank_hot, low, dims)


def bucket_places():
    shape = (B1D + 2 * B2D, 4 * SLOT)
    bucket, lane = iota(shape, 0), iota(shape, 1)
    near = jnp.clip(lane - (SLOT - 1) + B1D // 2, 0, B1D - 1)
    column = B1D + jnp.clip(lane - 2 * SLOT - (B2D - 1) + B2D // 2, 0, B2D - 1)
    row = B1D + B2D + jnp.clip(lane - 3 * SLOT - (B2D - 1) + B2D // 2, 0, B2D - 1)
    wanted = jnp.where(lane < 2 * SLOT, near, jnp.where(lane < 3 * SLOT, column, row))
    return bucket == wanted


def halves(pair):
    lane = iota((1, SLOT), 1)
    first = hot(lane < HEAD)
    second = hot(lane >= HEAD)
    return jnp.concatenate([pair * first, pair * second], axis=0)


def side_by_side(stacked):
    return jnp.concatenate([stacked[:SLOT], stacked[SLOT:]], axis=1)


def normed_of(value):
    average = jnp.mean(value, axis=-1, keepdims=True)
    centered = value - average
    spread = jnp.mean(centered * centered, axis=-1, keepdims=True)
    inverse = lax.rsqrt(spread + EPSILON)
    return centered * inverse, inverse


def norm_back(grad, normed, inverse):
    first_mean = jnp.mean(grad, axis=-1, keepdims=True)
    second_mean = jnp.mean(grad * normed, axis=-1, keepdims=True)
    return inverse * (grad - first_mean - normed * second_mean)


def table_columns(table):
    buckets = table.shape[1] // HEADS
    bucket = iota((buckets, table.shape[1]), 0) * HEADS
    lane = iota((buckets, table.shape[1]), 1)
    own = hot((lane >= bucket) & (lane < bucket + HEADS))
    lane = iota((16, table.shape[1]), 1)
    times = ((lane.astype(f32) + 0.5) * (1.0 / HEADS)).astype(jnp.int32)
    head = hot(lane - HEADS * times == iota((16, table.shape[1]), 0))
    return dot(own * table, head, NT).astype(bf16)


def bias_body(order_ref, column_ref, row_ref, table_ref, bias_ref, grids_ref, hot_rows_ref):
    pages = order_ref.shape[0]
    hots = [
        page_hot(order_ref[p : p + 1, :], column_ref[p : p + 1, :], row_ref[p : p + 1, :])
        for p in range(pages)
    ]
    every = jnp.concatenate(hots, axis=0)
    reach = dot(table_columns(table_ref[...]), hot(bucket_places()), TN)
    lane = iota((B2D, SLOT), 1)
    for h in range(HEADS):
        row = reach[h : h + 1, :]
        near = jnp.broadcast_to(row[:, : 2 * SLOT], (SLOT, 2 * SLOT))
        near = pltpu.roll(near, SLOT + 1, 1, stride=1, stride_axis=0)[:, :SLOT]
        across = jnp.broadcast_to(row[:, 2 * SLOT : 3 * SLOT], (B2D, SLOT))
        across = pltpu.roll(across, B2D + 1, 1, stride=1, stride_axis=0)
        down = jnp.broadcast_to(row[:, 3 * SLOT :], (B2D, SLOT))
        down = pltpu.roll(down, 1, 1, stride=1, stride_axis=0)
        cells = jnp.concatenate(
            [jnp.where(lane < B2D, across, 0.0), jnp.where(lane >= B2D, down, 0.0)], axis=0
        )
        blank = jnp.zeros((SLOT, SLOT), bf16)
        grids_ref[h, :SLOT, :SLOT] = near.astype(bf16)
        grids_ref[h, :SLOT, SLOT:] = blank
        grids_ref[h, SLOT:, :SLOT] = blank
        grids_ref[h, SLOT:, SLOT:] = cells.astype(bf16)
    for h in range(HEADS):
        hot_rows_ref[h] = dot(every, grids_ref[h]).astype(bf16)
    for p in range(pages):
        for h in range(HEADS):
            at = (p * HEADS + h) * SLOT
            rows = hot_rows_ref[h, p * SLOT : (p + 1) * SLOT, :]
            bias_ref[at : at + SLOT, :] = dot(rows, hots[p], NT)


def forward_body(weights, waits, lengths_ref, vectors, bias_ref, work, keep):
    input_ref, output_ref, up_ref, down_ref = weights
    rows_ref, gains_ref, up_bias_ref = vectors
    mixed_ref, packed_ref, attended_ref, sum_ref, first_ref, low_ref, act_ref, result_ref = work[:8]
    scores_ref, probs_ref = work[8:]
    rows, gains = rows_ref[...].astype(f32), gains_ref[...].astype(f32)
    tokens, width = mixed_ref.shape
    hidden = act_ref.shape[1]
    low_ref[...] = mixed_ref[...].astype(bf16)
    if keep:
        keep["mixed_low"][...] = low_ref[...]
    waits[0]()
    for part, add in ((0, rows[0:1]), (1, None), (2, rows[1:2])):
        cols = slice(part * width, (part + 1) * width)
        value = dot(low_ref[...], input_ref[:, cols])
        packed_ref[:, cols] = (value if add is None else value + add).astype(bf16)
    places = [(p, pair) for p in range(tokens // SLOT) for pair in range(PAIRS)]
    for p, pair in places:
        here, at = slice(p * SLOT, (p + 1) * SLOT), pair * SLOT
        top = (p * HEADS + 2 * pair) * SLOT
        queries = halves(packed_ref[here, at : at + SLOT]) * (HEAD**-0.5)
        keys = packed_ref[here, width + at : width + at + SLOT]
        scores_ref[top : top + 2 * SLOT, :] = dot(queries, keys, NT)
    for p, pair in places:
        top = (p * HEADS + 2 * pair) * SLOT
        rows_here = slice(top, top + 2 * SLOT)
        live = iota((2 * SLOT, SLOT), 1) < lengths_ref[p]
        scores = jnp.where(live, scores_ref[rows_here, :] + bias_ref[rows_here, :], MASKED)
        expo = jnp.exp(scores - jnp.max(scores, axis=-1, keepdims=True))
        probs = expo * (1.0 / jnp.sum(expo, axis=-1, keepdims=True))
        probs_ref[rows_here, :] = probs.astype(bf16)
    for p, pair in places:
        here, at = slice(p * SLOT, (p + 1) * SLOT), pair * SLOT
        top = (p * HEADS + 2 * pair) * SLOT
        values = halves(packed_ref[here, 2 * width + at : 2 * width + at + SLOT])
        probs = side_by_side(probs_ref[top : top + 2 * SLOT, :])
        attended_ref[here, at : at + SLOT] = dot(probs, values).astype(bf16)
    waits[1]()
    sum_ref[...] = dot(attended_ref[...], output_ref[...])
    for r in range(0, tokens, STRIP):
        strip = slice(r, r + STRIP)
        normed, inverse = normed_of(mixed_ref[strip] + sum_ref[strip] + rows[2:3])
        first = normed * gains[0:1] + rows[3:4]
        first_ref[strip] = first
        low_ref[strip] = first.astype(bf16)
        if keep:
            keep["first_norm"][strip] = normed
            keep["first_scale"][strip] = jnp.broadcast_to(inverse, (STRIP, SLOT))
            keep["first_low"][strip] = first.astype(bf16)
    waits[2]()
    for c in range(0, hidden, 2 * SLOT):
        cols = slice(c, c + 2 * SLOT)
        gate = dot(low_ref[...], up_ref[:, cols]) + up_bias_ref[:, cols].astype(f32)
        below = 0.5 + 0.5 * lax.erf(gate * 0.7071067811865476)
        act_ref[:, cols] = (gate * below).astype(bf16)
        if keep:
            density = jnp.exp(-0.5 * gate * gate) * 0.3989422804014327
            keep["slope"][:, cols] = (below + gate * density).astype(bf16)
    waits[3]()
    sum_ref[...] = dot(act_ref[...], down_ref[...])
    for r in range(0, tokens, STRIP):
        strip = slice(r, r + STRIP)
        normed, inverse = normed_of(first_ref[strip] + sum_ref[strip] + rows[4:5])
        result_ref[strip] = (normed * gains[1:2] + rows[5:6]).astype(bf16)
        if keep:
            keep["second_norm"][strip] = normed
            keep["second_scale"][strip] = jnp.broadcast_to(inverse, (STRIP, SLOT))


def attention_back(packed_ref, probs_ref, grad_ref, grad_packed_ref, scores_ref, grads_ref):
    tokens, width = grad_ref.shape
    places = [(p, pair) for p in range(tokens // SLOT) for pair in range(PAIRS)]

    def rows_of(p, pair):
        top = (p * HEADS + 2 * pair) * SLOT
        return slice(top, top + 2 * SLOT)

    def part_of(ref, p, pair, part=0):
        at = part * width + pair * SLOT
        return ref[p * SLOT : (p + 1) * SLOT, at : at + SLOT]

    for p, pair in places:
        grad, values = halves(part_of(grad_ref, p, pair)), part_of(packed_ref, p, pair, 2)
        scores_ref[rows_of(p, pair), :] = dot(grad, values, NT)
    for p, pair in places:
        rows = rows_of(p, pair)
        probs, grad_probs = probs_ref[rows, :].astype(f32), scores_ref[rows, :]
        inner = jnp.sum(probs * grad_probs, axis=-1, keepdims=True)
        grads_ref[rows, :] = (probs * (grad_probs - inner)).astype(bf16)
    for p, pair in places:
        rows = rows_of(p, pair)
        queries = halves(part_of(packed_ref, p, pair)) * (HEAD**-0.5)
        keys = halves(part_of(packed_ref, p, pair, 1)) * (HEAD**-0.5)
        grad = halves(part_of(grad_ref, p, pair))
        for part, value in (
            (0, dot(side_by_side(grads_ref[rows, :]), keys)),
            (1, dot(grads_ref[rows, :], queries, TN)),
            (2, dot(probs_ref[rows, :], grad, TN)),
        ):
            at = part * width + pair * SLOT
            grad_packed_ref[p * SLOT : (p + 1) * SLOT, at : at + SLOT] = value.astype(bf16)


def first_kernel(lengths_ref, *rest):
    ins, weight_ins, rest = rest[:10], rest[10:14], rest[14:]
    result_ref, mixed_ref, bias_ref, *weights = rest[:7]
    packed_ref, attended_ref, sum_ref, first_ref, low_ref, act_ref = rest[7:13]
    scores_ref, probs_ref, grids_ref, hot_rows_ref = rest[13:17]
    held, sems = rest[17:27], rest[27]
    small = [pltpu.make_async_copy(a, b, sems.at[i]) for i, (a, b) in enumerate(zip(ins, held))]
    copies = [
        pltpu.make_async_copy(a, b, sems.at[len(small) + i])
        for i, (a, b) in enumerate(zip(weight_ins, weights))
    ]
    for copy in small:
        copy.start()
    copies[0].start()
    for copy in small:
        copy.wait()
    tokens_ref, order_ref, region_ref, column_ref, row_ref = held[:5]
    rows_ref, gains_ref, up_bias_ref, taps_ref, table_ref = held[5:]
    conv_on = (lax.axis_index("section") == 0).astype(f32)
    taps = taps_ref[...].astype(f32) * conv_on
    conv_bias = rows_ref[...].astype(f32)[6:7] * conv_on
    for p in range(order_ref.shape[0]):
        here = slice(p * SLOT, (p + 1) * SLOT)
        order = order_ref[p : p + 1, :]
        rank_hot = rank_hot_of(order)
        masks = tap_columns(order, region_ref[p : p + 1, :], lengths_ref[p])
        places = dot(identity(), rank_hot, NT)
        sources = [
            dot(rank_hot, (shifted(places, j - REACH) * masks[:, j : j + 1]).astype(bf16))
            for j in range(TAPS)
        ]
        moved = dot(jnp.concatenate(sources, axis=0).astype(bf16), tokens_ref[here])
        total = tokens_ref[here].astype(f32) + conv_bias
        for j in range(TAPS):
            total = total + taps[j : j + 1] * moved[j * SLOT : (j + 1) * SLOT]
        mixed_ref[here] = total
    copies[1].start()
    copies[2].start()
    bias_body(order_ref, column_ref, row_ref, table_ref, bias_ref, grids_ref, hot_rows_ref)

    def wait_input():
        copies[0].wait()
        copies[3].start()

    forward_body(
        weights,
        [wait_input] + [copy.wait for copy in copies[1:]],
        lengths_ref,
        (rows_ref, gains_ref, up_bias_ref),
        bias_ref,
        (
            mixed_ref,
            packed_ref,
            attended_ref,
            sum_ref,
            first_ref,
            low_ref,
            act_ref,
            result_ref,
            scores_ref,
            probs_ref,
        ),
        None,
    )


KEPT = (
    ("mixed_low", 1, 0),
    ("packed", 3, 0),
    ("probs", 0, 0),
    ("attended", 1, 0),
    ("first_norm", 1, 1),
    ("first_scale", -1, 1),
    ("first_low", 1, 0),
    ("slope", 4, 0),
    ("act", 4, 0),
    ("second_norm", 1, 1),
    ("second_scale", -1, 1),
)


def kept_shapes(tokens, width, hidden):
    shapes = []
    for name, parts, wide in KEPT:
        dims = (tokens, hidden if parts == 4 else SLOT if parts < 0 else parts * width)
        if name == "probs":
            dims = (tokens * HEADS, SLOT)
        shapes.append((dims, f32 if wide else bf16))
    return shapes


def second_kernel(
    arrived_ref,
    cotangent_ref,
    lengths_ref,
    rows_ref,
    gains_ref,
    up_bias_ref,
    mixed_in_ref,
    bias_ref,
    input_ref,
    output_ref,
    up_ref,
    down_ref,
    result_ref,
    grad_in_ref,
    *rest,
):
    kept_list, rest = rest[: len(KEPT)], rest[len(KEPT) :]
    mixed_ref, sum_ref, first_ref, low_ref, gate_ref, grad_ref, grad_packed_ref = rest[:7]
    scores_ref, grads_ref = rest[7:]
    tokens, width = mixed_ref.shape
    keep = dict(zip([name for name, _, _ in KEPT], kept_list))
    first_section = lax.axis_index("section") == 0
    mixed_ref[...] = jnp.where(first_section, mixed_in_ref[...], arrived_ref[...].astype(f32))
    forward_body(
        (input_ref, output_ref, up_ref, down_ref),
        [lambda: None] * 4,
        lengths_ref,
        (rows_ref, gains_ref, up_bias_ref),
        bias_ref,
        (
            mixed_ref,
            keep["packed"],
            keep["attended"],
            sum_ref,
            first_ref,
            low_ref,
            keep["act"],
            result_ref,
            scores_ref,
            keep["probs"],
        ),
        keep,
    )
    gains = gains_ref[...].astype(f32)
    for r in range(0, tokens, STRIP):
        strip = slice(r, r + STRIP)
        grad = cotangent_ref[strip].astype(f32) * gains[1:2]
        grad_sum = norm_back(grad, keep["second_norm"][strip], keep["second_scale"][strip, :1])
        first_ref[strip] = grad_sum
        low_ref[strip] = grad_sum.astype(bf16)
    gate_body(low_ref, down_ref, keep["slope"], gate_ref)
    for c in range(0, width, 2 * SLOT):
        cols = slice(c, c + 2 * SLOT)
        sum_ref[:, cols] = first_ref[:, cols] + dot(gate_ref[...], up_ref[cols, :], NT)
    for r in range(0, tokens, STRIP):
        strip = slice(r, r + STRIP)
        grad = sum_ref[strip] * gains[0:1]
        grad_mid = norm_back(grad, keep["first_norm"][strip], keep["first_scale"][strip, :1])
        first_ref[strip] = grad_mid
        low_ref[strip] = grad_mid.astype(bf16)
    grad_ref[...] = dot(low_ref[...], output_ref[...], NT).astype(bf16)
    attention_back(
        keep["packed"], keep["probs"], grad_ref, grad_packed_ref, scores_ref, grads_ref
    )
    for c in range(0, width, 2 * SLOT):
        cols = slice(c, c + 2 * SLOT)
        grad_in = first_ref[:, cols] + dot(grad_packed_ref[...], input_ref[cols, :], NT)
        grad_in_ref[:, cols] = grad_in.astype(bf16)


def gate_body(grad_ref, down_ref, slope_ref, gate_ref):
    for c in range(0, gate_ref.shape[1], 2 * SLOT):
        cols = slice(c, c + 2 * SLOT)
        value = dot(grad_ref[...], down_ref[cols, :], NT) * slope_ref[:, cols].astype(f32)
        gate_ref[:, cols] = value.astype(bf16)


def store_shares(value, row, column, outs, cuts, share):
    rows, columns = value.shape
    value = value.astype(bf16)
    if not cuts:
        outs[0][row : row + rows, column : column + columns] = value
        return
    even = lax.axis_index("dp") % 2 == 0
    for pair in range(row // (2 * share), (row + rows) // (2 * share)):
        top = 2 * pair * share - row
        for i, (start, count, left, width) in enumerate(cuts):
            from_column, to_column = max(column, left), min(column + columns, left + width)
            if from_column >= to_column:
                continue
            cols = slice(from_column - column, to_column - column)
            first = value[top + start : top + start + count, cols]
            second = value[top + share + start : top + share + start + count, cols]
            cols = slice(from_column - left, to_column - left)
            at = pair % 2 * 4 + pair // 2
            outs[2 * i][at, :, cols] = jnp.where(even, second, first)
            outs[2 * i + 1][at, :, cols] = jnp.where(even, first, second)


def column_sum(value):
    return jnp.sum(value, axis=0, keepdims=True)


def feed_kernel(
    cotangent_ref, arrived_ref, gains_ref, normed_ref, scale_ref, act_ref, *rest, outs, cuts, share
):
    shares_out, (grad_sum_ref, low_ref, small_ref) = rest[:outs], rest[outs:]
    tokens = low_ref.shape[0]
    hidden = act_ref.shape[1]
    gains = gains_ref[...].astype(f32)
    last = lax.axis_index("section") == lax.axis_size("section") - 1
    sums = [0.0, 0.0, 0.0]
    for r in range(0, tokens, STRIP):
        strip = slice(r, r + STRIP)
        grad_out = jnp.where(
            last, cotangent_ref[strip].astype(f32), arrived_ref[strip].astype(f32)
        )
        normed = normed_ref[strip]
        grad_sum = norm_back(grad_out * gains[1:2], normed, scale_ref[strip, :1])
        low = grad_sum.astype(bf16)
        grad_sum_ref[strip] = grad_sum
        low_ref[strip] = low
        sums[0] = sums[0] + column_sum(low.astype(f32))
        sums[1] = sums[1] + column_sum(grad_out)
        sums[2] = sums[2] + column_sum(grad_out * normed)
    step = 3 * SLOT
    for r in range(0, hidden, step):
        value = dot(act_ref[:, r : r + step], low_ref[...], TN)
        store_shares(value, r, 0, shares_out, cuts, share)
    for i, value in enumerate(sums):
        small_ref[i : i + 1, :] = value


def gate_kernel(low_ref, slope_ref, first_low_ref, down_ref, after, *rest, outs, cuts, share):
    shares_out, (gate_ref, small_ref) = rest[:outs], rest[outs:]
    gate_body(low_ref, down_ref, slope_ref, gate_ref)
    width, hidden = first_low_ref.shape[1], gate_ref.shape[1]
    step = 3 * SLOT
    for r in range(0, width, step):
        left = first_low_ref[:, r : r + step]
        for c in range(0, hidden, width):
            value = dot(left, gate_ref[:, c : c + width], TN)
            store_shares(value, r, c, shares_out, cuts, share)
    for c in range(0, hidden, width):
        cols = slice(c, c + width)
        small_ref[:, cols] = column_sum(gate_ref[:, cols].astype(f32))


def backwards(every):
    shape = (2 * SLOT, 2 * SLOT)
    left, right = iota(shape, 0), iota(shape, 1)
    ends = jnp.where(left < SLOT, SLOT - 1, jnp.where(left < SLOT + B2D, 3 * SLOT - B2D - 1, 0))
    ends = jnp.where(left >= SLOT + B2D, 4 * SLOT - B2D - 1, ends)
    return dot(every, hot(left + right == ends)).astype(bf16)


def table_rows(sums):
    blank = jnp.zeros((SLOT, SLOT), f32)
    near = jnp.concatenate([sums[:SLOT, :SLOT], blank], axis=1)
    near = pltpu.roll(near, 0, 1, stride=1, stride_axis=0)
    lane = iota((B2D, SLOT), 1)
    across = jnp.where(lane < B2D, sums[SLOT : SLOT + B2D, SLOT:], 0.0)
    across = pltpu.roll(across, 0, 1, stride=1, stride_axis=0)
    down = jnp.where(lane >= B2D, sums[SLOT + B2D :, SLOT:], 0.0)
    down = pltpu.roll(down, B2D, 1, stride=1, stride_axis=0)
    return jnp.concatenate([column_sum(near), column_sum(across), column_sum(down)], axis=1)


def chain_kernel(
    grad_sum_ref,
    gate_ref,
    normed_ref,
    scale_ref,
    packed_ref,
    probs_ref,
    order_ref,
    column_ref,
    row_ref,
    gains_ref,
    up_ref,
    output_ref,
    after,
    mid_ref,
    low_ref,
    grad_packed_ref,
    small_ref,
    table_ref,
    sum_ref,
    grad_ref,
    reach_ref,
    scores_ref,
    grads_ref,
):
    tokens, width = sum_ref.shape
    pages = tokens // SLOT
    gains = gains_ref[...].astype(f32)
    for c in range(0, width, 2 * SLOT):
        cols = slice(c, c + 2 * SLOT)
        sum_ref[:, cols] = grad_sum_ref[:, cols] + dot(gate_ref[...], up_ref[cols, :], NT)
    first_sum = gain_sum = branch_sum = 0.0
    for r in range(0, tokens, STRIP):
        strip = slice(r, r + STRIP)
        grad_first, normed = sum_ref[strip], normed_ref[strip]
        grad_mid = norm_back(grad_first * gains[0:1], normed, scale_ref[strip, :1])
        low = grad_mid.astype(bf16)
        mid_ref[strip] = grad_mid
        low_ref[strip] = low
        first_sum = first_sum + column_sum(grad_first)
        gain_sum = gain_sum + column_sum(grad_first * normed)
        branch_sum = branch_sum + column_sum(low.astype(f32))
    grad_ref[...] = dot(low_ref[...], output_ref[...], NT).astype(bf16)
    hots = [
        page_hot(order_ref[p : p + 1, :], column_ref[p : p + 1, :], row_ref[p : p + 1, :])
        for p in range(pages)
    ]
    every = backwards(jnp.concatenate(hots, axis=0))
    reach_ref[...] = jnp.zeros_like(reach_ref)
    attention_back(packed_ref, probs_ref, grad_ref, grad_packed_ref, scores_ref, grads_ref)
    for head in range(HEADS):
        along = []
        for p in range(pages):
            top = (p * HEADS + head) * SLOT
            along.append(dot(grads_ref[top : top + SLOT, :], hots[p]).astype(bf16))
        sums = dot(every, jnp.concatenate(along, axis=0), TN)
        reach_ref[head : head + 1, :] = table_rows(sums)
    for i, value in enumerate((first_sum, gain_sum, branch_sum)):
        small_ref[i : i + 1, :] = value
    table_ref[...] = dot(
        bucket_places().astype(f32), reach_ref[...], NT, precision=lax.Precision.HIGHEST
    )


def last_kernel(
    attended_ref,
    low_ref,
    mixed_low_ref,
    grad_packed_ref,
    block_ref,
    after,
    *shares_out,
    outs,
    cuts,
    share,
):
    width = low_ref.shape[1]
    step = 3 * SLOT
    for r in range(0, width, step):
        rows = slice(r, r + step)
        value = dot(attended_ref[:, rows], low_ref[...], TN)
        store_shares(value, r, 0, shares_out, cuts, share)
        for c in range(0, 3 * width, width):
            value = dot(mixed_low_ref[:, rows], grad_packed_ref[:, c : c + width], TN)
            store_shares(value, r, width + c, shares_out, cuts, share)
        if cuts:
            store_shares(block_ref[rows], r, 4 * width, shares_out, cuts, share)


def input_kernel(
    mid_ref,
    grad_packed_ref,
    tokens_ref,
    small_down_ref,
    small_up_ref,
    small_chain_ref,
    table_ref,
    lengths_ref,
    order_ref,
    region_ref,
    taps_ref,
    input_ref,
    after,
    grad_in_ref,
    small_ref,
    block_ref,
    sum_ref,
    *,
    share,
):
    tokens, width = sum_ref.shape
    pages = tokens // SLOT
    conv_on = (lax.axis_index("section") == 0).astype(f32)
    taps = taps_ref[...].astype(f32) * conv_on
    for c in range(0, width, 2 * SLOT):
        cols = slice(c, c + 2 * SLOT)
        sum_ref[:, cols] = mid_ref[:, cols] + dot(grad_packed_ref[...], input_ref[cols, :], NT)
    tap_sums = [0.0] * TAPS
    mixed_sum = 0.0
    for p in range(pages):
        here = slice(p * SLOT, (p + 1) * SLOT)
        order = order_ref[p : p + 1, :]
        rank_hot = rank_hot_of(order)
        masks = tap_columns(order, region_ref[p : p + 1, :], lengths_ref[p])
        ordered = dot(rank_hot, tokens_ref[here], TN)
        grad_mixed = sum_ref[here]
        grad_order = place_rows(rank_hot, grad_mixed, TN)
        source = jnp.zeros_like(ordered)
        for j in range(TAPS):
            masked = grad_order * masks[:, j : j + 1]
            tap_sums[j] = tap_sums[j] + column_sum(masked * shifted(ordered, j - REACH))
            source = source + shifted(taps[j : j + 1] * masked, REACH - j)
        grad_in_ref[here] = grad_mixed + place_rows(rank_hot, source, NN)
        mixed_sum = mixed_sum + column_sum(grad_mixed)
    down, chain = small_down_ref[...], small_chain_ref[...]
    rows = [
        column_sum(grad_packed_ref[:, :width].astype(f32)),
        column_sum(grad_packed_ref[:, 2 * width :].astype(f32)),
        chain[2:3],
        chain[0:1],
        down[0:1],
        down[1:2],
        conv_on * mixed_sum,
        chain[1:2],
        down[2:3],
    ]
    for i, value in enumerate(rows + [conv_on * value for value in tap_sums]):
        small_ref[i : i + 1, :] = value
    if share:
        small_block(small_ref, small_up_ref, table_ref, block_ref, share)


SMALL_ROWS = 16


def small_block(small_ref, up_ref, table_ref, block_ref, share):
    width = small_ref.shape[1]
    shares = block_ref.shape[0] // share
    part = width // shares
    up_part = up_ref.shape[1] // shares
    buckets = (B1D + 2 * B2D) // shares
    block_ref[...] = jnp.zeros_like(block_ref)
    small, up = small_ref[...], jnp.broadcast_to(up_ref[...], (8, up_ref.shape[1]))
    for s in range(shares):
        top = s * share
        shift = (width - s * part) % width
        here = pltpu.roll(small, shift, 1) if shift else small
        block_ref[top : top + SMALL_ROWS, :] = here[:, :SLOT]
        shift = (up.shape[1] - s * up_part) % up.shape[1]
        here = pltpu.roll(up, shift, 1) if shift else up
        top += SMALL_ROWS
        block_ref[top : top + 1, :] = here[:1, :SLOT]
        block_ref[top + 1 : top + 2, :] = here[:1, SLOT : 2 * SLOT]
        top += 2
        block_ref[top : top + buckets, :] = table_ref[s * buckets : (s + 1) * buckets, :]


def place():
    index = lax.axis_index("dp")
    return index // 4, index // 2 % 2


def added(out_ref, out_at, parts, window=None):
    rows = out_ref.shape[-2]
    for r in range(0, rows, 16):
        strip = slice(r, r + 16)
        total = 0.0
        for ref, at, windowed in parts:
            if windowed:
                row, _, column, columns = window
                value = ref[at, row + r : row + r + 16, column : column + columns]
            else:
                value = ref[at, strip]
            total = total + value.astype(f32)
        if out_at is None:
            out_ref[strip] = total.astype(bf16)
        else:
            out_ref[out_at, strip] = total.astype(bf16)


def fetched(recv_hbm, first, window, scratch, sems):
    row, rows, column, columns = window
    copies = []
    for k in range(4):
        source = recv_hbm.at[first + k, pl.ds(row, rows), pl.ds(column, columns)]
        copies.append(pltpu.make_async_copy(source, scratch.at[k], sems.at[k]))
        copies[-1].start()
    return copies


def leave_kernel(mine_ref, recv_ref, *rest, window, fetch):
    first = 4 * (1 - place()[1])
    if fetch:
        out_ref, scratch, sems = rest[-3:]
        copies = fetched(recv_ref, first, window, scratch, sems)
    else:
        out_ref = rest[-1]
    for k in range(4):
        other = (recv_ref, first + k, True)
        if fetch:
            copies[k].wait()
            other = (scratch, k, False)
        added(out_ref, k, ((mine_ref, first + k, True), other), window)


def near_kernel(mine_ref, recv_ref, y_ref, after, leave_ref, keep_ref, *rest, window, fetch):
    z, y = place()
    if fetch:
        scratch, sems = rest
        for copy in fetched(recv_ref, 4 * y, window, scratch, sems):
            copy.wait()
    for out_ref, parity in ((leave_ref, 1 - z % 2), (keep_ref, z % 2)):
        for k in range(2):
            block = 2 * k + parity
            at = 4 * y + block
            other = (scratch, block, False) if fetch else (recv_ref, at, True)
            added(out_ref, k, ((mine_ref, at, True), other, (y_ref, block, False)), window)


def far_kernel(keep_ref, recv_ref, *rest):
    leave_ref, own_ref = rest[-2:]
    high = place()[0] // 2
    for out_ref, k in ((leave_ref, 1 - high), (own_ref, high)):
        added(out_ref, None, ((keep_ref, k, False), (recv_ref, k, False)))


def near_first_kernel(mine_ref, recv_ref, after, leave_ref, keep_ref):
    z, _ = place()
    for out_ref, parity in ((leave_ref, 1 - z % 2), (keep_ref, z % 2)):
        for k in range(4):
            at = 2 * k + parity
            added(out_ref, k, ((mine_ref, at, False), (recv_ref, at, False)))


def far_first_kernel(keep_ref, recv_ref, after, leave_ref, stay_ref):
    high = place()[0] // 2
    for out_ref, k in ((leave_ref, 1 - high), (stay_ref, high)):
        for y in range(2):
            at = 2 * y + k
            added(out_ref, y, ((keep_ref, at, False), (recv_ref, at, False)))


def cross_kernel(keep_ref, recv_ref, after, leave_ref, own_ref):
    y = place()[1]
    for out_ref, at in ((leave_ref, 1 - y), (own_ref, y)):
        added(out_ref, None, ((keep_ref, at, False), (recv_ref, at, False)))


def both(parts):
    return parts[0][...].astype(f32) + parts[1][...].astype(f32)


def down_end(*refs):
    out_ref, token_ref = refs[-2:]
    token_ref[...] = jnp.zeros_like(token_ref)
    rows = refs[0].shape[0]
    out_ref[:rows] = both(refs[:2])
    out_ref[rows:] = both(refs[2:4])


def up_end(*refs):
    out_ref, token_ref = refs[-2:]
    token_ref[...] = jnp.zeros_like(token_ref)
    columns = refs[0].shape[1]
    out_ref[:, :columns] = both(refs[:2])
    out_ref[:, columns:] = both(refs[2:4])


def last_end(*refs):
    sum_ref, block_ref = refs[-2:]
    input_ref, output_ref, bias_ref, gain_ref, tap_ref, up_ref, table_ref = refs[-9:-2]
    column = 0
    for i in range(0, len(refs) - 10, 2):
        columns = refs[i].shape[1]
        sum_ref[:, column : column + columns] = both(refs[i : i + 2])
        column += columns
    width, share = output_ref.shape[1], output_ref.shape[0]
    output_ref[...] = sum_ref[:, :width]
    input_ref[...] = sum_ref[:, width : 4 * width]
    block_ref[...] = sum_ref[:, 4 * width :]
    for i in range(7):
        bias_ref[i] = block_ref[i : i + 1, :share]
        tap_ref[i] = block_ref[9 + i : 10 + i, :share]
    gain_ref[...] = block_ref[7:9, :share]
    rest = up_ref.shape[1] - SLOT
    up_ref[:, :SLOT] = block_ref[SMALL_ROWS : SMALL_ROWS + 1, :]
    up_ref[:, SLOT:] = block_ref[SMALL_ROWS + 1 : SMALL_ROWS + 2, :rest]
    for i in range(table_ref.shape[1] // HEADS):
        at = SMALL_ROWS + 2 + i
        table_ref[:, i * HEADS : (i + 1) * HEADS] = block_ref[at : at + 1, :HEADS]


def kernel_call(body, name, ins, outs, scratch, flops=0, vmem=10):
    return pl.pallas_call(
        body,
        name=name,
        out_shape=[shape for shape, _ in outs],
        in_specs=[spec for _, spec in ins],
        out_specs=[spec for _, spec in outs],
        scratch_shapes=scratch,
        compiler_params=pltpu.CompilerParams(vmem_limit_bytes=vmem << 20),
        cost_estimate=pl.CostEstimate(flops=flops, bytes_accessed=0, transcendentals=0),
    )(*[value for value, _ in ins])


def near_by(value):
    return pltpu.with_memory_space_constraint(value, pltpu.VMEM)


def in_hbm(value):
    return pltpu.with_memory_space_constraint(value, pltpu.HBM)


def near_shape(dims, kind=bf16):
    return pltpu.VMEM(dims, kind)


class Summing:
    def __init__(self):
        self.pairs, self.windows, self.crossed, self.kept, self.ends = {}, {}, {}, {}, {}
        self.fetch = {}

    @staticmethod
    def _swap(value, bits):
        return near_by(lax.ppermute(value, "dp", [(i, i ^ bits) for i in range(16)]))

    @staticmethod
    def _add(body, name, ins, after, outs, cost=0, earlier=(), scratch=(), fetch=False):
        specs = [IN_VMEM] * len(ins)
        if fetch:
            specs[1] = IN_PLACE
        return kernel_call(
            body,
            name,
            [(near_by(value), spec) for value, spec in zip(ins, specs)]
            + [(value, IN_PLACE) for value in (after, *earlier)],
            [(near_shape(dims), IN_VMEM) for dims in outs],
            list(scratch),
            cost,
            4,
        )

    def core(self, theirs, mine, fetch=False, **windows):
        recv = self._swap(theirs, 1)
        for name, window in windows.items():
            self.pairs[name], self.windows[name] = [mine, recv], window
            self.fetch[name] = fetch

    def _fetching(self, name, body):
        window, fetch = self.windows[name], self.fetch[name]
        dims = (4, window[1], window[3])
        scratch = [pltpu.VMEM(dims, bf16), pltpu.SemaphoreType.DMA((4,))] if fetch else []
        body = functools.partial(body, window=window, fetch=fetch)
        return body, dict(scratch=scratch, fetch=fetch), dims

    def leave(self, name, after, earlier=None):
        body, more, dims = self._fetching(name, leave_kernel)
        earlier = [self.crossed[earlier]] if earlier else []
        (out,) = self._add(body, "leave", self.pairs[name], after, [dims], 0, earlier, **more)
        self.crossed[name] = self._swap(out, 2)
        return out

    def near(self, name, after):
        body, more, dims = self._fetching(name, near_kernel)
        dims = (2,) + dims[1:]
        ins = self.pairs[name] + [self.crossed[name]]
        out, keep = self._add(body, "near", ins, after, [dims, dims], COST, **more)
        self.kept[name] = [keep, self._swap(out, 4)]
        return out

    def far(self, name, after, earlier=()):
        ins = self.kept[name]
        dims = ins[0].shape[1:]
        earlier = [self.ends[other][1] for other in earlier]
        out, own = self._add(far_kernel, "far", ins, after, [dims, dims], COST, earlier)
        self.ends[name] = [own, self._swap(out, 8)]
        return out

    def near_first(self, name, after):
        ins = self.pairs[name]
        dims = (4,) + ins[0].shape[1:]
        out, keep = self._add(near_first_kernel, "near_first", ins, after, [dims, dims], COST)
        self.kept[name] = [keep, self._swap(out, 4)]
        return out

    def far_first(self, name, after):
        ins = self.kept[name]
        dims = (2,) + ins[0].shape[1:]
        out, stay = self._add(far_first_kernel, "far_first", ins, after, [dims, dims], COST)
        self.kept[name] = [stay, self._swap(out, 8)]
        return out

    def cross(self, name, after):
        ins = self.kept[name]
        dims = ins[0].shape[1:]
        out, own = self._add(cross_kernel, "cross", ins, after, [dims, dims], COST)
        self.ends[name] = [own, self._swap(out, 2)]
        return out


def local(
    tokens,
    cotangent,
    page_lengths,
    cut_order,
    cut_region,
    cell_column,
    cell_row,
    input_proj,
    output_proj,
    up_proj,
    down_proj,
    up_bias,
    bias_rows,
    gain_rows,
    conv_taps,
    bias_table,
):
    section_count = lax.axis_size("section")
    dp_count = lax.axis_size("dp")
    by_hops = dp_count == 16
    pages, _, width = tokens.shape
    hidden = up_proj.shape[2]
    count = pages * SLOT
    weights = [w[0] for w in (input_proj, output_proj, up_proj, down_proj)]
    rows, gains, taps = bias_rows[0], gain_rows[0], conv_taps[0]
    tokens, cotangent = tokens.reshape(count, width), cotangent.reshape(count, width)

    def shape(dims, kind):
        return jax.ShapeDtypeStruct(dims, kind)

    def inside(*values):
        return [(v, IN_VMEM) for v in values]

    def in_place(*values):
        return [(v, IN_PLACE) for v in values]

    def scalars(*values):
        return [(v, IN_SMEM) for v in values]

    wide, low = shape((count, width), f32), shape((count, width), bf16)
    wide_scratch = pltpu.VMEM((count, width), f32)
    low_scratch = pltpu.VMEM((count, width), bf16)
    packed_scratch = pltpu.VMEM((count, 3 * width), bf16)
    hidden_scratch = pltpu.VMEM((count, hidden), bf16)
    bias_dims = (pages * HEADS * SLOT, SLOT)

    def sems(number):
        return pltpu.SemaphoreType.DMA((number,))

    first_ins = [tokens, cut_order, cut_region, cell_column, cell_row, rows, gains, up_bias]
    first_ins += [taps, bias_table]
    result, mixed, bias, *near_weights = kernel_call(
        first_kernel,
        "first",
        scalars(in_hbm(page_lengths)) + in_place(*map(in_hbm, first_ins + weights)),
        inside(low, near_shape((count, width), f32), near_shape(bias_dims, f32))
        + inside(*[near_shape(w.shape) for w in weights]),
        [
            packed_scratch,
            low_scratch,
            wide_scratch,
            wide_scratch,
            low_scratch,
            hidden_scratch,
            pltpu.VMEM(bias_dims, f32),
            pltpu.VMEM(bias_dims, bf16),
            pltpu.VMEM((HEADS, 2 * SLOT, 2 * SLOT), bf16),
            pltpu.VMEM((HEADS, count, 2 * SLOT), bf16),
            *[pltpu.VMEM(v.shape, v.dtype) for v in first_ins],
            sems(len(first_ins) + len(weights)),
        ],
    )
    input_w, output_w, up_w, down_w = near_weights = list(map(near_by, near_weights))
    arrived = near_by(
        lax.ppermute(result, "section", [(i, i + 1) for i in range(section_count - 1)])
    )
    shapes = kept_shapes(count, width, hidden)
    layer_out, leaving, *kept_list = kernel_call(
        second_kernel,
        "second",
        inside(arrived, cotangent)
        + scalars(page_lengths)
        + inside(rows, gains, up_bias)
        + inside(*map(near_by, (mixed, bias, *near_weights))),
        inside(low, near_shape((count, width)), *[near_shape(*s) for s in shapes]),
        [
            wide_scratch,
            wide_scratch,
            wide_scratch,
            low_scratch,
            hidden_scratch,
            low_scratch,
            packed_scratch,
            pltpu.VMEM(bias_dims, f32),
            pltpu.VMEM(bias_dims, bf16),
        ],
    )
    kept = dict(zip([name for name, _, _ in KEPT], map(near_by, kept_list)))
    arrived_grad = near_by(
        lax.ppermute(leaving, "section", [(i + 1, i) for i in range(section_count - 1)])
    )
    part = width // dp_count

    def cut(dims, cuts):
        share = dims[0] // dp_count
        if not by_hops:
            outs, cuts = inside(shape(dims, bf16)), ()
        else:
            halves_out = [near_shape((dp_count // 2, c[1], c[3])) for c in cuts for _ in range(2)]
            outs = inside(*halves_out)
        return outs, dict(outs=len(outs), cuts=cuts, share=share)

    half = hidden // dp_count // 2
    down_outs, down_cut = cut((hidden, width), ((0, half, 0, width), (half, half, 0, width)))
    up_outs, up_cut = cut((width, hidden), ((0, part, 0, hidden),))
    *down_parts, grad_sum, grad_low, small_down = kernel_call(
        functools.partial(feed_kernel, **down_cut),
        "feed",
        inside(cotangent, arrived_grad, gains)
        + inside(kept["second_norm"], kept["second_scale"], kept["act"]),
        down_outs + inside(wide, low, shape((8, width), f32)),
        [],
    )
    *up_parts, gate, small_up = kernel_call(
        functools.partial(gate_kernel, **up_cut),
        "gate",
        inside(grad_low, kept["slope"], kept["first_low"], down_w) + in_place(small_down),
        up_outs + inside(shape((count, hidden), bf16), shape((1, hidden), f32)),
        [],
    )
    summing = Summing()
    after = small_up
    if by_hops:
        piece = (0, half, 0, width)
        side = hidden // 2
        summing.core(*down_parts[:2], d1=piece)
        summing.core(*down_parts[2:], d2=piece)
        summing.core(*up_parts, u1=(0, part, 0, side), u2=(0, part, side, side))
        after = summing.leave("d1", after)
        after = summing.near_first("d2", after)
        after = summing.leave("u1", after)
    grad_mid, grad_branch, grad_packed, small_chain, table = kernel_call(
        chain_kernel,
        "chain",
        inside(grad_sum, gate, kept["first_norm"], kept["first_scale"], kept["packed"])
        + inside(kept["probs"], cut_order, cell_column, cell_row, gains)
        + inside(up_w, output_w)
        + in_place(after),
        inside(wide, low, shape((count, 3 * width), bf16), shape((8, width), f32))
        + inside(shape((B1D + 2 * B2D, SLOT), f32)),
        [
            wide_scratch,
            low_scratch,
            pltpu.VMEM((SLOT, 4 * SLOT), f32),
            pltpu.VMEM(bias_dims, f32),
            pltpu.VMEM(bias_dims, bf16),
        ],
    )
    after = grad_mid
    if by_hops:
        after = summing.near("d1", after)
        after = summing.far_first("d2", after)
        after = summing.leave("u2", after)
    grad_in, small_rows, block = kernel_call(
        functools.partial(input_kernel, share=part if by_hops else 0),
        "input",
        inside(grad_mid, grad_packed, tokens, small_down, small_up, small_chain, table)
        + scalars(page_lengths)
        + inside(cut_order, cut_region, taps, input_w)
        + in_place(after),
        inside(wide, shape((16, width), f32), near_shape((width, SLOT), f32)),
        [wide_scratch],
    )
    after = block
    columns = 4 * width + (SLOT if by_hops else 0)
    last_outs, last_cut = cut((width, columns), ((0, part, 0, columns),))
    last_parts = kernel_call(
        functools.partial(last_kernel, **last_cut),
        "last",
        inside(kept["attended"], grad_branch, kept["mixed_low"], grad_packed, near_by(block))
        + in_place(after),
        last_outs,
        [],
    )
    after = last_parts[0]
    if by_hops:
        token = near_shape((8, SLOT), f32)
        windows, column = {}, 0
        for name, end in (("a1", 2 * width), ("a2", 3 * width + 2 * SLOT), ("a3", columns)):
            windows[name], column = (0, part, column, end - column), end
        summing.core(*last_parts, fetch=True, **windows)
        ends = summing.ends
        after = summing.near("u1", after)
        after = summing.far("d1", after)
        after = summing.cross("d2", after)
        after = summing.leave("a1", after, "u2")
        after = summing.near("u2", after)
        after = summing.far("u1", after, ["d1"])
        after = summing.leave("a2", after)
        down_grad, after = kernel_call(
            down_end,
            "down_end",
            inside(*map(near_by, ends["d1"] + ends["d2"])) + in_place(after),
            inside(shape((hidden // dp_count, width), f32), token),
            [],
            vmem=4,
        )
        after = summing.far("u2", after)
        after = summing.near("a1", after)
        after = summing.leave("a3", after)
        after = summing.near("a2", after)
        after = summing.far("a1", after)
        up_grad, after = kernel_call(
            up_end,
            "up_end",
            inside(*map(near_by, ends["u1"] + ends["u2"])) + in_place(after),
            inside(shape((part, hidden), f32), token),
            [],
            vmem=4,
        )
        after = summing.near("a3", after)
        after = summing.far("a2", after)
        after = summing.far("a3", after)
        input_grad, output_grad, bias_grad, gain_grad, tap_grad, up_bias_grad, table_grad = (
            kernel_call(
                last_end,
                "last_end",
                inside(*map(near_by, ends["a1"] + ends["a2"] + ends["a3"])) + in_place(after),
                inside(
                    shape((part, 3 * width), f32),
                    shape((part, width), f32),
                    shape((7, 1, part), f32),
                    shape((2, part), f32),
                    shape((TAPS, 1, part), f32),
                    shape((1, hidden // dp_count), f32),
                    shape((1, table.shape[0] * HEADS // dp_count), f32),
                ),
                [pltpu.VMEM((part, columns), f32), pltpu.VMEM((part, SLOT), f32)],
                vmem=4,
            )
        )
    else:

        def scattered(value):
            return lax.psum_scatter(value, "dp", scatter_dimension=0, tiled=True).astype(f32)

        down_grad, up_grad, last_grad = (
            scattered(parts[0]) for parts in (down_parts, up_parts, last_parts)
        )
        input_grad, output_grad = last_grad[:, width:], last_grad[:, :width]
        small = [
            small_rows.reshape(16, dp_count, part).transpose(1, 0, 2).reshape(dp_count, -1),
            small_up.reshape(dp_count, -1),
            table[:, :HEADS].reshape(dp_count, -1),
        ]
        small = jnp.concatenate(small, axis=1)
        used = small.shape[1]
        small = jnp.pad(small, ((0, 0), (0, -used % SLOT))).reshape(-1, SLOT)
        small = scattered(small).reshape(-1)
        vectors = small[: 16 * part].reshape(16, part)
        bias_grad, tap_grad = vectors[:7, None], vectors[9:, None]
        gain_grad = vectors[7:9]
        at = 16 * part + hidden // dp_count
        up_bias_grad, table_grad = small[None, 16 * part : at], small[None, at:used]
    return (
        layer_out.reshape(1, pages, SLOT, width),
        grad_in.reshape(1, pages, SLOT, width),
        input_grad[None],
        output_grad[None],
        up_grad[None],
        down_grad[None],
        up_bias_grad,
        bias_grad.transpose(1, 0, 2),
        gain_grad[None],
        tap_grad.transpose(1, 0, 2),
        table_grad,
    )


def solution(mesh):
    by_section = [P("section", None, None)] * 4
    placed = (
        P("dp", None, None),
        P("dp", None, None),
        P("dp"),
        P("dp", None),
        P("dp", None),
        P("dp", None),
        P("dp", None),
        *by_section,
        P("section", None),
        P("section", None, None),
        P("section", None, None),
        P("section", None, None),
        P("section", None),
    )
    return jax.shard_map(
        local,
        mesh=mesh,
        in_specs=placed,
        out_specs=(
            P("section", "dp", None, None),
            P("section", "dp", None, None),
            P("section", "dp", None),
            P("section", "dp", None),
            P("section", "dp", None),
            P("section", "dp", None),
            P("section", "dp"),
            P("section", None, "dp"),
            P("section", None, "dp"),
            P("section", None, "dp"),
            P("section", "dp"),
        ),
        check_vma=False,
    )
```

```python
import functools

import jax
import jax.numpy as jnp
from jax import lax
from jax.experimental import pallas as pl
from jax.experimental.pallas import tpu as pltpu
from jax.sharding import PartitionSpec as P

HEADS = 12
HEAD = 64
B1D = 32
B2D = 64
SLOT = 128
PAIRS = HEADS // 2
TAPS = 7
REACH = 3
EPSILON = 1e-05
COST = 20_000_000_000
MASKED = -1000000000.0
STRIP = 64

f32 = jnp.float32
bf16 = jnp.bfloat16
NN = ((1,), (0,))
NT = ((1,), (1,))
TN = ((0,), (0,))

IN_VMEM = pl.BlockSpec(memory_space=pltpu.VMEM)
IN_SMEM = pl.BlockSpec(memory_space=pltpu.SMEM)
IN_PLACE = pl.BlockSpec(memory_space=pl.ANY)


def dot(left, right, dims=NN, precision=None):
    return lax.dot_general(
        left, right, (dims, ((), ())), precision=precision, preferred_element_type=f32
    )


def iota(shape, axis):
    return lax.broadcasted_iota(jnp.int32, shape, axis)


def hot(mask):
    return mask.astype(f32).astype(bf16)


def identity():
    return hot(iota((SLOT, SLOT), 0) == iota((SLOT, SLOT), 1))


def rank_hot_of(order):
    return hot(order == iota((SLOT, SLOT), 0))


def page_hot(order, column, row):
    cells = iota((SLOT, SLOT), 0)
    wanted = jnp.where(cells < B2D, column, row + B2D)
    cell_hot = dot(identity(), hot(wanted == cells), NT).astype(bf16)
    return jnp.concatenate([rank_hot_of(order), cell_hot], axis=1)


def tap_columns(order, region, length):
    shape = (8, SLOT)
    order, region = jnp.broadcast_to(order, shape), jnp.broadcast_to(region, shape)
    live = (order < length).astype(jnp.int32)
    lane, tap = iota(shape, 1), iota(shape, 0)
    masks = jnp.zeros(shape, f32)
    for j in range(TAPS):
        offset = j - REACH
        shift = (-offset) % SLOT
        region_j = pltpu.roll(region, shift, 1) if shift else region
        live_j = pltpu.roll(live, shift, 1) if shift else live
        joined = (lane + offset >= 0) & (lane + offset < SLOT) & (region_j == region) & (live_j > 0)
        masks = jnp.where((tap == j) & joined, 1.0, masks)
    return dot(identity(), masks.astype(bf16), NT)


def shifted(rows, offset):
    shift = (-offset) % SLOT
    return pltpu.roll(rows, shift, 0) if shift else rows


def place_rows(rank_hot, rows, dims):
    high = rows.astype(bf16)
    low = (rows - high.astype(f32)).astype(bf16)
    return dot(rank_hot, high, dims) + dot(rank_hot, low, dims)


def bucket_places():
    shape = (B1D + 2 * B2D, 4 * SLOT)
    bucket, lane = iota(shape, 0), iota(shape, 1)
    near = jnp.clip(lane - (SLOT - 1) + B1D // 2, 0, B1D - 1)
    column = B1D + jnp.clip(lane - 2 * SLOT - (B2D - 1) + B2D // 2, 0, B2D - 1)
    row = B1D + B2D + jnp.clip(lane - 3 * SLOT - (B2D - 1) + B2D // 2, 0, B2D - 1)
    wanted = jnp.where(lane < 2 * SLOT, near, jnp.where(lane < 3 * SLOT, column, row))
    return bucket == wanted


def halves(pair):
    lane = iota((1, SLOT), 1)
    first = hot(lane < HEAD)
    second = hot(lane >= HEAD)
    return jnp.concatenate([pair * first, pair * second], axis=0)


def side_by_side(stacked):
    return jnp.concatenate([stacked[:SLOT], stacked[SLOT:]], axis=1)


def normed_of(value):
    average = jnp.mean(value, axis=-1, keepdims=True)
    centered = value - average
    spread = jnp.mean(centered * centered, axis=-1, keepdims=True)
    inverse = lax.rsqrt(spread + EPSILON)
    return centered * inverse, inverse


def norm_back(grad, normed, inverse):
    first_mean = jnp.mean(grad, axis=-1, keepdims=True)
    second_mean = jnp.mean(grad * normed, axis=-1, keepdims=True)
    return inverse * (grad - first_mean - normed * second_mean)


def table_columns(table):
    buckets = table.shape[1] // HEADS
    bucket = iota((buckets, table.shape[1]), 0) * HEADS
    lane = iota((buckets, table.shape[1]), 1)
    own = hot((lane >= bucket) & (lane < bucket + HEADS))
    lane = iota((16, table.shape[1]), 1)
    times = ((lane.astype(f32) + 0.5) * (1.0 / HEADS)).astype(jnp.int32)
    head = hot(lane - HEADS * times == iota((16, table.shape[1]), 0))
    return dot(own * table, head, NT).astype(bf16)


def bias_body(order_ref, column_ref, row_ref, table_ref, bias_ref, grids_ref, hot_rows_ref):
    pages = order_ref.shape[0]
    hots = [
        page_hot(order_ref[p : p + 1, :], column_ref[p : p + 1, :], row_ref[p : p + 1, :])
        for p in range(pages)
    ]
    every = jnp.concatenate(hots, axis=0)
    reach = dot(table_columns(table_ref[...]), hot(bucket_places()), TN)
    lane = iota((B2D, SLOT), 1)
    for h in range(HEADS):
        row = reach[h : h + 1, :]
        near = jnp.broadcast_to(row[:, : 2 * SLOT], (SLOT, 2 * SLOT))
        near = pltpu.roll(near, SLOT + 1, 1, stride=1, stride_axis=0)[:, :SLOT]
        across = jnp.broadcast_to(row[:, 2 * SLOT : 3 * SLOT], (B2D, SLOT))
        across = pltpu.roll(across, B2D + 1, 1, stride=1, stride_axis=0)
        down = jnp.broadcast_to(row[:, 3 * SLOT :], (B2D, SLOT))
        down = pltpu.roll(down, 1, 1, stride=1, stride_axis=0)
        cells = jnp.concatenate(
            [jnp.where(lane < B2D, across, 0.0), jnp.where(lane >= B2D, down, 0.0)], axis=0
        )
        blank = jnp.zeros((SLOT, SLOT), bf16)
        grids_ref[h, :SLOT, :SLOT] = near.astype(bf16)
        grids_ref[h, :SLOT, SLOT:] = blank
        grids_ref[h, SLOT:, :SLOT] = blank
        grids_ref[h, SLOT:, SLOT:] = cells.astype(bf16)
    for h in range(HEADS):
        hot_rows_ref[h] = dot(every, grids_ref[h]).astype(bf16)
    for p in range(pages):
        for h in range(HEADS):
            at = (p * HEADS + h) * SLOT
            rows = hot_rows_ref[h, p * SLOT : (p + 1) * SLOT, :]
            bias_ref[at : at + SLOT, :] = dot(rows, hots[p], NT)


def forward_body(weights, waits, lengths_ref, vectors, bias_ref, work, keep):
    input_ref, output_ref, up_ref, down_ref = weights
    rows_ref, gains_ref, up_bias_ref = vectors
    mixed_ref, packed_ref, attended_ref, sum_ref, first_ref, low_ref, act_ref, result_ref = work[:8]
    scores_ref, probs_ref = work[8:]
    rows, gains = rows_ref[...].astype(f32), gains_ref[...].astype(f32)
    tokens, width = mixed_ref.shape
    hidden = act_ref.shape[1]
    low_ref[...] = mixed_ref[...].astype(bf16)
    if keep:
        keep["mixed_low"][...] = low_ref[...]
    waits[0]()
    for part, add in ((0, rows[0:1]), (1, None), (2, rows[1:2])):
        cols = slice(part * width, (part + 1) * width)
        value = dot(low_ref[...], input_ref[:, cols])
        packed_ref[:, cols] = (value if add is None else value + add).astype(bf16)
    places = [(p, pair) for p in range(tokens // SLOT) for pair in range(PAIRS)]
    for p, pair in places:
        here, at = slice(p * SLOT, (p + 1) * SLOT), pair * SLOT
        top = (p * HEADS + 2 * pair) * SLOT
        queries = halves(packed_ref[here, at : at + SLOT]) * (HEAD**-0.5)
        keys = packed_ref[here, width + at : width + at + SLOT]
        scores_ref[top : top + 2 * SLOT, :] = dot(queries, keys, NT)
    for p, pair in places:
        top = (p * HEADS + 2 * pair) * SLOT
        rows_here = slice(top, top + 2 * SLOT)
        live = iota((2 * SLOT, SLOT), 1) < lengths_ref[p]
        scores = jnp.where(live, scores_ref[rows_here, :] + bias_ref[rows_here, :], MASKED)
        expo = jnp.exp(scores - jnp.max(scores, axis=-1, keepdims=True))
        probs = expo * (1.0 / jnp.sum(expo, axis=-1, keepdims=True))
        probs_ref[rows_here, :] = probs.astype(bf16)
    for p, pair in places:
        here, at = slice(p * SLOT, (p + 1) * SLOT), pair * SLOT
        top = (p * HEADS + 2 * pair) * SLOT
        values = halves(packed_ref[here, 2 * width + at : 2 * width + at + SLOT])
        probs = side_by_side(probs_ref[top : top + 2 * SLOT, :])
        attended_ref[here, at : at + SLOT] = dot(probs, values).astype(bf16)
    waits[1]()
    sum_ref[...] = dot(attended_ref[...], output_ref[...])
    for r in range(0, tokens, STRIP):
        strip = slice(r, r + STRIP)
        normed, inverse = normed_of(mixed_ref[strip] + sum_ref[strip] + rows[2:3])
        first = normed * gains[0:1] + rows[3:4]
        first_ref[strip] = first
        low_ref[strip] = first.astype(bf16)
        if keep:
            keep["first_norm"][strip] = normed
            keep["first_scale"][strip] = jnp.broadcast_to(inverse, (STRIP, SLOT))
            keep["first_low"][strip] = first.astype(bf16)
    waits[2]()
    for c in range(0, hidden, 2 * SLOT):
        cols = slice(c, c + 2 * SLOT)
        gate = dot(low_ref[...], up_ref[:, cols]) + up_bias_ref[:, cols].astype(f32)
        below = 0.5 + 0.5 * lax.erf(gate * 0.7071067811865476)
        act_ref[:, cols] = (gate * below).astype(bf16)
        if keep:
            density = jnp.exp(-0.5 * gate * gate) * 0.3989422804014327
            keep["slope"][:, cols] = (below + gate * density).astype(bf16)
    waits[3]()
    sum_ref[...] = dot(act_ref[...], down_ref[...])
    for r in range(0, tokens, STRIP):
        strip = slice(r, r + STRIP)
        normed, inverse = normed_of(first_ref[strip] + sum_ref[strip] + rows[4:5])
        result_ref[strip] = (normed * gains[1:2] + rows[5:6]).astype(bf16)
        if keep:
            keep["second_norm"][strip] = normed
            keep["second_scale"][strip] = jnp.broadcast_to(inverse, (STRIP, SLOT))


def attention_back(packed_ref, probs_ref, grad_ref, grad_packed_ref, scores_ref, grads_ref):
    tokens, width = grad_ref.shape
    places = [(p, pair) for p in range(tokens // SLOT) for pair in range(PAIRS)]

    def rows_of(p, pair):
        top = (p * HEADS + 2 * pair) * SLOT
        return slice(top, top + 2 * SLOT)

    def part_of(ref, p, pair, part=0):
        at = part * width + pair * SLOT
        return ref[p * SLOT : (p + 1) * SLOT, at : at + SLOT]

    for p, pair in places:
        grad, values = halves(part_of(grad_ref, p, pair)), part_of(packed_ref, p, pair, 2)
        scores_ref[rows_of(p, pair), :] = dot(grad, values, NT)
    for p, pair in places:
        rows = rows_of(p, pair)
        probs, grad_probs = probs_ref[rows, :].astype(f32), scores_ref[rows, :]
        inner = jnp.sum(probs * grad_probs, axis=-1, keepdims=True)
        grads_ref[rows, :] = (probs * (grad_probs - inner)).astype(bf16)
    for p, pair in places:
        rows = rows_of(p, pair)
        queries = halves(part_of(packed_ref, p, pair)) * (HEAD**-0.5)
        keys = halves(part_of(packed_ref, p, pair, 1)) * (HEAD**-0.5)
        grad = halves(part_of(grad_ref, p, pair))
        for part, value in (
            (0, dot(side_by_side(grads_ref[rows, :]), keys)),
            (1, dot(grads_ref[rows, :], queries, TN)),
            (2, dot(probs_ref[rows, :], grad, TN)),
        ):
            at = part * width + pair * SLOT
            grad_packed_ref[p * SLOT : (p + 1) * SLOT, at : at + SLOT] = value.astype(bf16)


def first_kernel(lengths_ref, *rest):
    ins, weight_ins, rest = rest[:10], rest[10:14], rest[14:]
    result_ref, mixed_ref, bias_ref, *weights = rest[:7]
    packed_ref, attended_ref, sum_ref, first_ref, low_ref, act_ref = rest[7:13]
    scores_ref, probs_ref, grids_ref, hot_rows_ref = rest[13:17]
    held, sems = rest[17:27], rest[27]
    small = [pltpu.make_async_copy(a, b, sems.at[i]) for i, (a, b) in enumerate(zip(ins, held))]
    copies = [
        pltpu.make_async_copy(a, b, sems.at[len(small) + i])
        for i, (a, b) in enumerate(zip(weight_ins, weights))
    ]
    for copy in small:
        copy.start()
    copies[0].start()
    for copy in small:
        copy.wait()
    tokens_ref, order_ref, region_ref, column_ref, row_ref = held[:5]
    rows_ref, gains_ref, up_bias_ref, taps_ref, table_ref = held[5:]
    conv_on = (lax.axis_index("section") == 0).astype(f32)
    taps = taps_ref[...].astype(f32) * conv_on
    conv_bias = rows_ref[...].astype(f32)[6:7] * conv_on
    for p in range(order_ref.shape[0]):
        here = slice(p * SLOT, (p + 1) * SLOT)
        order = order_ref[p : p + 1, :]
        rank_hot = rank_hot_of(order)
        masks = tap_columns(order, region_ref[p : p + 1, :], lengths_ref[p])
        places = dot(identity(), rank_hot, NT)
        sources = [
            dot(rank_hot, (shifted(places, j - REACH) * masks[:, j : j + 1]).astype(bf16))
            for j in range(TAPS)
        ]
        moved = dot(jnp.concatenate(sources, axis=0).astype(bf16), tokens_ref[here])
        total = tokens_ref[here].astype(f32) + conv_bias
        for j in range(TAPS):
            total = total + taps[j : j + 1] * moved[j * SLOT : (j + 1) * SLOT]
        mixed_ref[here] = total
    copies[1].start()
    copies[2].start()
    bias_body(order_ref, column_ref, row_ref, table_ref, bias_ref, grids_ref, hot_rows_ref)

    def wait_input():
        copies[0].wait()
        copies[3].start()

    forward_body(
        weights,
        [wait_input] + [copy.wait for copy in copies[1:]],
        lengths_ref,
        (rows_ref, gains_ref, up_bias_ref),
        bias_ref,
        (
            mixed_ref,
            packed_ref,
            attended_ref,
            sum_ref,
            first_ref,
            low_ref,
            act_ref,
            result_ref,
            scores_ref,
            probs_ref,
        ),
        None,
    )


KEPT = (
    ("mixed_low", 1, 0),
    ("packed", 3, 0),
    ("probs", 0, 0),
    ("attended", 1, 0),
    ("first_norm", 1, 1),
    ("first_scale", -1, 1),
    ("first_low", 1, 0),
    ("slope", 4, 0),
    ("act", 4, 0),
    ("second_norm", 1, 1),
    ("second_scale", -1, 1),
)


def kept_shapes(tokens, width, hidden):
    shapes = []
    for name, parts, wide in KEPT:
        dims = (tokens, hidden if parts == 4 else SLOT if parts < 0 else parts * width)
        if name == "probs":
            dims = (tokens * HEADS, SLOT)
        shapes.append((dims, f32 if wide else bf16))
    return shapes


def second_kernel(
    arrived_ref,
    cotangent_ref,
    lengths_ref,
    rows_ref,
    gains_ref,
    up_bias_ref,
    mixed_in_ref,
    bias_ref,
    input_ref,
    output_ref,
    up_ref,
    down_ref,
    result_ref,
    grad_in_ref,
    *rest,
):
    kept_list, rest = rest[: len(KEPT)], rest[len(KEPT) :]
    mixed_ref, sum_ref, first_ref, low_ref, gate_ref, grad_ref, grad_packed_ref = rest[:7]
    scores_ref, grads_ref = rest[7:]
    tokens, width = mixed_ref.shape
    keep = dict(zip([name for name, _, _ in KEPT], kept_list))
    first_section = lax.axis_index("section") == 0
    mixed_ref[...] = jnp.where(first_section, mixed_in_ref[...], arrived_ref[...].astype(f32))
    forward_body(
        (input_ref, output_ref, up_ref, down_ref),
        [lambda: None] * 4,
        lengths_ref,
        (rows_ref, gains_ref, up_bias_ref),
        bias_ref,
        (
            mixed_ref,
            keep["packed"],
            keep["attended"],
            sum_ref,
            first_ref,
            low_ref,
            keep["act"],
            result_ref,
            scores_ref,
            keep["probs"],
        ),
        keep,
    )
    gains = gains_ref[...].astype(f32)
    for r in range(0, tokens, STRIP):
        strip = slice(r, r + STRIP)
        grad = cotangent_ref[strip].astype(f32) * gains[1:2]
        grad_sum = norm_back(grad, keep["second_norm"][strip], keep["second_scale"][strip, :1])
        first_ref[strip] = grad_sum
        low_ref[strip] = grad_sum.astype(bf16)
    gate_body(low_ref, down_ref, keep["slope"], gate_ref)
    for c in range(0, width, 2 * SLOT):
        cols = slice(c, c + 2 * SLOT)
        sum_ref[:, cols] = first_ref[:, cols] + dot(gate_ref[...], up_ref[cols, :], NT)
    for r in range(0, tokens, STRIP):
        strip = slice(r, r + STRIP)
        grad = sum_ref[strip] * gains[0:1]
        grad_mid = norm_back(grad, keep["first_norm"][strip], keep["first_scale"][strip, :1])
        first_ref[strip] = grad_mid
        low_ref[strip] = grad_mid.astype(bf16)
    grad_ref[...] = dot(low_ref[...], output_ref[...], NT).astype(bf16)
    attention_back(
        keep["packed"], keep["probs"], grad_ref, grad_packed_ref, scores_ref, grads_ref
    )
    for c in range(0, width, 2 * SLOT):
        cols = slice(c, c + 2 * SLOT)
        grad_in = first_ref[:, cols] + dot(grad_packed_ref[...], input_ref[cols, :], NT)
        grad_in_ref[:, cols] = grad_in.astype(bf16)


def gate_body(grad_ref, down_ref, slope_ref, gate_ref):
    for c in range(0, gate_ref.shape[1], 2 * SLOT):
        cols = slice(c, c + 2 * SLOT)
        value = dot(grad_ref[...], down_ref[cols, :], NT) * slope_ref[:, cols].astype(f32)
        gate_ref[:, cols] = value.astype(bf16)


def store_shares(value, row, column, outs, cuts, share):
    rows, columns = value.shape
    value = value.astype(bf16)
    if not cuts:
        outs[0][row : row + rows, column : column + columns] = value
        return
    even = lax.axis_index("dp") % 2 == 0
    for pair in range(row // (2 * share), (row + rows) // (2 * share)):
        top = 2 * pair * share - row
        for i, (start, count, left, width) in enumerate(cuts):
            from_column, to_column = max(column, left), min(column + columns, left + width)
            if from_column >= to_column:
                continue
            cols = slice(from_column - column, to_column - column)
            first = value[top + start : top + start + count, cols]
            second = value[top + share + start : top + share + start + count, cols]
            cols = slice(from_column - left, to_column - left)
            at = pair % 2 * 4 + pair // 2
            outs[2 * i][at, :, cols] = jnp.where(even, second, first)
            outs[2 * i + 1][at, :, cols] = jnp.where(even, first, second)


def column_sum(value):
    return jnp.sum(value, axis=0, keepdims=True)


def feed_kernel(
    cotangent_ref, arrived_ref, gains_ref, normed_ref, scale_ref, act_ref, *rest, outs, cuts, share
):
    shares_out, (grad_sum_ref, low_ref, small_ref) = rest[:outs], rest[outs:]
    tokens = low_ref.shape[0]
    hidden = act_ref.shape[1]
    gains = gains_ref[...].astype(f32)
    last = lax.axis_index("section") == lax.axis_size("section") - 1
    sums = [0.0, 0.0, 0.0]
    for r in range(0, tokens, STRIP):
        strip = slice(r, r + STRIP)
        grad_out = jnp.where(
            last, cotangent_ref[strip].astype(f32), arrived_ref[strip].astype(f32)
        )
        normed = normed_ref[strip]
        grad_sum = norm_back(grad_out * gains[1:2], normed, scale_ref[strip, :1])
        low = grad_sum.astype(bf16)
        grad_sum_ref[strip] = grad_sum
        low_ref[strip] = low
        sums[0] = sums[0] + column_sum(low.astype(f32))
        sums[1] = sums[1] + column_sum(grad_out)
        sums[2] = sums[2] + column_sum(grad_out * normed)
    step = 3 * SLOT
    for r in range(0, hidden, step):
        value = dot(act_ref[:, r : r + step], low_ref[...], TN)
        store_shares(value, r, 0, shares_out, cuts, share)
    for i, value in enumerate(sums):
        small_ref[i : i + 1, :] = value


def gate_kernel(low_ref, slope_ref, first_low_ref, down_ref, after, *rest, outs, cuts, share):
    shares_out, (gate_ref, small_ref) = rest[:outs], rest[outs:]
    gate_body(low_ref, down_ref, slope_ref, gate_ref)
    width, hidden = first_low_ref.shape[1], gate_ref.shape[1]
    step = 3 * SLOT
    for r in range(0, width, step):
        left = first_low_ref[:, r : r + step]
        for c in range(0, hidden, width):
            value = dot(left, gate_ref[:, c : c + width], TN)
            store_shares(value, r, c, shares_out, cuts, share)
    for c in range(0, hidden, width):
        cols = slice(c, c + width)
        small_ref[:, cols] = column_sum(gate_ref[:, cols].astype(f32))


def backwards(every):
    shape = (2 * SLOT, 2 * SLOT)
    left, right = iota(shape, 0), iota(shape, 1)
    ends = jnp.where(left < SLOT, SLOT - 1, jnp.where(left < SLOT + B2D, 3 * SLOT - B2D - 1, 0))
    ends = jnp.where(left >= SLOT + B2D, 4 * SLOT - B2D - 1, ends)
    return dot(every, hot(left + right == ends)).astype(bf16)


def table_rows(sums):
    blank = jnp.zeros((SLOT, SLOT), f32)
    near = jnp.concatenate([sums[:SLOT, :SLOT], blank], axis=1)
    near = pltpu.roll(near, 0, 1, stride=1, stride_axis=0)
    lane = iota((B2D, SLOT), 1)
    across = jnp.where(lane < B2D, sums[SLOT : SLOT + B2D, SLOT:], 0.0)
    across = pltpu.roll(across, 0, 1, stride=1, stride_axis=0)
    down = jnp.where(lane >= B2D, sums[SLOT + B2D :, SLOT:], 0.0)
    down = pltpu.roll(down, B2D, 1, stride=1, stride_axis=0)
    return jnp.concatenate([column_sum(near), column_sum(across), column_sum(down)], axis=1)


def chain_kernel(
    grad_sum_ref,
    gate_ref,
    normed_ref,
    scale_ref,
    packed_ref,
    probs_ref,
    order_ref,
    column_ref,
    row_ref,
    gains_ref,
    up_ref,
    output_ref,
    after,
    mid_ref,
    low_ref,
    grad_packed_ref,
    small_ref,
    table_ref,
    sum_ref,
    grad_ref,
    reach_ref,
    scores_ref,
    grads_ref,
):
    tokens, width = sum_ref.shape
    pages = tokens // SLOT
    gains = gains_ref[...].astype(f32)
    for c in range(0, width, 2 * SLOT):
        cols = slice(c, c + 2 * SLOT)
        sum_ref[:, cols] = grad_sum_ref[:, cols] + dot(gate_ref[...], up_ref[cols, :], NT)
    first_sum = gain_sum = branch_sum = 0.0
    for r in range(0, tokens, STRIP):
        strip = slice(r, r + STRIP)
        grad_first, normed = sum_ref[strip], normed_ref[strip]
        grad_mid = norm_back(grad_first * gains[0:1], normed, scale_ref[strip, :1])
        low = grad_mid.astype(bf16)
        mid_ref[strip] = grad_mid
        low_ref[strip] = low
        first_sum = first_sum + column_sum(grad_first)
        gain_sum = gain_sum + column_sum(grad_first * normed)
        branch_sum = branch_sum + column_sum(low.astype(f32))
    grad_ref[...] = dot(low_ref[...], output_ref[...], NT).astype(bf16)
    hots = [
        page_hot(order_ref[p : p + 1, :], column_ref[p : p + 1, :], row_ref[p : p + 1, :])
        for p in range(pages)
    ]
    every = backwards(jnp.concatenate(hots, axis=0))
    reach_ref[...] = jnp.zeros_like(reach_ref)
    attention_back(packed_ref, probs_ref, grad_ref, grad_packed_ref, scores_ref, grads_ref)
    for head in range(HEADS):
        along = []
        for p in range(pages):
            top = (p * HEADS + head) * SLOT
            along.append(dot(grads_ref[top : top + SLOT, :], hots[p]).astype(bf16))
        sums = dot(every, jnp.concatenate(along, axis=0), TN)
        reach_ref[head : head + 1, :] = table_rows(sums)
    for i, value in enumerate((first_sum, gain_sum, branch_sum)):
        small_ref[i : i + 1, :] = value
    table_ref[...] = dot(
        bucket_places().astype(f32), reach_ref[...], NT, precision=lax.Precision.HIGHEST
    )


def last_kernel(
    attended_ref,
    low_ref,
    mixed_low_ref,
    grad_packed_ref,
    block_ref,
    after,
    *shares_out,
    outs,
    cuts,
    share,
):
    width = low_ref.shape[1]
    step = 3 * SLOT
    for r in range(0, width, step):
        rows = slice(r, r + step)
        value = dot(attended_ref[:, rows], low_ref[...], TN)
        store_shares(value, r, 0, shares_out, cuts, share)
        for c in range(0, 3 * width, width):
            value = dot(mixed_low_ref[:, rows], grad_packed_ref[:, c : c + width], TN)
            store_shares(value, r, width + c, shares_out, cuts, share)
        if cuts:
            store_shares(block_ref[rows], r, 4 * width, shares_out, cuts, share)


def input_kernel(
    mid_ref,
    grad_packed_ref,
    tokens_ref,
    small_down_ref,
    small_up_ref,
    small_chain_ref,
    table_ref,
    lengths_ref,
    order_ref,
    region_ref,
    taps_ref,
    input_ref,
    after,
    grad_in_ref,
    small_ref,
    block_ref,
    sum_ref,
    *,
    share,
):
    tokens, width = sum_ref.shape
    pages = tokens // SLOT
    conv_on = (lax.axis_index("section") == 0).astype(f32)
    taps = taps_ref[...].astype(f32) * conv_on
    for c in range(0, width, 2 * SLOT):
        cols = slice(c, c + 2 * SLOT)
        sum_ref[:, cols] = mid_ref[:, cols] + dot(grad_packed_ref[...], input_ref[cols, :], NT)
    tap_sums = [0.0] * TAPS
    mixed_sum = 0.0
    for p in range(pages):
        here = slice(p * SLOT, (p + 1) * SLOT)
        order = order_ref[p : p + 1, :]
        rank_hot = rank_hot_of(order)
        masks = tap_columns(order, region_ref[p : p + 1, :], lengths_ref[p])
        ordered = dot(rank_hot, tokens_ref[here], TN)
        grad_mixed = sum_ref[here]
        grad_order = place_rows(rank_hot, grad_mixed, TN)
        source = jnp.zeros_like(ordered)
        for j in range(TAPS):
            masked = grad_order * masks[:, j : j + 1]
            tap_sums[j] = tap_sums[j] + column_sum(masked * shifted(ordered, j - REACH))
            source = source + shifted(taps[j : j + 1] * masked, REACH - j)
        grad_in_ref[here] = grad_mixed + place_rows(rank_hot, source, NN)
        mixed_sum = mixed_sum + column_sum(grad_mixed)
    down, chain = small_down_ref[...], small_chain_ref[...]
    rows = [
        column_sum(grad_packed_ref[:, :width].astype(f32)),
        column_sum(grad_packed_ref[:, 2 * width :].astype(f32)),
        chain[2:3],
        chain[0:1],
        down[0:1],
        down[1:2],
        conv_on * mixed_sum,
        chain[1:2],
        down[2:3],
    ]
    for i, value in enumerate(rows + [conv_on * value for value in tap_sums]):
        small_ref[i : i + 1, :] = value
    if share:
        small_block(small_ref, small_up_ref, table_ref, block_ref, share)


SMALL_ROWS = 16


def small_block(small_ref, up_ref, table_ref, block_ref, share):
    width = small_ref.shape[1]
    shares = block_ref.shape[0] // share
    part = width // shares
    up_part = up_ref.shape[1] // shares
    buckets = (B1D + 2 * B2D) // shares
    block_ref[...] = jnp.zeros_like(block_ref)
    small, up = small_ref[...], jnp.broadcast_to(up_ref[...], (8, up_ref.shape[1]))
    for s in range(shares):
        top = s * share
        shift = (width - s * part) % width
        here = pltpu.roll(small, shift, 1) if shift else small
        block_ref[top : top + SMALL_ROWS, :] = here[:, :SLOT]
        shift = (up.shape[1] - s * up_part) % up.shape[1]
        here = pltpu.roll(up, shift, 1) if shift else up
        top += SMALL_ROWS
        block_ref[top : top + 1, :] = here[:1, :SLOT]
        block_ref[top + 1 : top + 2, :] = here[:1, SLOT : 2 * SLOT]
        top += 2
        block_ref[top : top + buckets, :] = table_ref[s * buckets : (s + 1) * buckets, :]


def place():
    index = lax.axis_index("dp")
    return index // 4, index // 2 % 2


def added(out_ref, out_at, parts, window=None):
    rows = out_ref.shape[-2]
    for r in range(0, rows, 16):
        strip = slice(r, r + 16)
        total = 0.0
        for ref, at, windowed in parts:
            if windowed:
                row, _, column, columns = window
                value = ref[at, row + r : row + r + 16, column : column + columns]
            else:
                value = ref[at, strip]
            total = total + value.astype(f32)
        if out_at is None:
            out_ref[strip] = total.astype(bf16)
        else:
            out_ref[out_at, strip] = total.astype(bf16)


def fetched(recv_hbm, first, window, scratch, sems):
    row, rows, column, columns = window
    copies = []
    for k in range(4):
        source = recv_hbm.at[first + k, pl.ds(row, rows), pl.ds(column, columns)]
        copies.append(pltpu.make_async_copy(source, scratch.at[k], sems.at[k]))
        copies[-1].start()
    return copies


def leave_kernel(mine_ref, recv_ref, *rest, window, fetch):
    first = 4 * (1 - place()[1])
    if fetch:
        out_ref, scratch, sems = rest[-3:]
        copies = fetched(recv_ref, first, window, scratch, sems)
    else:
        out_ref = rest[-1]
    for k in range(4):
        other = (recv_ref, first + k, True)
        if fetch:
            copies[k].wait()
            other = (scratch, k, False)
        added(out_ref, k, ((mine_ref, first + k, True), other), window)


def near_kernel(mine_ref, recv_ref, y_ref, *rest, window, fetch):
    z, y = place()
    leave_ref, keep_ref = rest[-4:-2] if fetch else rest[-2:]
    if fetch:
        scratch, sems = rest[-2:]
        for copy in fetched(recv_ref, 4 * y, window, scratch, sems):
            copy.wait()
    for out_ref, parity in ((leave_ref, 1 - z % 2), (keep_ref, z % 2)):
        for k in range(2):
            block = 2 * k + parity
            at = 4 * y + block
            other = (scratch, block, False) if fetch else (recv_ref, at, True)
            added(out_ref, k, ((mine_ref, at, True), other, (y_ref, block, False)), window)


def far_kernel(keep_ref, recv_ref, *rest):
    leave_ref, own_ref = rest[-2:]
    high = place()[0] // 2
    for out_ref, k in ((leave_ref, 1 - high), (own_ref, high)):
        added(out_ref, None, ((keep_ref, k, False), (recv_ref, k, False)))


def near_first_kernel(mine_ref, recv_ref, after, leave_ref, keep_ref):
    z, _ = place()
    for out_ref, parity in ((leave_ref, 1 - z % 2), (keep_ref, z % 2)):
        for k in range(4):
            at = 2 * k + parity
            added(out_ref, k, ((mine_ref, at, False), (recv_ref, at, False)))


def far_first_kernel(keep_ref, recv_ref, after, leave_ref, stay_ref):
    high = place()[0] // 2
    for out_ref, k in ((leave_ref, 1 - high), (stay_ref, high)):
        for y in range(2):
            at = 2 * y + k
            added(out_ref, y, ((keep_ref, at, False), (recv_ref, at, False)))


def cross_kernel(keep_ref, recv_ref, after, leave_ref, own_ref):
    y = place()[1]
    for out_ref, at in ((leave_ref, 1 - y), (own_ref, y)):
        added(out_ref, None, ((keep_ref, at, False), (recv_ref, at, False)))


def both(parts):
    return parts[0][...].astype(f32) + parts[1][...].astype(f32)


def down_end(*refs):
    out_ref, token_ref = refs[-2:]
    token_ref[...] = jnp.zeros_like(token_ref)
    rows = refs[0].shape[0]
    out_ref[:rows] = both(refs[:2])
    out_ref[rows:] = both(refs[2:4])


def up_end(*refs):
    out_ref, token_ref = refs[-2:]
    token_ref[...] = jnp.zeros_like(token_ref)
    columns = refs[0].shape[1]
    out_ref[:, :columns] = both(refs[:2])
    out_ref[:, columns:] = both(refs[2:4])


def last_end(*refs):
    sum_ref, block_ref = refs[-2:]
    input_ref, output_ref, bias_ref, gain_ref, tap_ref, up_ref, table_ref = refs[-9:-2]
    column = 0
    for i in range(0, len(refs) - 10, 2):
        columns = refs[i].shape[1]
        sum_ref[:, column : column + columns] = both(refs[i : i + 2])
        column += columns
    width, share = output_ref.shape[1], output_ref.shape[0]
    output_ref[...] = sum_ref[:, :width]
    input_ref[...] = sum_ref[:, width : 4 * width]
    block_ref[...] = sum_ref[:, 4 * width :]
    for i in range(7):
        bias_ref[i] = block_ref[i : i + 1, :share]
        tap_ref[i] = block_ref[9 + i : 10 + i, :share]
    gain_ref[...] = block_ref[7:9, :share]
    rest = up_ref.shape[1] - SLOT
    up_ref[:, :SLOT] = block_ref[SMALL_ROWS : SMALL_ROWS + 1, :]
    up_ref[:, SLOT:] = block_ref[SMALL_ROWS + 1 : SMALL_ROWS + 2, :rest]
    for i in range(table_ref.shape[1] // HEADS):
        at = SMALL_ROWS + 2 + i
        table_ref[:, i * HEADS : (i + 1) * HEADS] = block_ref[at : at + 1, :HEADS]


def kernel_call(body, name, ins, outs, scratch, flops=0, vmem=10):
    return pl.pallas_call(
        body,
        name=name,
        out_shape=[shape for shape, _ in outs],
        in_specs=[spec for _, spec in ins],
        out_specs=[spec for _, spec in outs],
        scratch_shapes=scratch,
        compiler_params=pltpu.CompilerParams(vmem_limit_bytes=vmem << 20),
        cost_estimate=pl.CostEstimate(flops=flops, bytes_accessed=0, transcendentals=0),
    )(*[value for value, _ in ins])


def near_by(value):
    return pltpu.with_memory_space_constraint(value, pltpu.VMEM)


def in_hbm(value):
    return pltpu.with_memory_space_constraint(value, pltpu.HBM)


def near_shape(dims, kind=bf16):
    return pltpu.VMEM(dims, kind)


class Summing:
    def __init__(self):
        self.pairs, self.windows, self.crossed, self.kept, self.ends = {}, {}, {}, {}, {}
        self.fetch = {}

    @staticmethod
    def _swap(value, bits):
        return near_by(lax.ppermute(value, "dp", [(i, i ^ bits) for i in range(16)]))

    @staticmethod
    def _add(body, name, ins, after, outs, cost=0, earlier=(), scratch=(), fetch=False):
        specs = [IN_VMEM] * len(ins)
        if fetch:
            specs[1] = IN_PLACE
        return kernel_call(
            body,
            name,
            [(near_by(value), spec) for value, spec in zip(ins, specs)]
            + [(value, IN_PLACE) for value in (after, *earlier)],
            [(near_shape(dims), IN_VMEM) for dims in outs],
            list(scratch),
            cost,
            4,
        )

    def core(self, theirs, mine, fetch=False, **windows):
        recv = self._swap(theirs, 1)
        for name, window in windows.items():
            self.pairs[name], self.windows[name] = [mine, recv], window
            self.fetch[name] = fetch

    def _fetching(self, name, body):
        window, fetch = self.windows[name], self.fetch[name]
        dims = (4, window[1], window[3])
        scratch = [pltpu.VMEM(dims, bf16), pltpu.SemaphoreType.DMA((4,))] if fetch else []
        body = functools.partial(body, window=window, fetch=fetch)
        return body, dict(scratch=scratch, fetch=fetch), dims

    def leave(self, name, after, earlier=None):
        body, more, dims = self._fetching(name, leave_kernel)
        earlier = [self.crossed[earlier]] if earlier else []
        (out,) = self._add(body, "leave", self.pairs[name], after, [dims], 0, earlier, **more)
        self.crossed[name] = self._swap(out, 2)
        return out

    def near(self, name, after, earlier=()):
        body, more, dims = self._fetching(name, near_kernel)
        dims = (2,) + dims[1:]
        ins = self.pairs[name] + [self.crossed[name]]
        earlier = [self.ends[other][1] for other in earlier]
        out, keep = self._add(body, "near", ins, after, [dims, dims], COST, earlier, **more)
        self.kept[name] = [keep, self._swap(out, 4)]
        return out

    def far(self, name, after, earlier=()):
        ins = self.kept[name]
        dims = ins[0].shape[1:]
        earlier = [self.ends[other][1] for other in earlier]
        out, own = self._add(far_kernel, "far", ins, after, [dims, dims], COST, earlier)
        self.ends[name] = [own, self._swap(out, 8)]
        return out

    def near_first(self, name, after):
        ins = self.pairs[name]
        dims = (4,) + ins[0].shape[1:]
        out, keep = self._add(near_first_kernel, "near_first", ins, after, [dims, dims], COST)
        self.kept[name] = [keep, self._swap(out, 4)]
        return out

    def far_first(self, name, after):
        ins = self.kept[name]
        dims = (2,) + ins[0].shape[1:]
        out, stay = self._add(far_first_kernel, "far_first", ins, after, [dims, dims], COST)
        self.kept[name] = [stay, self._swap(out, 8)]
        return out

    def cross(self, name, after):
        ins = self.kept[name]
        dims = ins[0].shape[1:]
        out, own = self._add(cross_kernel, "cross", ins, after, [dims, dims], COST)
        self.ends[name] = [own, self._swap(out, 2)]
        return out


def local(
    tokens,
    cotangent,
    page_lengths,
    cut_order,
    cut_region,
    cell_column,
    cell_row,
    input_proj,
    output_proj,
    up_proj,
    down_proj,
    up_bias,
    bias_rows,
    gain_rows,
    conv_taps,
    bias_table,
):
    section_count = lax.axis_size("section")
    dp_count = lax.axis_size("dp")
    by_hops = dp_count == 16
    pages, _, width = tokens.shape
    hidden = up_proj.shape[2]
    count = pages * SLOT
    weights = [w[0] for w in (input_proj, output_proj, up_proj, down_proj)]
    rows, gains, taps = bias_rows[0], gain_rows[0], conv_taps[0]
    tokens, cotangent = tokens.reshape(count, width), cotangent.reshape(count, width)

    def shape(dims, kind):
        return jax.ShapeDtypeStruct(dims, kind)

    def inside(*values):
        return [(v, IN_VMEM) for v in values]

    def in_place(*values):
        return [(v, IN_PLACE) for v in values]

    def scalars(*values):
        return [(v, IN_SMEM) for v in values]

    wide, low = shape((count, width), f32), shape((count, width), bf16)
    wide_scratch = pltpu.VMEM((count, width), f32)
    low_scratch = pltpu.VMEM((count, width), bf16)
    packed_scratch = pltpu.VMEM((count, 3 * width), bf16)
    hidden_scratch = pltpu.VMEM((count, hidden), bf16)
    bias_dims = (pages * HEADS * SLOT, SLOT)

    def sems(number):
        return pltpu.SemaphoreType.DMA((number,))

    first_ins = [tokens, cut_order, cut_region, cell_column, cell_row, rows, gains, up_bias]
    first_ins += [taps, bias_table]
    result, mixed, bias, *near_weights = kernel_call(
        first_kernel,
        "first",
        scalars(in_hbm(page_lengths)) + in_place(*map(in_hbm, first_ins + weights)),
        inside(low, near_shape((count, width), f32), near_shape(bias_dims, f32))
        + inside(*[near_shape(w.shape) for w in weights]),
        [
            packed_scratch,
            low_scratch,
            wide_scratch,
            wide_scratch,
            low_scratch,
            hidden_scratch,
            pltpu.VMEM(bias_dims, f32),
            pltpu.VMEM(bias_dims, bf16),
            pltpu.VMEM((HEADS, 2 * SLOT, 2 * SLOT), bf16),
            pltpu.VMEM((HEADS, count, 2 * SLOT), bf16),
            *[pltpu.VMEM(v.shape, v.dtype) for v in first_ins],
            sems(len(first_ins) + len(weights)),
        ],
    )
    input_w, output_w, up_w, down_w = near_weights = list(map(near_by, near_weights))
    arrived = near_by(
        lax.ppermute(result, "section", [(i, i + 1) for i in range(section_count - 1)])
    )
    shapes = kept_shapes(count, width, hidden)
    layer_out, leaving, *kept_list = kernel_call(
        second_kernel,
        "second",
        inside(arrived, cotangent)
        + scalars(page_lengths)
        + inside(rows, gains, up_bias)
        + inside(*map(near_by, (mixed, bias, *near_weights))),
        inside(low, near_shape((count, width)), *[near_shape(*s) for s in shapes]),
        [
            wide_scratch,
            wide_scratch,
            wide_scratch,
            low_scratch,
            hidden_scratch,
            low_scratch,
            packed_scratch,
            pltpu.VMEM(bias_dims, f32),
            pltpu.VMEM(bias_dims, bf16),
        ],
    )
    kept = dict(zip([name for name, _, _ in KEPT], map(near_by, kept_list)))
    arrived_grad = near_by(
        lax.ppermute(leaving, "section", [(i + 1, i) for i in range(section_count - 1)])
    )
    part = width // dp_count

    def cut(dims, cuts):
        share = dims[0] // dp_count
        if not by_hops:
            outs, cuts = inside(shape(dims, bf16)), ()
        else:
            halves_out = [near_shape((dp_count // 2, c[1], c[3])) for c in cuts for _ in range(2)]
            outs = inside(*halves_out)
        return outs, dict(outs=len(outs), cuts=cuts, share=share)

    half = hidden // dp_count // 2
    down_outs, down_cut = cut((hidden, width), ((0, half, 0, width), (half, half, 0, width)))
    up_outs, up_cut = cut((width, hidden), ((0, part, 0, hidden),))
    *down_parts, grad_sum, grad_low, small_down = kernel_call(
        functools.partial(feed_kernel, **down_cut),
        "feed",
        inside(cotangent, arrived_grad, gains)
        + inside(kept["second_norm"], kept["second_scale"], kept["act"]),
        down_outs + inside(wide, low, shape((8, width), f32)),
        [],
    )
    *up_parts, gate, small_up = kernel_call(
        functools.partial(gate_kernel, **up_cut),
        "gate",
        inside(grad_low, kept["slope"], kept["first_low"], down_w) + in_place(small_down),
        up_outs + inside(shape((count, hidden), bf16), shape((1, hidden), f32)),
        [],
    )
    summing = Summing()
    after = small_up
    if by_hops:
        piece = (0, half, 0, width)
        side = hidden // 2
        summing.core(*down_parts[:2], d1=piece)
        summing.core(*down_parts[2:], d2=piece)
        summing.core(*up_parts, u1=(0, part, 0, side), u2=(0, part, side, side))
        after = summing.leave("d1", after)
        after = summing.near_first("d2", after)
        after = summing.leave("u1", after)
    grad_mid, grad_branch, grad_packed, small_chain, table = kernel_call(
        chain_kernel,
        "chain",
        inside(grad_sum, gate, kept["first_norm"], kept["first_scale"], kept["packed"])
        + inside(kept["probs"], cut_order, cell_column, cell_row, gains)
        + inside(up_w, output_w)
        + in_place(after),
        inside(wide, low, shape((count, 3 * width), bf16), shape((8, width), f32))
        + inside(shape((B1D + 2 * B2D, SLOT), f32)),
        [
            wide_scratch,
            low_scratch,
            pltpu.VMEM((SLOT, 4 * SLOT), f32),
            pltpu.VMEM(bias_dims, f32),
            pltpu.VMEM(bias_dims, bf16),
        ],
    )
    after = grad_mid
    if by_hops:
        after = summing.near("d1", after)
        after = summing.far_first("d2", after)
        after = summing.leave("u2", after)
    grad_in, small_rows, block = kernel_call(
        functools.partial(input_kernel, share=part if by_hops else 0),
        "input",
        inside(grad_mid, grad_packed, tokens, small_down, small_up, small_chain, table)
        + scalars(page_lengths)
        + inside(cut_order, cut_region, taps, input_w)
        + in_place(after),
        inside(wide, shape((16, width), f32), near_shape((width, SLOT), f32)),
        [wide_scratch],
    )
    after = block
    columns = 4 * width + (SLOT if by_hops else 0)
    last_outs, last_cut = cut((width, columns), ((0, part, 0, columns),))
    last_parts = kernel_call(
        functools.partial(last_kernel, **last_cut),
        "last",
        inside(kept["attended"], grad_branch, kept["mixed_low"], grad_packed, near_by(block))
        + in_place(after),
        last_outs,
        [],
    )
    after = last_parts[0]
    if by_hops:
        token = near_shape((8, SLOT), f32)
        windows, column = {}, 0
        for name, end in (("a1", 2 * width - 2 * SLOT), ("a2", 3 * width + SLOT), ("a3", columns)):
            windows[name], column = (0, part, column, end - column), end
        summing.core(*last_parts, fetch=True, **windows)
        ends = summing.ends
        after = summing.near("u1", after)
        after = summing.far("d1", after)
        after = summing.cross("d2", after)
        after = summing.leave("a1", after, "u2")
        after = summing.near("u2", after)
        after = summing.far("u1", after, ["d1"])
        after = summing.leave("a2", after)
        down_grad, after = kernel_call(
            down_end,
            "down_end",
            inside(*map(near_by, ends["d1"] + ends["d2"])) + in_place(after),
            inside(shape((hidden // dp_count, width), f32), token),
            [],
            vmem=4,
        )
        after = summing.far("u2", after)
        after = summing.near("a1", after)
        after = summing.leave("a3", after)
        after = summing.near("a2", after, ["u1", "u2"])
        after = summing.far("a1", after)
        after = summing.near("a3", after)
        after = summing.far("a2", after)
        after = summing.far("a3", after)
        up_grad, after = kernel_call(
            up_end,
            "up_end",
            inside(*map(near_by, ends["u1"] + ends["u2"])) + in_place(after),
            inside(shape((part, hidden), f32), token),
            [],
            vmem=4,
        )
        input_grad, output_grad, bias_grad, gain_grad, tap_grad, up_bias_grad, table_grad = (
            kernel_call(
                last_end,
                "last_end",
                inside(*map(near_by, ends["a1"] + ends["a2"] + ends["a3"])) + in_place(after),
                inside(
                    shape((part, 3 * width), f32),
                    shape((part, width), f32),
                    shape((7, 1, part), f32),
                    shape((2, part), f32),
                    shape((TAPS, 1, part), f32),
                    shape((1, hidden // dp_count), f32),
                    shape((1, table.shape[0] * HEADS // dp_count), f32),
                ),
                [pltpu.VMEM((part, columns), f32), pltpu.VMEM((part, SLOT), f32)],
                vmem=4,
            )
        )
    else:

        def scattered(value):
            return lax.psum_scatter(value, "dp", scatter_dimension=0, tiled=True).astype(f32)

        down_grad, up_grad, last_grad = (
            scattered(parts[0]) for parts in (down_parts, up_parts, last_parts)
        )
        input_grad, output_grad = last_grad[:, width:], last_grad[:, :width]
        small = [
            small_rows.reshape(16, dp_count, part).transpose(1, 0, 2).reshape(dp_count, -1),
            small_up.reshape(dp_count, -1),
            table[:, :HEADS].reshape(dp_count, -1),
        ]
        small = jnp.concatenate(small, axis=1)
        used = small.shape[1]
        small = jnp.pad(small, ((0, 0), (0, -used % SLOT))).reshape(-1, SLOT)
        small = scattered(small).reshape(-1)
        vectors = small[: 16 * part].reshape(16, part)
        bias_grad, tap_grad = vectors[:7, None], vectors[9:, None]
        gain_grad = vectors[7:9]
        at = 16 * part + hidden // dp_count
        up_bias_grad, table_grad = small[None, 16 * part : at], small[None, at:used]
    return (
        layer_out.reshape(1, pages, SLOT, width),
        grad_in.reshape(1, pages, SLOT, width),
        input_grad[None],
        output_grad[None],
        up_grad[None],
        down_grad[None],
        up_bias_grad,
        bias_grad.transpose(1, 0, 2),
        gain_grad[None],
        tap_grad.transpose(1, 0, 2),
        table_grad,
    )


def solution(mesh):
    by_section = [P("section", None, None)] * 4
    placed = (
        P("dp", None, None),
        P("dp", None, None),
        P("dp"),
        P("dp", None),
        P("dp", None),
        P("dp", None),
        P("dp", None),
        *by_section,
        P("section", None),
        P("section", None, None),
        P("section", None, None),
        P("section", None, None),
        P("section", None),
    )
    return jax.shard_map(
        local,
        mesh=mesh,
        in_specs=placed,
        out_specs=(
            P("section", "dp", None, None),
            P("section", "dp", None, None),
            P("section", "dp", None),
            P("section", "dp", None),
            P("section", "dp", None),
            P("section", "dp", None),
            P("section", "dp"),
            P("section", None, "dp"),
            P("section", None, "dp"),
            P("section", None, "dp"),
            P("section", "dp"),
        ),
        check_vma=False,
    )
```

```python
import functools

import jax
import jax.numpy as jnp
from jax import lax
from jax.experimental import pallas as pl
from jax.experimental.pallas import tpu as pltpu
from jax.sharding import PartitionSpec as P

HEADS = 12
HEAD = 64
B1D = 32
B2D = 64
SLOT = 128
PAIRS = HEADS // 2
TAPS = 7
REACH = 3
EPSILON = 1e-05
COST = 20_000_000_000
MASKED = -1000000000.0
STRIP = 64

f32 = jnp.float32
bf16 = jnp.bfloat16
NN = ((1,), (0,))
NT = ((1,), (1,))
TN = ((0,), (0,))

IN_VMEM = pl.BlockSpec(memory_space=pltpu.VMEM)
IN_SMEM = pl.BlockSpec(memory_space=pltpu.SMEM)
IN_PLACE = pl.BlockSpec(memory_space=pl.ANY)


def dot(left, right, dims=NN, precision=None):
    return lax.dot_general(
        left, right, (dims, ((), ())), precision=precision, preferred_element_type=f32
    )


def iota(shape, axis):
    return lax.broadcasted_iota(jnp.int32, shape, axis)


def hot(mask):
    return mask.astype(f32).astype(bf16)


def identity():
    return hot(iota((SLOT, SLOT), 0) == iota((SLOT, SLOT), 1))


def rank_hot_of(order):
    return hot(order == iota((SLOT, SLOT), 0))


def page_hot(order, column, row):
    cells = iota((SLOT, SLOT), 0)
    wanted = jnp.where(cells < B2D, column, row + B2D)
    cell_hot = dot(identity(), hot(wanted == cells), NT).astype(bf16)
    return jnp.concatenate([rank_hot_of(order), cell_hot], axis=1)


def tap_columns(order, region, length):
    shape = (8, SLOT)
    order, region = jnp.broadcast_to(order, shape), jnp.broadcast_to(region, shape)
    live = (order < length).astype(jnp.int32)
    lane, tap = iota(shape, 1), iota(shape, 0)
    masks = jnp.zeros(shape, f32)
    for j in range(TAPS):
        offset = j - REACH
        shift = (-offset) % SLOT
        region_j = pltpu.roll(region, shift, 1) if shift else region
        live_j = pltpu.roll(live, shift, 1) if shift else live
        joined = (lane + offset >= 0) & (lane + offset < SLOT) & (region_j == region) & (live_j > 0)
        masks = jnp.where((tap == j) & joined, 1.0, masks)
    return dot(identity(), masks.astype(bf16), NT)


def shifted(rows, offset):
    shift = (-offset) % SLOT
    return pltpu.roll(rows, shift, 0) if shift else rows


def place_rows(rank_hot, rows, dims):
    high = rows.astype(bf16)
    low = (rows - high.astype(f32)).astype(bf16)
    return dot(rank_hot, high, dims) + dot(rank_hot, low, dims)


def bucket_places():
    shape = (B1D + 2 * B2D, 4 * SLOT)
    bucket, lane = iota(shape, 0), iota(shape, 1)
    near = jnp.clip(lane - (SLOT - 1) + B1D // 2, 0, B1D - 1)
    column = B1D + jnp.clip(lane - 2 * SLOT - (B2D - 1) + B2D // 2, 0, B2D - 1)
    row = B1D + B2D + jnp.clip(lane - 3 * SLOT - (B2D - 1) + B2D // 2, 0, B2D - 1)
    wanted = jnp.where(lane < 2 * SLOT, near, jnp.where(lane < 3 * SLOT, column, row))
    return bucket == wanted


def halves(pair):
    lane = iota((1, SLOT), 1)
    first = hot(lane < HEAD)
    second = hot(lane >= HEAD)
    return jnp.concatenate([pair * first, pair * second], axis=0)


def side_by_side(stacked):
    return jnp.concatenate([stacked[:SLOT], stacked[SLOT:]], axis=1)


def normed_of(value):
    average = jnp.mean(value, axis=-1, keepdims=True)
    centered = value - average
    spread = jnp.mean(centered * centered, axis=-1, keepdims=True)
    inverse = lax.rsqrt(spread + EPSILON)
    return centered * inverse, inverse


def norm_back(grad, normed, inverse):
    first_mean = jnp.mean(grad, axis=-1, keepdims=True)
    second_mean = jnp.mean(grad * normed, axis=-1, keepdims=True)
    return inverse * (grad - first_mean - normed * second_mean)


def table_columns(table):
    buckets = table.shape[1] // HEADS
    bucket = iota((buckets, table.shape[1]), 0) * HEADS
    lane = iota((buckets, table.shape[1]), 1)
    own = hot((lane >= bucket) & (lane < bucket + HEADS))
    lane = iota((16, table.shape[1]), 1)
    times = ((lane.astype(f32) + 0.5) * (1.0 / HEADS)).astype(jnp.int32)
    head = hot(lane - HEADS * times == iota((16, table.shape[1]), 0))
    return dot(own * table, head, NT).astype(bf16)


def bias_body(
    order_ref, column_ref, row_ref, table_ref, bias_ref, grids_ref, hot_rows_ref, between
):
    pages = order_ref.shape[0]
    hots = [
        page_hot(order_ref[p : p + 1, :], column_ref[p : p + 1, :], row_ref[p : p + 1, :])
        for p in range(pages)
    ]
    every = jnp.concatenate(hots, axis=0)
    reach = dot(table_columns(table_ref[...]), hot(bucket_places()), TN)
    lane = iota((B2D, SLOT), 1)
    for h in range(HEADS):
        row = reach[h : h + 1, :]
        near = jnp.broadcast_to(row[:, : 2 * SLOT], (SLOT, 2 * SLOT))
        near = pltpu.roll(near, SLOT + 1, 1, stride=1, stride_axis=0)[:, :SLOT]
        across = jnp.broadcast_to(row[:, 2 * SLOT : 3 * SLOT], (B2D, SLOT))
        across = pltpu.roll(across, B2D + 1, 1, stride=1, stride_axis=0)
        down = jnp.broadcast_to(row[:, 3 * SLOT :], (B2D, SLOT))
        down = pltpu.roll(down, 1, 1, stride=1, stride_axis=0)
        cells = jnp.concatenate(
            [jnp.where(lane < B2D, across, 0.0), jnp.where(lane >= B2D, down, 0.0)], axis=0
        )
        blank = jnp.zeros((SLOT, SLOT), bf16)
        grids_ref[h, :SLOT, :SLOT] = near.astype(bf16)
        grids_ref[h, :SLOT, SLOT:] = blank
        grids_ref[h, SLOT:, :SLOT] = blank
        grids_ref[h, SLOT:, SLOT:] = cells.astype(bf16)
        between(h)
    for h in range(HEADS):
        hot_rows_ref[h] = dot(every, grids_ref[h]).astype(bf16)
    for p in range(pages):
        for h in range(HEADS):
            at = (p * HEADS + h) * SLOT
            rows = hot_rows_ref[h, p * SLOT : (p + 1) * SLOT, :]
            bias_ref[at : at + SLOT, :] = dot(rows, hots[p], NT)


def project(chunk, low_ref, input_ref, rows, packed_ref):
    width = low_ref.shape[1]
    start = chunk * 2 * SLOT
    part, at = start // width, start % width
    value = dot(low_ref[...], input_ref[:, start : start + 2 * SLOT])
    if part != 1:
        row = part // 2
        value = value + rows[row : row + 1, at : at + 2 * SLOT]
    packed_ref[:, start : start + 2 * SLOT] = value.astype(bf16)


def forward_body(weights, waits, lengths_ref, vectors, bias_ref, work, keep):
    input_ref, output_ref, up_ref, down_ref = weights
    rows_ref, gains_ref, up_bias_ref = vectors
    mixed_ref, packed_ref, attended_ref, sum_ref, first_ref, low_ref, act_ref, result_ref = work[:8]
    scores_ref, probs_ref = work[8:]
    rows, gains = rows_ref[...].astype(f32), gains_ref[...].astype(f32)
    tokens, width = mixed_ref.shape
    hidden = act_ref.shape[1]
    if keep:
        low_ref[...] = mixed_ref[...].astype(bf16)
        keep["mixed_low"][...] = low_ref[...]
        for chunk in range(3 * width // (2 * SLOT)):
            project(chunk, low_ref, input_ref, rows, packed_ref)
    places = [(p, pair) for p in range(tokens // SLOT) for pair in range(PAIRS)]
    for p, pair in places:
        here, at = slice(p * SLOT, (p + 1) * SLOT), pair * SLOT
        top = (p * HEADS + 2 * pair) * SLOT
        queries = halves(packed_ref[here, at : at + SLOT]) * (HEAD**-0.5)
        keys = packed_ref[here, width + at : width + at + SLOT]
        scores_ref[top : top + 2 * SLOT, :] = dot(queries, keys, NT)
    for p, pair in places:
        top = (p * HEADS + 2 * pair) * SLOT
        rows_here = slice(top, top + 2 * SLOT)
        live = iota((2 * SLOT, SLOT), 1) < lengths_ref[p]
        scores = jnp.where(live, scores_ref[rows_here, :] + bias_ref[rows_here, :], MASKED)
        expo = jnp.exp(scores - jnp.max(scores, axis=-1, keepdims=True))
        probs = expo * (1.0 / jnp.sum(expo, axis=-1, keepdims=True))
        probs_ref[rows_here, :] = probs.astype(bf16)
    for p, pair in places:
        here, at = slice(p * SLOT, (p + 1) * SLOT), pair * SLOT
        top = (p * HEADS + 2 * pair) * SLOT
        values = halves(packed_ref[here, 2 * width + at : 2 * width + at + SLOT])
        probs = side_by_side(probs_ref[top : top + 2 * SLOT, :])
        attended_ref[here, at : at + SLOT] = dot(probs, values).astype(bf16)
    waits[1]()
    sum_ref[...] = dot(attended_ref[...], output_ref[...])
    for r in range(0, tokens, STRIP):
        strip = slice(r, r + STRIP)
        normed, inverse = normed_of(mixed_ref[strip] + sum_ref[strip] + rows[2:3])
        first = normed * gains[0:1] + rows[3:4]
        first_ref[strip] = first
        low_ref[strip] = first.astype(bf16)
        if keep:
            keep["first_norm"][strip] = normed
            keep["first_scale"][strip] = jnp.broadcast_to(inverse, (STRIP, SLOT))
            keep["first_low"][strip] = first.astype(bf16)
    waits[2]()
    for c in range(0, hidden, 2 * SLOT):
        cols = slice(c, c + 2 * SLOT)
        gate = dot(low_ref[...], up_ref[:, cols]) + up_bias_ref[:, cols].astype(f32)
        below = 0.5 + 0.5 * lax.erf(gate * 0.7071067811865476)
        act_ref[:, cols] = (gate * below).astype(bf16)
        if keep:
            density = jnp.exp(-0.5 * gate * gate) * 0.3989422804014327
            keep["slope"][:, cols] = (below + gate * density).astype(bf16)
    waits[3]()
    sum_ref[...] = dot(act_ref[...], down_ref[...])
    for r in range(0, tokens, STRIP):
        strip = slice(r, r + STRIP)
        normed, inverse = normed_of(first_ref[strip] + sum_ref[strip] + rows[4:5])
        result_ref[strip] = (normed * gains[1:2] + rows[5:6]).astype(bf16)
        if keep:
            keep["second_norm"][strip] = normed
            keep["second_scale"][strip] = jnp.broadcast_to(inverse, (STRIP, SLOT))


def attention_back(packed_ref, probs_ref, grad_ref, grad_packed_ref, scores_ref, grads_ref):
    tokens, width = grad_ref.shape
    places = [(p, pair) for p in range(tokens // SLOT) for pair in range(PAIRS)]

    def rows_of(p, pair):
        top = (p * HEADS + 2 * pair) * SLOT
        return slice(top, top + 2 * SLOT)

    def part_of(ref, p, pair, part=0):
        at = part * width + pair * SLOT
        return ref[p * SLOT : (p + 1) * SLOT, at : at + SLOT]

    for p, pair in places:
        grad, values = halves(part_of(grad_ref, p, pair)), part_of(packed_ref, p, pair, 2)
        scores_ref[rows_of(p, pair), :] = dot(grad, values, NT)
    for p, pair in places:
        rows = rows_of(p, pair)
        probs, grad_probs = probs_ref[rows, :].astype(f32), scores_ref[rows, :]
        inner = jnp.sum(probs * grad_probs, axis=-1, keepdims=True)
        grads_ref[rows, :] = (probs * (grad_probs - inner)).astype(bf16)
    for p, pair in places:
        rows = rows_of(p, pair)
        queries = halves(part_of(packed_ref, p, pair)) * (HEAD**-0.5)
        keys = halves(part_of(packed_ref, p, pair, 1)) * (HEAD**-0.5)
        grad = halves(part_of(grad_ref, p, pair))
        for part, value in (
            (0, dot(side_by_side(grads_ref[rows, :]), keys)),
            (1, dot(grads_ref[rows, :], queries, TN)),
            (2, dot(probs_ref[rows, :], grad, TN)),
        ):
            at = part * width + pair * SLOT
            grad_packed_ref[p * SLOT : (p + 1) * SLOT, at : at + SLOT] = value.astype(bf16)


def first_kernel(lengths_ref, *rest):
    ins, weight_ins, rest = rest[:10], rest[10:14], rest[14:]
    result_ref, mixed_ref, bias_ref, *weights = rest[:7]
    packed_ref, attended_ref, sum_ref, first_ref, low_ref, act_ref = rest[7:13]
    scores_ref, probs_ref, grids_ref, hot_rows_ref = rest[13:17]
    held, sems = rest[17:27], rest[27]
    small = [pltpu.make_async_copy(a, b, sems.at[i]) for i, (a, b) in enumerate(zip(ins, held))]
    copies = [
        pltpu.make_async_copy(a, b, sems.at[len(small) + i])
        for i, (a, b) in enumerate(zip(weight_ins, weights))
    ]
    for copy in small:
        copy.start()
    copies[0].start()
    for copy in small:
        copy.wait()
    tokens_ref, order_ref, region_ref, column_ref, row_ref = held[:5]
    rows_ref, gains_ref, up_bias_ref, taps_ref, table_ref = held[5:]
    conv_on = (lax.axis_index("section") == 0).astype(f32)
    taps = taps_ref[...].astype(f32) * conv_on
    conv_bias = rows_ref[...].astype(f32)[6:7] * conv_on
    for p in range(order_ref.shape[0]):
        here = slice(p * SLOT, (p + 1) * SLOT)
        order = order_ref[p : p + 1, :]
        rank_hot = rank_hot_of(order)
        masks = tap_columns(order, region_ref[p : p + 1, :], lengths_ref[p])
        places = dot(identity(), rank_hot, NT)
        sources = [
            dot(rank_hot, (shifted(places, j - REACH) * masks[:, j : j + 1]).astype(bf16))
            for j in range(TAPS)
        ]
        moved = dot(jnp.concatenate(sources, axis=0).astype(bf16), tokens_ref[here])
        total = tokens_ref[here].astype(f32) + conv_bias
        for j in range(TAPS):
            total = total + taps[j : j + 1] * moved[j * SLOT : (j + 1) * SLOT]
        mixed_ref[here] = total
    copies[1].start()
    copies[2].start()
    low_ref[...] = mixed_ref[...].astype(bf16)
    copies[0].wait()
    copies[3].start()
    vectors = rows_ref[...].astype(f32)
    chunks = packed_ref.shape[1] // (2 * SLOT)

    def between(head):
        for chunk in range(head * chunks // HEADS, (head + 1) * chunks // HEADS):
            project(chunk, low_ref, weights[0], vectors, packed_ref)

    bias_body(
        order_ref, column_ref, row_ref, table_ref, bias_ref, grids_ref, hot_rows_ref, between
    )
    forward_body(
        weights,
        [None] + [copy.wait for copy in copies[1:]],
        lengths_ref,
        (rows_ref, gains_ref, up_bias_ref),
        bias_ref,
        (
            mixed_ref,
            packed_ref,
            attended_ref,
            sum_ref,
            first_ref,
            low_ref,
            act_ref,
            result_ref,
            scores_ref,
            probs_ref,
        ),
        None,
    )


KEPT = (
    ("mixed_low", 1, 0),
    ("packed", 3, 0),
    ("probs", 0, 0),
    ("attended", 1, 0),
    ("first_norm", 1, 1),
    ("first_scale", -1, 1),
    ("first_low", 1, 0),
    ("slope", 4, 0),
    ("act", 4, 0),
    ("second_norm", 1, 1),
    ("second_scale", -1, 1),
)


def kept_shapes(tokens, width, hidden):
    shapes = []
    for name, parts, wide in KEPT:
        dims = (tokens, hidden if parts == 4 else SLOT if parts < 0 else parts * width)
        if name == "probs":
            dims = (tokens * HEADS, SLOT)
        shapes.append((dims, f32 if wide else bf16))
    return shapes


def second_kernel(
    arrived_ref,
    cotangent_ref,
    lengths_ref,
    rows_ref,
    gains_ref,
    up_bias_ref,
    mixed_in_ref,
    bias_ref,
    input_ref,
    output_ref,
    up_ref,
    down_ref,
    result_ref,
    grad_in_ref,
    *rest,
):
    kept_list, rest = rest[: len(KEPT)], rest[len(KEPT) :]
    mixed_ref, sum_ref, first_ref, low_ref, gate_ref, grad_ref, grad_packed_ref = rest[:7]
    scores_ref, grads_ref = rest[7:]
    tokens, width = mixed_ref.shape
    keep = dict(zip([name for name, _, _ in KEPT], kept_list))
    first_section = lax.axis_index("section") == 0
    mixed_ref[...] = jnp.where(first_section, mixed_in_ref[...], arrived_ref[...].astype(f32))
    forward_body(
        (input_ref, output_ref, up_ref, down_ref),
        [lambda: None] * 4,
        lengths_ref,
        (rows_ref, gains_ref, up_bias_ref),
        bias_ref,
        (
            mixed_ref,
            keep["packed"],
            keep["attended"],
            sum_ref,
            first_ref,
            low_ref,
            keep["act"],
            result_ref,
            scores_ref,
            keep["probs"],
        ),
        keep,
    )
    gains = gains_ref[...].astype(f32)
    for r in range(0, tokens, STRIP):
        strip = slice(r, r + STRIP)
        grad = cotangent_ref[strip].astype(f32) * gains[1:2]
        grad_sum = norm_back(grad, keep["second_norm"][strip], keep["second_scale"][strip, :1])
        first_ref[strip] = grad_sum
        low_ref[strip] = grad_sum.astype(bf16)
    gate_body(low_ref, down_ref, keep["slope"], gate_ref)
    for c in range(0, width, 2 * SLOT):
        cols = slice(c, c + 2 * SLOT)
        sum_ref[:, cols] = first_ref[:, cols] + dot(gate_ref[...], up_ref[cols, :], NT)
    for r in range(0, tokens, STRIP):
        strip = slice(r, r + STRIP)
        grad = sum_ref[strip] * gains[0:1]
        grad_mid = norm_back(grad, keep["first_norm"][strip], keep["first_scale"][strip, :1])
        first_ref[strip] = grad_mid
        low_ref[strip] = grad_mid.astype(bf16)
    grad_ref[...] = dot(low_ref[...], output_ref[...], NT).astype(bf16)
    attention_back(
        keep["packed"], keep["probs"], grad_ref, grad_packed_ref, scores_ref, grads_ref
    )
    for c in range(0, width, 2 * SLOT):
        cols = slice(c, c + 2 * SLOT)
        grad_in = first_ref[:, cols] + dot(grad_packed_ref[...], input_ref[cols, :], NT)
        grad_in_ref[:, cols] = grad_in.astype(bf16)


def gate_body(grad_ref, down_ref, slope_ref, gate_ref):
    for c in range(0, gate_ref.shape[1], 2 * SLOT):
        cols = slice(c, c + 2 * SLOT)
        value = dot(grad_ref[...], down_ref[cols, :], NT) * slope_ref[:, cols].astype(f32)
        gate_ref[:, cols] = value.astype(bf16)


def store_shares(value, row, column, outs, cuts, share):
    rows, columns = value.shape
    value = value.astype(bf16)
    if not cuts:
        outs[0][row : row + rows, column : column + columns] = value
        return
    even = lax.axis_index("dp") % 2 == 0
    for pair in range(row // (2 * share), (row + rows) // (2 * share)):
        top = 2 * pair * share - row
        for i, (start, count, left, width) in enumerate(cuts):
            from_column, to_column = max(column, left), min(column + columns, left + width)
            if from_column >= to_column:
                continue
            cols = slice(from_column - column, to_column - column)
            first = value[top + start : top + start + count, cols]
            second = value[top + share + start : top + share + start + count, cols]
            cols = slice(from_column - left, to_column - left)
            at = pair % 2 * 4 + pair // 2
            outs[2 * i][at, :, cols] = jnp.where(even, second, first)
            outs[2 * i + 1][at, :, cols] = jnp.where(even, first, second)


def column_sum(value):
    return jnp.sum(value, axis=0, keepdims=True)


def feed_kernel(
    cotangent_ref, arrived_ref, gains_ref, normed_ref, scale_ref, act_ref, *rest, outs, cuts, share
):
    shares_out, (grad_sum_ref, low_ref, small_ref) = rest[:outs], rest[outs:]
    tokens = low_ref.shape[0]
    hidden = act_ref.shape[1]
    gains = gains_ref[...].astype(f32)
    last = lax.axis_index("section") == lax.axis_size("section") - 1
    sums = [0.0, 0.0, 0.0]
    for r in range(0, tokens, STRIP):
        strip = slice(r, r + STRIP)
        grad_out = jnp.where(
            last, cotangent_ref[strip].astype(f32), arrived_ref[strip].astype(f32)
        )
        normed = normed_ref[strip]
        grad_sum = norm_back(grad_out * gains[1:2], normed, scale_ref[strip, :1])
        low = grad_sum.astype(bf16)
        grad_sum_ref[strip] = grad_sum
        low_ref[strip] = low
        sums[0] = sums[0] + column_sum(low.astype(f32))
        sums[1] = sums[1] + column_sum(grad_out)
        sums[2] = sums[2] + column_sum(grad_out * normed)
    step = 3 * SLOT
    for r in range(0, hidden, step):
        value = dot(act_ref[:, r : r + step], low_ref[...], TN)
        store_shares(value, r, 0, shares_out, cuts, share)
    for i, value in enumerate(sums):
        small_ref[i : i + 1, :] = value


def gate_kernel(low_ref, slope_ref, first_low_ref, down_ref, after, *rest, outs, cuts, share):
    shares_out, (gate_ref, small_ref) = rest[:outs], rest[outs:]
    gate_body(low_ref, down_ref, slope_ref, gate_ref)
    width, hidden = first_low_ref.shape[1], gate_ref.shape[1]
    step = 3 * SLOT
    for r in range(0, width, step):
        left = first_low_ref[:, r : r + step]
        for c in range(0, hidden, width):
            value = dot(left, gate_ref[:, c : c + width], TN)
            store_shares(value, r, c, shares_out, cuts, share)
    for c in range(0, hidden, width):
        cols = slice(c, c + width)
        small_ref[:, cols] = column_sum(gate_ref[:, cols].astype(f32))


def backwards(every):
    shape = (2 * SLOT, 2 * SLOT)
    left, right = iota(shape, 0), iota(shape, 1)
    ends = jnp.where(left < SLOT, SLOT - 1, jnp.where(left < SLOT + B2D, 3 * SLOT - B2D - 1, 0))
    ends = jnp.where(left >= SLOT + B2D, 4 * SLOT - B2D - 1, ends)
    return dot(every, hot(left + right == ends)).astype(bf16)


def table_rows(sums):
    blank = jnp.zeros((SLOT, SLOT), f32)
    near = jnp.concatenate([sums[:SLOT, :SLOT], blank], axis=1)
    near = pltpu.roll(near, 0, 1, stride=1, stride_axis=0)
    lane = iota((B2D, SLOT), 1)
    across = jnp.where(lane < B2D, sums[SLOT : SLOT + B2D, SLOT:], 0.0)
    across = pltpu.roll(across, 0, 1, stride=1, stride_axis=0)
    down = jnp.where(lane >= B2D, sums[SLOT + B2D :, SLOT:], 0.0)
    down = pltpu.roll(down, B2D, 1, stride=1, stride_axis=0)
    return jnp.concatenate([column_sum(near), column_sum(across), column_sum(down)], axis=1)


def chain_kernel(
    grad_sum_ref,
    gate_ref,
    normed_ref,
    scale_ref,
    packed_ref,
    probs_ref,
    order_ref,
    column_ref,
    row_ref,
    gains_ref,
    up_ref,
    output_ref,
    after,
    mid_ref,
    low_ref,
    grad_packed_ref,
    small_ref,
    table_ref,
    sum_ref,
    grad_ref,
    reach_ref,
    scores_ref,
    grads_ref,
):
    tokens, width = sum_ref.shape
    pages = tokens // SLOT
    gains = gains_ref[...].astype(f32)
    for c in range(0, width, 2 * SLOT):
        cols = slice(c, c + 2 * SLOT)
        sum_ref[:, cols] = grad_sum_ref[:, cols] + dot(gate_ref[...], up_ref[cols, :], NT)
    first_sum = gain_sum = branch_sum = 0.0
    for r in range(0, tokens, STRIP):
        strip = slice(r, r + STRIP)
        grad_first, normed = sum_ref[strip], normed_ref[strip]
        grad_mid = norm_back(grad_first * gains[0:1], normed, scale_ref[strip, :1])
        low = grad_mid.astype(bf16)
        mid_ref[strip] = grad_mid
        low_ref[strip] = low
        first_sum = first_sum + column_sum(grad_first)
        gain_sum = gain_sum + column_sum(grad_first * normed)
        branch_sum = branch_sum + column_sum(low.astype(f32))
    grad_ref[...] = dot(low_ref[...], output_ref[...], NT).astype(bf16)
    hots = [
        page_hot(order_ref[p : p + 1, :], column_ref[p : p + 1, :], row_ref[p : p + 1, :])
        for p in range(pages)
    ]
    every = backwards(jnp.concatenate(hots, axis=0))
    reach_ref[...] = jnp.zeros_like(reach_ref)
    attention_back(packed_ref, probs_ref, grad_ref, grad_packed_ref, scores_ref, grads_ref)
    for head in range(HEADS):
        along = []
        for p in range(pages):
            top = (p * HEADS + head) * SLOT
            along.append(dot(grads_ref[top : top + SLOT, :], hots[p]).astype(bf16))
        sums = dot(every, jnp.concatenate(along, axis=0), TN)
        reach_ref[head : head + 1, :] = table_rows(sums)
    for i, value in enumerate((first_sum, gain_sum, branch_sum)):
        small_ref[i : i + 1, :] = value
    table_ref[...] = dot(
        bucket_places().astype(f32), reach_ref[...], NT, precision=lax.Precision.HIGHEST
    )


def last_kernel(
    attended_ref,
    low_ref,
    mixed_low_ref,
    grad_packed_ref,
    block_ref,
    after,
    *shares_out,
    outs,
    cuts,
    share,
):
    width = low_ref.shape[1]
    step = 3 * SLOT
    for r in range(0, width, step):
        rows = slice(r, r + step)
        value = dot(attended_ref[:, rows], low_ref[...], TN)
        store_shares(value, r, 0, shares_out, cuts, share)
        for c in range(0, 3 * width, width):
            value = dot(mixed_low_ref[:, rows], grad_packed_ref[:, c : c + width], TN)
            store_shares(value, r, width + c, shares_out, cuts, share)
        if cuts:
            store_shares(block_ref[rows], r, 4 * width, shares_out, cuts, share)


def input_kernel(
    mid_ref,
    grad_packed_ref,
    tokens_ref,
    small_down_ref,
    small_up_ref,
    small_chain_ref,
    table_ref,
    lengths_ref,
    order_ref,
    region_ref,
    taps_ref,
    input_ref,
    after,
    grad_in_ref,
    small_ref,
    block_ref,
    sum_ref,
    *,
    share,
):
    tokens, width = sum_ref.shape
    pages = tokens // SLOT
    conv_on = (lax.axis_index("section") == 0).astype(f32)
    taps = taps_ref[...].astype(f32) * conv_on
    for c in range(0, width, 2 * SLOT):
        cols = slice(c, c + 2 * SLOT)
        sum_ref[:, cols] = mid_ref[:, cols] + dot(grad_packed_ref[...], input_ref[cols, :], NT)
    tap_sums = [0.0] * TAPS
    mixed_sum = 0.0
    for p in range(pages):
        here = slice(p * SLOT, (p + 1) * SLOT)
        order = order_ref[p : p + 1, :]
        rank_hot = rank_hot_of(order)
        masks = tap_columns(order, region_ref[p : p + 1, :], lengths_ref[p])
        ordered = dot(rank_hot, tokens_ref[here], TN)
        grad_mixed = sum_ref[here]
        grad_order = place_rows(rank_hot, grad_mixed, TN)
        source = jnp.zeros_like(ordered)
        for j in range(TAPS):
            masked = grad_order * masks[:, j : j + 1]
            tap_sums[j] = tap_sums[j] + column_sum(masked * shifted(ordered, j - REACH))
            source = source + shifted(taps[j : j + 1] * masked, REACH - j)
        grad_in_ref[here] = grad_mixed + place_rows(rank_hot, source, NN)
        mixed_sum = mixed_sum + column_sum(grad_mixed)
    down, chain = small_down_ref[...], small_chain_ref[...]
    rows = [
        column_sum(grad_packed_ref[:, :width].astype(f32)),
        column_sum(grad_packed_ref[:, 2 * width :].astype(f32)),
        chain[2:3],
        chain[0:1],
        down[0:1],
        down[1:2],
        conv_on * mixed_sum,
        chain[1:2],
        down[2:3],
    ]
    for i, value in enumerate(rows + [conv_on * value for value in tap_sums]):
        small_ref[i : i + 1, :] = value
    if share:
        small_block(small_ref, small_up_ref, table_ref, block_ref, share)


SMALL_ROWS = 16


def small_block(small_ref, up_ref, table_ref, block_ref, share):
    width = small_ref.shape[1]
    shares = block_ref.shape[0] // share
    part = width // shares
    up_part = up_ref.shape[1] // shares
    buckets = (B1D + 2 * B2D) // shares
    block_ref[...] = jnp.zeros_like(block_ref)
    small, up = small_ref[...], jnp.broadcast_to(up_ref[...], (8, up_ref.shape[1]))
    for s in range(shares):
        top = s * share
        shift = (width - s * part) % width
        here = pltpu.roll(small, shift, 1) if shift else small
        block_ref[top : top + SMALL_ROWS, :] = here[:, :SLOT]
        shift = (up.shape[1] - s * up_part) % up.shape[1]
        here = pltpu.roll(up, shift, 1) if shift else up
        top += SMALL_ROWS
        block_ref[top : top + 1, :] = here[:1, :SLOT]
        block_ref[top + 1 : top + 2, :] = here[:1, SLOT : 2 * SLOT]
        top += 2
        block_ref[top : top + buckets, :] = table_ref[s * buckets : (s + 1) * buckets, :]


def place():
    index = lax.axis_index("dp")
    return index // 4, index // 2 % 2


def added(out_ref, out_at, parts, window=None):
    rows = out_ref.shape[-2]
    for r in range(0, rows, 16):
        strip = slice(r, r + 16)
        total = 0.0
        for ref, at, windowed in parts:
            if windowed:
                row, _, column, columns = window
                value = ref[at, row + r : row + r + 16, column : column + columns]
            else:
                value = ref[at, strip]
            total = total + value.astype(f32)
        if out_at is None:
            out_ref[strip] = total.astype(bf16)
        else:
            out_ref[out_at, strip] = total.astype(bf16)


def fetched(recv_hbm, first, window, scratch, sems):
    row, rows, column, columns = window
    copies = []
    for k in range(4):
        source = recv_hbm.at[first + k, pl.ds(row, rows), pl.ds(column, columns)]
        copies.append(pltpu.make_async_copy(source, scratch.at[k], sems.at[k]))
        copies[-1].start()
    return copies


def leave_kernel(mine_ref, recv_ref, *rest, window, fetch):
    first = 4 * (1 - place()[1])
    if fetch:
        out_ref, scratch, sems = rest[-3:]
        copies = fetched(recv_ref, first, window, scratch, sems)
    else:
        out_ref = rest[-1]
    for k in range(4):
        other = (recv_ref, first + k, True)
        if fetch:
            copies[k].wait()
            other = (scratch, k, False)
        added(out_ref, k, ((mine_ref, first + k, True), other), window)


def near_kernel(mine_ref, recv_ref, y_ref, *rest, window, fetch):
    z, y = place()
    leave_ref, keep_ref = rest[-4:-2] if fetch else rest[-2:]
    if fetch:
        scratch, sems = rest[-2:]
        for copy in fetched(recv_ref, 4 * y, window, scratch, sems):
            copy.wait()
    for out_ref, parity in ((leave_ref, 1 - z % 2), (keep_ref, z % 2)):
        for k in range(2):
            block = 2 * k + parity
            at = 4 * y + block
            other = (scratch, block, False) if fetch else (recv_ref, at, True)
            added(out_ref, k, ((mine_ref, at, True), other, (y_ref, block, False)), window)


def far_kernel(keep_ref, recv_ref, *rest):
    leave_ref, own_ref = rest[-2:]
    high = place()[0] // 2
    for out_ref, k in ((leave_ref, 1 - high), (own_ref, high)):
        added(out_ref, None, ((keep_ref, k, False), (recv_ref, k, False)))


def near_first_kernel(mine_ref, recv_ref, after, leave_ref, keep_ref):
    z, _ = place()
    for out_ref, parity in ((leave_ref, 1 - z % 2), (keep_ref, z % 2)):
        for k in range(4):
            at = 2 * k + parity
            added(out_ref, k, ((mine_ref, at, False), (recv_ref, at, False)))


def far_first_kernel(keep_ref, recv_ref, after, leave_ref, stay_ref):
    high = place()[0] // 2
    for out_ref, k in ((leave_ref, 1 - high), (stay_ref, high)):
        for y in range(2):
            at = 2 * y + k
            added(out_ref, y, ((keep_ref, at, False), (recv_ref, at, False)))


def cross_kernel(keep_ref, recv_ref, after, leave_ref, own_ref):
    y = place()[1]
    for out_ref, at in ((leave_ref, 1 - y), (own_ref, y)):
        added(out_ref, None, ((keep_ref, at, False), (recv_ref, at, False)))


def both(parts):
    return parts[0][...].astype(f32) + parts[1][...].astype(f32)


def down_end(*refs):
    out_ref, token_ref = refs[-2:]
    token_ref[...] = jnp.zeros_like(token_ref)
    rows = refs[0].shape[0]
    out_ref[:rows] = both(refs[:2])
    out_ref[rows:] = both(refs[2:4])


def up_end(*refs):
    out_ref, token_ref = refs[-2:]
    token_ref[...] = jnp.zeros_like(token_ref)
    columns = refs[0].shape[1]
    out_ref[:, :columns] = both(refs[:2])
    out_ref[:, columns:] = both(refs[2:4])


def last_end(*refs):
    sum_ref, block_ref = refs[-2:]
    input_ref, output_ref, bias_ref, gain_ref, tap_ref, up_ref, table_ref = refs[-9:-2]
    column = 0
    for i in range(0, len(refs) - 10, 2):
        columns = refs[i].shape[1]
        sum_ref[:, column : column + columns] = both(refs[i : i + 2])
        column += columns
    width, share = output_ref.shape[1], output_ref.shape[0]
    output_ref[...] = sum_ref[:, :width]
    input_ref[...] = sum_ref[:, width : 4 * width]
    block_ref[...] = sum_ref[:, 4 * width :]
    for i in range(7):
        bias_ref[i] = block_ref[i : i + 1, :share]
        tap_ref[i] = block_ref[9 + i : 10 + i, :share]
    gain_ref[...] = block_ref[7:9, :share]
    rest = up_ref.shape[1] - SLOT
    up_ref[:, :SLOT] = block_ref[SMALL_ROWS : SMALL_ROWS + 1, :]
    up_ref[:, SLOT:] = block_ref[SMALL_ROWS + 1 : SMALL_ROWS + 2, :rest]
    for i in range(table_ref.shape[1] // HEADS):
        at = SMALL_ROWS + 2 + i
        table_ref[:, i * HEADS : (i + 1) * HEADS] = block_ref[at : at + 1, :HEADS]


def kernel_call(body, name, ins, outs, scratch, flops=0, vmem=10):
    return pl.pallas_call(
        body,
        name=name,
        out_shape=[shape for shape, _ in outs],
        in_specs=[spec for _, spec in ins],
        out_specs=[spec for _, spec in outs],
        scratch_shapes=scratch,
        compiler_params=pltpu.CompilerParams(vmem_limit_bytes=vmem << 20),
        cost_estimate=pl.CostEstimate(flops=flops, bytes_accessed=0, transcendentals=0),
    )(*[value for value, _ in ins])


def near_by(value):
    return pltpu.with_memory_space_constraint(value, pltpu.VMEM)


def in_hbm(value):
    return pltpu.with_memory_space_constraint(value, pltpu.HBM)


def near_shape(dims, kind=bf16):
    return pltpu.VMEM(dims, kind)


class Summing:
    def __init__(self):
        self.pairs, self.windows, self.crossed, self.kept, self.ends = {}, {}, {}, {}, {}
        self.fetch = {}

    @staticmethod
    def _swap(value, bits):
        return near_by(lax.ppermute(value, "dp", [(i, i ^ bits) for i in range(16)]))

    @staticmethod
    def _add(body, name, ins, after, outs, cost=0, earlier=(), scratch=(), fetch=False):
        specs = [IN_VMEM] * len(ins)
        if fetch:
            specs[1] = IN_PLACE
        return kernel_call(
            body,
            name,
            [(near_by(value), spec) for value, spec in zip(ins, specs)]
            + [(value, IN_PLACE) for value in (after, *earlier)],
            [(near_shape(dims), IN_VMEM) for dims in outs],
            list(scratch),
            cost,
            4,
        )

    def core(self, theirs, mine, fetch=False, **windows):
        recv = self._swap(theirs, 1)
        for name, window in windows.items():
            self.pairs[name], self.windows[name] = [mine, recv], window
            self.fetch[name] = fetch

    def _fetching(self, name, body):
        window, fetch = self.windows[name], self.fetch[name]
        dims = (4, window[1], window[3])
        scratch = [pltpu.VMEM(dims, bf16), pltpu.SemaphoreType.DMA((4,))] if fetch else []
        body = functools.partial(body, window=window, fetch=fetch)
        return body, dict(scratch=scratch, fetch=fetch), dims

    def leave(self, name, after, earlier=None):
        body, more, dims = self._fetching(name, leave_kernel)
        earlier = [self.crossed[earlier]] if earlier else []
        (out,) = self._add(body, "leave", self.pairs[name], after, [dims], 0, earlier, **more)
        self.crossed[name] = self._swap(out, 2)
        return out

    def near(self, name, after, earlier=()):
        body, more, dims = self._fetching(name, near_kernel)
        dims = (2,) + dims[1:]
        ins = self.pairs[name] + [self.crossed[name]]
        earlier = [self.ends[other][1] for other in earlier]
        out, keep = self._add(body, "near", ins, after, [dims, dims], COST, earlier, **more)
        self.kept[name] = [keep, self._swap(out, 4)]
        return out

    def far(self, name, after, earlier=()):
        ins = self.kept[name]
        dims = ins[0].shape[1:]
        earlier = [self.ends[other][1] for other in earlier]
        out, own = self._add(far_kernel, "far", ins, after, [dims, dims], COST, earlier)
        self.ends[name] = [own, self._swap(out, 8)]
        return out

    def near_first(self, name, after):
        ins = self.pairs[name]
        dims = (4,) + ins[0].shape[1:]
        out, keep = self._add(near_first_kernel, "near_first", ins, after, [dims, dims], COST)
        self.kept[name] = [keep, self._swap(out, 4)]
        return out

    def far_first(self, name, after):
        ins = self.kept[name]
        dims = (2,) + ins[0].shape[1:]
        out, stay = self._add(far_first_kernel, "far_first", ins, after, [dims, dims], COST)
        self.kept[name] = [stay, self._swap(out, 8)]
        return out

    def cross(self, name, after):
        ins = self.kept[name]
        dims = ins[0].shape[1:]
        out, own = self._add(cross_kernel, "cross", ins, after, [dims, dims], COST)
        self.ends[name] = [own, self._swap(out, 2)]
        return out


def local(
    tokens,
    cotangent,
    page_lengths,
    cut_order,
    cut_region,
    cell_column,
    cell_row,
    input_proj,
    output_proj,
    up_proj,
    down_proj,
    up_bias,
    bias_rows,
    gain_rows,
    conv_taps,
    bias_table,
):
    section_count = lax.axis_size("section")
    dp_count = lax.axis_size("dp")
    by_hops = dp_count == 16
    pages, _, width = tokens.shape
    hidden = up_proj.shape[2]
    count = pages * SLOT
    weights = [w[0] for w in (input_proj, output_proj, up_proj, down_proj)]
    rows, gains, taps = bias_rows[0], gain_rows[0], conv_taps[0]
    tokens, cotangent = tokens.reshape(count, width), cotangent.reshape(count, width)

    def shape(dims, kind):
        return jax.ShapeDtypeStruct(dims, kind)

    def inside(*values):
        return [(v, IN_VMEM) for v in values]

    def in_place(*values):
        return [(v, IN_PLACE) for v in values]

    def scalars(*values):
        return [(v, IN_SMEM) for v in values]

    wide, low = shape((count, width), f32), shape((count, width), bf16)
    wide_scratch = pltpu.VMEM((count, width), f32)
    low_scratch = pltpu.VMEM((count, width), bf16)
    packed_scratch = pltpu.VMEM((count, 3 * width), bf16)
    hidden_scratch = pltpu.VMEM((count, hidden), bf16)
    bias_dims = (pages * HEADS * SLOT, SLOT)

    def sems(number):
        return pltpu.SemaphoreType.DMA((number,))

    first_ins = [tokens, cut_order, cut_region, cell_column, cell_row, rows, gains, up_bias]
    first_ins += [taps, bias_table]
    result, mixed, bias, *near_weights = kernel_call(
        first_kernel,
        "first",
        scalars(in_hbm(page_lengths)) + in_place(*map(in_hbm, first_ins + weights)),
        inside(low, near_shape((count, width), f32), near_shape(bias_dims, f32))
        + inside(*[near_shape(w.shape) for w in weights]),
        [
            packed_scratch,
            low_scratch,
            wide_scratch,
            wide_scratch,
            low_scratch,
            hidden_scratch,
            pltpu.VMEM(bias_dims, f32),
            pltpu.VMEM(bias_dims, bf16),
            pltpu.VMEM((HEADS, 2 * SLOT, 2 * SLOT), bf16),
            pltpu.VMEM((HEADS, count, 2 * SLOT), bf16),
            *[pltpu.VMEM(v.shape, v.dtype) for v in first_ins],
            sems(len(first_ins) + len(weights)),
        ],
    )
    input_w, output_w, up_w, down_w = near_weights = list(map(near_by, near_weights))
    arrived = near_by(
        lax.ppermute(result, "section", [(i, i + 1) for i in range(section_count - 1)])
    )
    shapes = kept_shapes(count, width, hidden)
    layer_out, leaving, *kept_list = kernel_call(
        second_kernel,
        "second",
        inside(arrived, cotangent)
        + scalars(page_lengths)
        + inside(rows, gains, up_bias)
        + inside(*map(near_by, (mixed, bias, *near_weights))),
        inside(low, near_shape((count, width)), *[near_shape(*s) for s in shapes]),
        [
            wide_scratch,
            wide_scratch,
            wide_scratch,
            low_scratch,
            hidden_scratch,
            low_scratch,
            packed_scratch,
            pltpu.VMEM(bias_dims, f32),
            pltpu.VMEM(bias_dims, bf16),
        ],
    )
    kept = dict(zip([name for name, _, _ in KEPT], map(near_by, kept_list)))
    arrived_grad = near_by(
        lax.ppermute(leaving, "section", [(i + 1, i) for i in range(section_count - 1)])
    )
    part = width // dp_count

    def cut(dims, cuts):
        share = dims[0] // dp_count
        if not by_hops:
            outs, cuts = inside(shape(dims, bf16)), ()
        else:
            halves_out = [near_shape((dp_count // 2, c[1], c[3])) for c in cuts for _ in range(2)]
            outs = inside(*halves_out)
        return outs, dict(outs=len(outs), cuts=cuts, share=share)

    half = hidden // dp_count // 2
    down_outs, down_cut = cut((hidden, width), ((0, half, 0, width), (half, half, 0, width)))
    up_outs, up_cut = cut((width, hidden), ((0, part, 0, hidden),))
    *down_parts, grad_sum, grad_low, small_down = kernel_call(
        functools.partial(feed_kernel, **down_cut),
        "feed",
        inside(cotangent, arrived_grad, gains)
        + inside(kept["second_norm"], kept["second_scale"], kept["act"]),
        down_outs + inside(wide, low, shape((8, width), f32)),
        [],
    )
    *up_parts, gate, small_up = kernel_call(
        functools.partial(gate_kernel, **up_cut),
        "gate",
        inside(grad_low, kept["slope"], kept["first_low"], down_w) + in_place(small_down),
        up_outs + inside(shape((count, hidden), bf16), shape((1, hidden), f32)),
        [],
    )
    summing = Summing()
    after = small_up
    if by_hops:
        piece = (0, half, 0, width)
        side = hidden // 2
        summing.core(*down_parts[:2], d1=piece)
        summing.core(*down_parts[2:], d2=piece)
        summing.core(*up_parts, u1=(0, part, 0, side), u2=(0, part, side, side))
        after = summing.leave("d1", after)
        after = summing.near_first("d2", after)
        after = summing.leave("u1", after)
    grad_mid, grad_branch, grad_packed, small_chain, table = kernel_call(
        chain_kernel,
        "chain",
        inside(grad_sum, gate, kept["first_norm"], kept["first_scale"], kept["packed"])
        + inside(kept["probs"], cut_order, cell_column, cell_row, gains)
        + inside(up_w, output_w)
        + in_place(after),
        inside(wide, low, shape((count, 3 * width), bf16), shape((8, width), f32))
        + inside(shape((B1D + 2 * B2D, SLOT), f32)),
        [
            wide_scratch,
            low_scratch,
            pltpu.VMEM((SLOT, 4 * SLOT), f32),
            pltpu.VMEM(bias_dims, f32),
            pltpu.VMEM(bias_dims, bf16),
        ],
    )
    after = grad_mid
    if by_hops:
        after = summing.near("d1", after)
        after = summing.far_first("d2", after)
        after = summing.leave("u2", after)
    grad_in, small_rows, block = kernel_call(
        functools.partial(input_kernel, share=part if by_hops else 0),
        "input",
        inside(grad_mid, grad_packed, tokens, small_down, small_up, small_chain, table)
        + scalars(page_lengths)
        + inside(cut_order, cut_region, taps, input_w)
        + in_place(after),
        inside(wide, shape((16, width), f32), near_shape((width, SLOT), f32)),
        [wide_scratch],
    )
    after = block
    columns = 4 * width + (SLOT if by_hops else 0)
    last_outs, last_cut = cut((width, columns), ((0, part, 0, columns),))
    last_parts = kernel_call(
        functools.partial(last_kernel, **last_cut),
        "last",
        inside(kept["attended"], grad_branch, kept["mixed_low"], grad_packed, near_by(block))
        + in_place(after),
        last_outs,
        [],
    )
    after = last_parts[0]
    if by_hops:
        token = near_shape((8, SLOT), f32)
        windows, column = {}, 0
        for name, end in (("a1", 2 * width - 2 * SLOT), ("a2", 3 * width + SLOT), ("a3", columns)):
            windows[name], column = (0, part, column, end - column), end
        summing.core(*last_parts, fetch=True, **windows)
        ends = summing.ends
        after = summing.near("u1", after)
        after = summing.far("d1", after)
        after = summing.cross("d2", after)
        after = summing.leave("a1", after, "u2")
        after = summing.near("u2", after)
        after = summing.far("u1", after, ["d1"])
        after = summing.leave("a2", after)
        down_grad, after = kernel_call(
            down_end,
            "down_end",
            inside(*map(near_by, ends["d1"] + ends["d2"])) + in_place(after),
            inside(shape((hidden // dp_count, width), f32), token),
            [],
            vmem=4,
        )
        after = summing.far("u2", after)
        after = summing.near("a1", after)
        after = summing.leave("a3", after)
        after = summing.near("a2", after, ["u1", "u2"])
        after = summing.far("a1", after)
        after = summing.near("a3", after)
        after = summing.far("a2", after)
        after = summing.far("a3", after)
        up_grad, after = kernel_call(
            up_end,
            "up_end",
            inside(*map(near_by, ends["u1"] + ends["u2"])) + in_place(after),
            inside(shape((part, hidden), f32), token),
            [],
            vmem=4,
        )
        input_grad, output_grad, bias_grad, gain_grad, tap_grad, up_bias_grad, table_grad = (
            kernel_call(
                last_end,
                "last_end",
                inside(*map(near_by, ends["a1"] + ends["a2"] + ends["a3"])) + in_place(after),
                inside(
                    shape((part, 3 * width), f32),
                    shape((part, width), f32),
                    shape((7, 1, part), f32),
                    shape((2, part), f32),
                    shape((TAPS, 1, part), f32),
                    shape((1, hidden // dp_count), f32),
                    shape((1, table.shape[0] * HEADS // dp_count), f32),
                ),
                [pltpu.VMEM((part, columns), f32), pltpu.VMEM((part, SLOT), f32)],
                vmem=4,
            )
        )
    else:

        def scattered(value):
            return lax.psum_scatter(value, "dp", scatter_dimension=0, tiled=True).astype(f32)

        down_grad, up_grad, last_grad = (
            scattered(parts[0]) for parts in (down_parts, up_parts, last_parts)
        )
        input_grad, output_grad = last_grad[:, width:], last_grad[:, :width]
        small = [
            small_rows.reshape(16, dp_count, part).transpose(1, 0, 2).reshape(dp_count, -1),
            small_up.reshape(dp_count, -1),
            table[:, :HEADS].reshape(dp_count, -1),
        ]
        small = jnp.concatenate(small, axis=1)
        used = small.shape[1]
        small = jnp.pad(small, ((0, 0), (0, -used % SLOT))).reshape(-1, SLOT)
        small = scattered(small).reshape(-1)
        vectors = small[: 16 * part].reshape(16, part)
        bias_grad, tap_grad = vectors[:7, None], vectors[9:, None]
        gain_grad = vectors[7:9]
        at = 16 * part + hidden // dp_count
        up_bias_grad, table_grad = small[None, 16 * part : at], small[None, at:used]
    return (
        layer_out.reshape(1, pages, SLOT, width),
        grad_in.reshape(1, pages, SLOT, width),
        input_grad[None],
        output_grad[None],
        up_grad[None],
        down_grad[None],
        up_bias_grad,
        bias_grad.transpose(1, 0, 2),
        gain_grad[None],
        tap_grad.transpose(1, 0, 2),
        table_grad,
    )


def solution(mesh):
    by_section = [P("section", None, None)] * 4
    placed = (
        P("dp", None, None),
        P("dp", None, None),
        P("dp"),
        P("dp", None),
        P("dp", None),
        P("dp", None),
        P("dp", None),
        *by_section,
        P("section", None),
        P("section", None, None),
        P("section", None, None),
        P("section", None, None),
        P("section", None),
    )
    return jax.shard_map(
        local,
        mesh=mesh,
        in_specs=placed,
        out_specs=(
            P("section", "dp", None, None),
            P("section", "dp", None, None),
            P("section", "dp", None),
            P("section", "dp", None),
            P("section", "dp", None),
            P("section", "dp", None),
            P("section", "dp"),
            P("section", None, "dp"),
            P("section", None, "dp"),
            P("section", None, "dp"),
            P("section", "dp"),
        ),
        check_vma=False,
    )
```
